32 devices in a mesh: grp: 2 (over y), ctx: 4 (over z), tp: 4 (over x, core).
Axes of the slice: x: 2, y: 2, z: 4, core: 2. Of those that a mesh axis runs over, the one named last changes fastest.
Arguments:
- residual: bfloat16 [1024, 7168], P(('grp', 'ctx'), 'tp'), parts along dimension 0, may hold values from -20 to 20
- latent: bfloat16 [576, 1024], P(None, ('grp', 'ctx')), parts along dimension 1, may hold values from -4 to 4
- queries: bfloat16 [1024, 36864], P(('grp', 'ctx'), 'tp'), parts along dimension 0, may hold values from -32 to 32
- lengths: int32 [8], P('grp'), parts along dimension 0, may hold values from 1 to 384, 512 in all
- value_weight: bfloat16 [512, 8192], P(None, 'tp'), may hold values from -1 to 1
- output_weight: bfloat16 [8192, 7168], P('ctx', 'tp'), may hold values from -0.0625 to 0.0625
- norm_gain: float32 [7168], P('tp'), may hold values from 0.1 to 1.9
- gate_weight: bfloat16 [7168, 10240], P('tp', 'ctx'), may hold values from -0.0625 to 0.0625
- up_weight: bfloat16 [7168, 10240], P('tp', 'ctx'), may hold values from -0.0625 to 0.0625
- down_weight: bfloat16 [10240, 7168], P('ctx', 'tp'), may hold values from -0.0625 to 0.0625
Outputs:
- attended: bfloat16 [1024, 7168], P(('grp', 'ctx'), 'tp'), parts along dimension 0
- layer_out: bfloat16 [1024, 7168], P(('grp', 'ctx'), 'tp'), parts along dimension 0
The draws below stay inside these ranges and needn't reach their ends.
There are 2 independent parts, one for each index of `grp`. The reference program is written for one: setup_inputs(seed, part) draws one part's arguments, and reference() takes and returns one part's arrays. A program takes and returns all parts, laid end to end along the dimension named above; an argument that names none is the same for every part. Nothing has to cross between parts.
Inputs may be any that keep to these rules, and one draw needn't show every extreme that they name: The 4 traces fill the sequence in order and their lengths sum to 512.
All inputs are finite; a program needn't handle non-finite values.
Results may differ from the reference program's by a relative error of at most 0.02.
Values may be sent and summed in bfloat16 or wider, within the bound.
No kernel may reach another device: no remote copies, remote signals or barrier semaphores. Data moves between devices by JAX's collectives and lax.ppermute only.
A program may use at most 128 MiB of HBM per device.

```python
import math
import jax
import jax.numpy as jnp
import numpy as np
from jax import lax

D = 7168
HEADS = 64
LAT = 512
ROPE = 64
VHEAD = 128
FF = 10240
SEQS = 4
TOKENS = 512
DGROUP = 1792
HGROUP = 2048
FGROUP = 2560
N_CTX = 4
N_TP = 4


def latent_base(key):
    width_all = LAT + ROPE
    base = jnp.clip(jax.random.normal(jax.random.fold_in(key, 11), (width_all, TOKENS), jnp.float32), -4.0, 4.0)
    return base


def draw_latent(key, part):
    return latent_base(key).astype(jnp.bfloat16)


def draw_queries(key, part):
    width_all = LAT + ROPE
    base = 0.8 * jnp.clip(jax.random.normal(jax.random.fold_in(key, 13), (TOKENS, HEADS, width_all), jnp.float32), -4.0, 4.0)
    return base.reshape(TOKENS, HEADS * width_all).astype(jnp.bfloat16)


def draw_residual(key, part):
    row_scale = jnp.exp(jax.random.uniform(jax.random.fold_in(key, 21), (TOKENS, 1), jnp.float32, jnp.log(0.2), jnp.log(2.0)))
    jitter = jnp.exp(jax.random.uniform(jax.random.fold_in(key, 22), (1, D), jnp.float32, jnp.log(0.7), jnp.log(1.4)))
    ramp = jnp.arange(D, dtype=jnp.float32)[None, :] / (D - 1)
    col_scale = 3.0 ** ramp * jitter / 1.9
    noise_part = jnp.clip(jax.random.normal(jax.random.fold_in(key, 23), (TOKENS, D), jnp.float32), -4.0, 4.0)
    value_all = row_scale * noise_part * col_scale
    return jnp.clip(value_all, -20.0, 20.0).astype(jnp.bfloat16)


def shard_levels(key, shape, pieces, least, high):
    level = 1.0
    for dim, blocks in pieces:
        heights = jax.random.uniform(jax.random.fold_in(jax.random.fold_in(key, 6), dim), (blocks,), jnp.float32, least / len(pieces), high / len(pieces))
        level = level * jnp.repeat(jnp.exp(heights), shape[dim] // blocks).reshape((-1,) + (1,) * (len(shape) - 1 - dim))
    return level


def length_profile(count, total, bound, skew):
    loads = [(1 << 20) // math.isqrt(rank ** skew) + 1 for rank in range(2, count + 1)]
    surplus, given = total - bound - (count - 1), [1] * (count - 1)
    while surplus > 0:
        candidates = [i for i in range(count - 1) if given[i] < bound]
        mass, remaining = sum([loads[i] for i in candidates]), surplus
        for i in candidates:
            more = min(bound - given[i], max(1, remaining * loads[i] // mass), surplus)
            given[i] = given[i] + more
            surplus = surplus - more
    return np.array([bound] + given)


def ragged_sizes(rng, number_of, total, bound, slope):
    if number_of == 2:
        one = jax.random.randint(rng, (), max(1, total - bound), min(bound, total - 1) + 1)
        return jnp.stack([one, total - one])
    sizes = jnp.asarray(length_profile(number_of, total, bound, slope), jnp.int32)
    twos = (number_of - 1) // 2
    source_of, taker = sizes[1:1 + 2 * twos:2], sizes[2:2 + 2 * twos:2]
    margin = jnp.minimum(source_of - 1, bound - taker)
    passed = jax.random.randint(jax.random.fold_in(rng, 1), (twos,), 0, 1 << 20) % (margin + 1)
    sizes = sizes.at[1:1 + 2 * twos:2].set(source_of - passed).at[2:2 + 2 * twos:2].set(taker + passed)
    return sizes[jax.random.permutation(jax.random.fold_in(rng, 2), number_of)]


def bell_draw(key, extent, scale, limit, shards=(), held_as=jnp.bfloat16):
    result = scale * jax.random.normal(key, extent, jnp.float32)
    if shards:
        result = result * shard_levels(key, extent, shards, -0.22, 0.18)
    return jnp.clip(result, -limit, limit).astype(held_as)


def setup_inputs(seed: int = 0, part: int = 0) -> dict:
    key_of = jax.random.split(jax.random.key(seed), 11)
    part_keys = jax.random.split(jax.random.fold_in(key_of[10], part), 11)
    residual = draw_residual(jax.random.fold_in(jax.random.fold_in(key_of[10], part), 71), part)
    latent = draw_latent(jax.random.fold_in(jax.random.fold_in(key_of[10], part), 71), part)
    queries = draw_queries(jax.random.fold_in(jax.random.fold_in(key_of[10], part), 71), part)
    lengths = ragged_sizes(part_keys[3], SEQS, TOKENS, TOKENS * 3 // 4, 0).astype(jnp.int32)
    value_weight = bell_draw(key_of[4], (LAT, HEADS * VHEAD), (LAT // 16) ** -0.5, 1.0, ((1, 4),))
    output_weight = bell_draw(key_of[5], (HEADS * VHEAD, D), (HEADS * VHEAD) ** -0.5, 0.0625, ((0, 4), (1, 4)))
    norm_gain = jnp.clip(1.0 + 0.18 * jax.random.normal(key_of[6], (D,), jnp.float32), 0.1, 1.9)
    gate_weight = bell_draw(key_of[7], (D, FF), D ** -0.5, 0.0625, ((0, 4), (1, 4)))
    up_weight = bell_draw(key_of[8], (D, FF), D ** -0.5, 0.0625, ((0, 4), (1, 4)))
    down_weight = bell_draw(key_of[9], (FF, D), FF ** -0.5, 0.0625, ((0, 4), (1, 4)))
    return dict(residual=residual, latent=latent, queries=queries, lengths=lengths, value_weight=value_weight, output_weight=output_weight, norm_gain=norm_gain, gate_weight=gate_weight, up_weight=up_weight, down_weight=down_weight)


score_scale = 192.0 ** (-0.5)
rope_base = 10000.0
norm_eps = 1e-06
masked_score = -1e+30

def rope_freqs(half_width):
    return rope_base ** (-jnp.arange(half_width, dtype=jnp.float32) / half_width)

def trace_info(token_index, lengths):
    trace_ends = jnp.cumsum(lengths).astype(jnp.int32)
    starts = (trace_ends - lengths).astype(jnp.int32)
    trace_ids = lax.optimization_barrier(jnp.sum((token_index[:, None] >= trace_ends[None, :]).astype(jnp.int32), axis=1)).astype(jnp.int32)
    member = trace_ids[:, None] == jnp.arange(lengths.shape[0], dtype=jnp.int32)[None, :]
    pos_shift = lax.optimization_barrier(jnp.sum(jnp.where(member, (0 - starts)[None, :], 0), axis=1)).astype(jnp.int32)
    return (trace_ids, token_index + pos_shift)

def rope_keys(latent, positions, latent_width):
    values = latent.astype(jnp.float32)
    half_width = (values.shape[0] - latent_width) // 2
    angles = rope_freqs(half_width)[:, None] * positions.astype(jnp.float32)[None, :]
    first_half = values[latent_width:latent_width + half_width]
    second_half = values[latent_width + half_width:]
    cosine = jnp.cos(angles)
    sine_value = jnp.sin(angles)
    return jnp.concatenate([values[:latent_width], first_half * cosine - second_half * sine_value, first_half * sine_value + second_half * cosine], axis=0).astype(jnp.bfloat16)

def rope_queries(queries, positions, latent_width):
    values = queries.astype(jnp.float32)
    half_width = (values.shape[2] - latent_width) // 2
    angles = positions.astype(jnp.float32)[:, None] * rope_freqs(half_width)[None, :]
    cosine = jnp.cos(angles)[:, None, :]
    sine_value = jnp.sin(angles)[:, None, :]
    first_half = values[:, :, latent_width:latent_width + half_width]
    second_half = values[:, :, latent_width + half_width:]
    return jnp.concatenate([values[:, :, :latent_width], first_half * cosine - second_half * sine_value, first_half * sine_value + second_half * cosine], axis=2).astype(jnp.bfloat16)

def add_terms(total_sum, block_pair):
    block_term = jnp.dot(block_pair[0], block_pair[1], preferred_element_type=jnp.float32).astype(jnp.bfloat16)
    return (total_sum + lax.optimization_barrier(block_term).astype(jnp.float32), None)

def reference(residual, latent, queries, lengths, value_weight, output_weight, norm_gain, gate_weight, up_weight, down_weight):
    token_count = residual.shape[0]
    token_index = jnp.arange(token_count, dtype=jnp.int32)
    trace_ids, positions = trace_info(token_index, lengths)
    keys_rot = rope_keys(latent, positions, LAT)
    rotated = rope_queries(queries.reshape(token_count, HEADS, LAT + ROPE), positions, LAT)
    allowed = (trace_ids[:, None] == trace_ids[None, :]) & (token_index[None, :] <= token_index[:, None])
    key_values = keys_rot[:LAT]

    def one_head(head_queries):
        scores = jnp.dot(head_queries, keys_rot, preferred_element_type=jnp.float32) * score_scale
        scores = jnp.where(allowed, scores, masked_score)
        row_top = lax.optimization_barrier(jnp.max(scores, axis=1, keepdims=True))
        exponent = jnp.where(allowed, jnp.exp(scores - row_top), 0.0)
        row_total = lax.optimization_barrier(jnp.sum(exponent, axis=1, keepdims=True))
        weighted = lax.dot_general(exponent.astype(jnp.bfloat16), key_values, (((1,), (1,)), ((), ())), preferred_element_type=jnp.float32)
        return (weighted / row_total).astype(jnp.bfloat16)
    mixed_latent = lax.map(one_head, jnp.transpose(rotated, (1, 0, 2)))
    head_mix = jnp.einsum('hnl,lhd->nhd', mixed_latent.astype(jnp.float32), value_weight.reshape(LAT, HEADS, VHEAD).astype(jnp.float32))
    heads_out = head_mix.astype(jnp.bfloat16).reshape(token_count, HEADS * VHEAD)
    head_blocks = heads_out.reshape(token_count, N_CTX, HGROUP).transpose(1, 0, 2)
    head_sum, _ = lax.scan(add_terms, jnp.zeros((token_count, D), jnp.float32), (head_blocks, output_weight.reshape(N_CTX, HGROUP, D)))
    attended = (residual.astype(jnp.float32) + head_sum).astype(jnp.bfloat16)
    attended_float = attended.astype(jnp.float32)
    inverse_rms = lax.rsqrt(lax.optimization_barrier(jnp.mean(attended_float * attended_float, axis=1, keepdims=True)) + norm_eps)
    scaled = (attended_float * inverse_rms * norm_gain[None, :]).astype(jnp.bfloat16)
    scaled_blocks = scaled.reshape(token_count, N_TP, DGROUP).transpose(1, 0, 2)
    zeros_units = jnp.zeros((token_count, FF), jnp.float32)
    gate_sum, _ = lax.scan(add_terms, zeros_units, (scaled_blocks, gate_weight.reshape(N_TP, DGROUP, FF)))
    up_sum, _ = lax.scan(add_terms, zeros_units, (scaled_blocks, up_weight.reshape(N_TP, DGROUP, FF)))
    hidden = (jax.nn.silu(gate_sum) * up_sum).astype(jnp.bfloat16)
    hidden_blocks = hidden.reshape(token_count, N_CTX, FGROUP).transpose(1, 0, 2)
    down_sum, _ = lax.scan(add_terms, jnp.zeros((token_count, D), jnp.float32), (hidden_blocks, down_weight.reshape(N_CTX, FGROUP, D)))
    layer_out = (attended_float + down_sum).astype(jnp.bfloat16)
    return (attended, layer_out)
```

```python
import jax
import jax.numpy as jnp
from jax import lax
from jax.sharding import PartitionSpec as P

D = 7168
LAT = 512
ROPE = 64
VHEAD = 128


score_scale = 192.0 ** (-0.5)
rope_base = 10000.0
norm_eps = 1e-06
masked_score = -1e30


def rope_freqs(half_width):
    return rope_base ** (-jnp.arange(half_width, dtype=jnp.float32) / half_width)


def trace_info(token_index, lengths):
    trace_ends = jnp.cumsum(lengths)
    starts = trace_ends - lengths
    trace_ids = jnp.sum((token_index[:, None] >= trace_ends[None, :]).astype(jnp.int32), axis=1)
    member = trace_ids[:, None] == jnp.arange(lengths.shape[0], dtype=jnp.int32)[None, :]
    pos_shift = jnp.sum(jnp.where(member, (0 - starts)[None, :], 0), axis=1)
    return (trace_ids, token_index + pos_shift)


def rope_keys(latent, positions, latent_width):
    values = latent.astype(jnp.float32)
    half_width = (values.shape[0] - latent_width) // 2
    angles = rope_freqs(half_width)[:, None] * positions.astype(jnp.float32)[None, :]
    first_half = values[latent_width : latent_width + half_width]
    second_half = values[latent_width + half_width :]
    cosine = jnp.cos(angles)
    sine_value = jnp.sin(angles)
    return jnp.concatenate(
        [
            values[:latent_width],
            first_half * cosine - second_half * sine_value,
            first_half * sine_value + second_half * cosine,
        ],
        axis=0,
    ).astype(jnp.bfloat16)


def rope_queries(queries, positions, latent_width):
    values = queries.astype(jnp.float32)
    half_width = (values.shape[2] - latent_width) // 2
    angles = positions.astype(jnp.float32)[:, None] * rope_freqs(half_width)[None, :]
    cosine = jnp.cos(angles)[:, None, :]
    sine_value = jnp.sin(angles)[:, None, :]
    first_half = values[:, :, latent_width : latent_width + half_width]
    second_half = values[:, :, latent_width + half_width :]
    return jnp.concatenate(
        [
            values[:, :, :latent_width],
            first_half * cosine - second_half * sine_value,
            first_half * sine_value + second_half * cosine,
        ],
        axis=2,
    ).astype(jnp.bfloat16)


def score_rows(state_carry, query_block, block_index, block_trace, key_piece, key_index, key_trace):
    row_top, row_total, mixed_sum = state_carry
    allowed = (key_trace[None, :] == block_trace[:, None]) & (
        key_index[None, :] <= block_index[:, None]
    )
    scores = (
        jnp.einsum("qhe,ek->hqk", query_block, key_piece, preferred_element_type=jnp.float32)
        * score_scale
    )
    scores = jnp.where(allowed[None], scores, masked_score)
    new_top = jnp.maximum(row_top, jnp.max(scores, axis=2))
    exponent = jnp.where(allowed[None], jnp.exp(scores - new_top[:, :, None]), 0.0)
    row_total = jnp.sum(exponent, axis=2)
    mixed_sum = jnp.einsum(
        "hqk,lk->hql",
        exponent.astype(jnp.bfloat16),
        key_piece[:LAT],
        preferred_element_type=jnp.float32,
    )
    return (new_top, row_total, mixed_sum)


def swap(value, axis_name, bit):
    width = lax.axis_size(axis_name)
    return lax.ppermute(value, axis_name, [(i, i ^ bit) for i in range(width)])


def pick(value, index):
    return lax.dynamic_index_in_dim(value, index, 0, keepdims=False)


def wide(value):
    return value.astype(jnp.float32)


def matmul(a, b):
    return jnp.dot(a, b, preferred_element_type=jnp.float32).astype(jnp.bfloat16)


def spread_heads(heads_out, n_ctx, n_tp):
    pieces = heads_out.reshape(n_ctx, heads_out.shape[0] // n_ctx, heads_out.shape[1])
    return [
        lax.ppermute(
            pieces[s],
            ("ctx", "tp"),
            [(c * n_tp + t, t * n_tp + (c ^ s)) for c in range(n_ctx) for t in range(n_tp)],
        )
        for s in range(n_ctx)
    ]


def pair_rows(first, second):
    return jnp.concatenate(
        [first[0], second[1], second[0], first[1], first[2], second[3], second[2], first[3]], axis=0
    )


def reduce_ctx(kept, sent):
    came = swap(sent, "ctx", 1)
    mine = wide(kept[0]) + wide(came[0])
    other = (wide(kept[1]) + wide(came[1])).astype(jnp.bfloat16)
    return mine + wide(swap(other, "ctx", 2))


def gather_ctx(rows):
    pair = jnp.concatenate([rows, swap(rows, "ctx", 2)], axis=0)
    return jnp.concatenate([pair, swap(pair, "ctx", 1)], axis=0)


def paired_tail(
    heads_out, residual, output_weight, norm_gain, gate_weight, up_weight, down_weight, n_ctx, n_tp
):
    row_count, width = residual.shape
    half = row_count // 2
    model_width = width * n_tp
    c = lax.axis_index("ctx")
    t = lax.axis_index("tp")
    core = t & 1
    first_half = (t >> 1) ^ (c >> 1)
    own = spread_heads(heads_out, n_ctx, n_tp)
    own_all = jnp.stack(own)
    far = swap(own_all, "tp", 2)
    near = swap(own_all, "tp", 1)
    far_near = swap(far, "tp", 1)
    rows_a = pair_rows(own_all, near)
    order = [2, 3, 0, 1]
    rows_b = pair_rows([far[i] for i in order], [far_near[i] for i in order])
    residual_halves = residual.reshape(2, half, width)

    def project(rows, which):
        blocks = matmul(rows, output_weight).reshape(n_ctx, half, width)
        place = t ^ c
        head_sum = reduce_ctx(
            (pick(blocks, place), pick(blocks, place ^ 2)),
            jnp.stack([pick(blocks, place ^ 1), pick(blocks, place ^ 3)]),
        )
        attended = (wide(pick(residual_halves, which)) + head_sum).astype(jnp.bfloat16)
        return attended, gather_ctx(attended)

    attended_a, all_a = project(rows_a, first_half)
    attended_b, all_b = project(rows_b, 1 - first_half)

    def gate_up(all_rows):
        values = wide(all_rows)
        squares = jnp.sum(values * values, axis=1).reshape(2, 2 * half)
        scaled = (values * norm_gain[None, :]).astype(jnp.bfloat16)
        sums = [matmul(scaled, w).reshape(2, 2 * half, -1) for w in (gate_weight, up_weight)]
        kept, came = [], []
        for term in sums + [squares]:
            came.append(swap(pick(term, 1 - core), "tp", 1))
            kept.append(pick(term, core))
        return kept, came

    kept_a, came_a = gate_up(all_a)
    across = [
        swap((wide(k) + wide(r)).astype(k.dtype), "tp", 2) for k, r in zip(kept_a, came_a)
    ]
    kept_b, came_b = gate_up(all_b)
    gate, up, squares = [wide(k) + wide(r) + wide(x) for k, r, x in zip(kept_b, came_b, across)]
    inverse_rms = lax.rsqrt(squares / model_width + norm_eps)[:, None]
    hidden = (jax.nn.silu(gate * inverse_rms) * (up * inverse_rms)).astype(jnp.bfloat16)
    hidden_far = swap(hidden, "tp", 2)
    hidden_near = swap(hidden, "tp", 1)
    hidden_far_near = swap(hidden_far, "tp", 1)

    def down(mine, other, attended):
        blocks = matmul(jnp.concatenate([mine, other], axis=0), down_weight)
        blocks = blocks.reshape(2, 2, half, width)
        total = reduce_ctx(pick(blocks, core), pick(blocks, 1 - core))
        return (wide(attended) + total).astype(jnp.bfloat16)

    out_b = down(hidden, hidden_near, attended_b)
    out_a = down(hidden_far, hidden_far_near, attended_a)

    def in_order(a, b):
        first = first_half == 0
        return jnp.concatenate([jnp.where(first, a, b), jnp.where(first, b, a)], axis=0)

    return in_order(attended_a, attended_b), in_order(out_a, out_b)


def on_device(
    residual,
    latent,
    queries,
    lengths,
    value_weight,
    output_weight,
    norm_gain,
    gate_weight,
    up_weight,
    down_weight,
):
    row_count = residual.shape[0]
    ctx_place = lax.axis_index("ctx")
    local_heads = value_weight.shape[1] // VHEAD
    own_index = ctx_place * row_count + jnp.arange(row_count, dtype=jnp.int32)
    own_trace, own_position = trace_info(own_index, lengths)
    rotated_keys = rope_keys(latent, own_position, LAT)
    rotated_queries = rope_queries(
        queries.reshape(row_count, local_heads, LAT + ROPE), own_position, LAT
    )
    last_query = ctx_place * row_count + row_count - 1
    start_state = (
        jnp.full((local_heads, row_count), masked_score, jnp.float32),
        jnp.zeros((local_heads, row_count), jnp.float32),
        jnp.zeros((local_heads, row_count, LAT), jnp.float32),
    )
    key_piece = lax.all_gather(rotated_keys, "ctx", axis=1, tiled=True)
    key_index = jnp.arange(key_piece.shape[1], dtype=jnp.int32)
    key_trace, _ = trace_info(key_index, lengths)
    folded = lax.cond(
        jnp.int32(0) <= last_query,
        lambda held: score_rows(
            held, rotated_queries, own_index, own_trace, key_piece, key_index, key_trace
        ),
        lambda held: held,
        start_state,
    )
    row_top, row_total, mixed_sum = folded
    mixed_latent = (mixed_sum / row_total[:, :, None]).astype(jnp.bfloat16)
    heads_out = (
        jnp.einsum(
            "hql,lhd->qhd",
            mixed_latent,
            value_weight.reshape(LAT, local_heads, VHEAD),
            preferred_element_type=jnp.float32,
        )
        .astype(jnp.bfloat16)
        .reshape(row_count, local_heads * VHEAD)
    )
    n_ctx, n_tp = lax.axis_size("ctx"), lax.axis_size("tp")
    if n_ctx == 4 and n_tp == 4 and row_count % 64 == 0:
        return paired_tail(
            heads_out,
            residual,
            output_weight,
            norm_gain,
            gate_weight,
            up_weight,
            down_weight,
            n_ctx,
            n_tp,
        )
    all_heads = lax.all_gather(heads_out, "tp", axis=1, tiled=True)
    head_block = lax.all_to_all(all_heads, "ctx", split_axis=1, concat_axis=0, tiled=True)
    head_sum = lax.psum_scatter(
        jnp.dot(head_block, output_weight, preferred_element_type=jnp.float32).astype(jnp.bfloat16),
        "ctx",
        scatter_dimension=0,
        tiled=True,
    ).astype(jnp.float32)
    attended = (residual.astype(jnp.float32) + head_sum).astype(jnp.bfloat16)
    attended_float = attended.astype(jnp.float32)
    squares = lax.psum(jnp.sum(attended_float * attended_float, axis=1), "tp")
    inverse_rms = lax.rsqrt(squares / D + norm_eps)
    scaled = (attended_float * inverse_rms[:, None] * norm_gain[None, :]).astype(jnp.bfloat16)
    scaled_all = lax.all_gather(scaled, "ctx", axis=0, tiled=True)
    unit_count = gate_weight.shape[1]
    gate_up = jnp.concatenate([gate_weight, up_weight], axis=1)
    summed = lax.psum_scatter(
        jnp.dot(scaled_all, gate_up, preferred_element_type=jnp.float32).astype(jnp.bfloat16),
        "tp",
        scatter_dimension=0,
        tiled=True,
    ).astype(jnp.float32)
    hidden_share = (jax.nn.silu(summed[:, :unit_count]) * summed[:, unit_count:]).astype(
        jnp.bfloat16
    )
    hidden_all = lax.all_gather(hidden_share, "tp", axis=0, tiled=True)
    down_sum = lax.psum_scatter(
        jnp.dot(hidden_all, down_weight, preferred_element_type=jnp.float32).astype(jnp.bfloat16),
        "ctx",
        scatter_dimension=0,
        tiled=True,
    ).astype(jnp.float32)
    layer_out = (attended_float + down_sum).astype(jnp.bfloat16)
    return (attended, layer_out)


def solution(mesh):
    in_specs = (
        P(("grp", "ctx"), "tp"),
        P(None, ("grp", "ctx")),
        P(("grp", "ctx"), "tp"),
        P("grp"),
        P(None, "tp"),
        P("ctx", "tp"),
        P("tp"),
        P("tp", "ctx"),
        P("tp", "ctx"),
        P("ctx", "tp"),
    )
    out_specs = (P(("grp", "ctx"), "tp"), P(("grp", "ctx"), "tp"))
    return jax.shard_map(
        on_device, mesh=mesh, in_specs=in_specs, out_specs=out_specs, check_vma=False
    )
```

```python
import functools

import jax
import jax.numpy as jnp
from jax import lax
from jax.experimental import pallas as pl
from jax.experimental.pallas import tpu as pltpu
from jax.sharding import PartitionSpec as P

D = 7168
LAT = 512
ROPE = 64
VHEAD = 128


score_scale = 192.0 ** (-0.5)
rope_base = 10000.0
norm_eps = 1e-06
masked_score = -1e30


def rope_freqs(half_width):
    return rope_base ** (-jnp.arange(half_width, dtype=jnp.float32) / half_width)


def trace_info(token_index, lengths):
    trace_ends = jnp.cumsum(lengths)
    starts = trace_ends - lengths
    trace_ids = jnp.sum((token_index[:, None] >= trace_ends[None, :]).astype(jnp.int32), axis=1)
    member = trace_ids[:, None] == jnp.arange(lengths.shape[0], dtype=jnp.int32)[None, :]
    pos_shift = jnp.sum(jnp.where(member, (0 - starts)[None, :], 0), axis=1)
    return (trace_ids, token_index + pos_shift)


def rope_keys(latent, positions, latent_width):
    values = latent.astype(jnp.float32)
    half_width = (values.shape[0] - latent_width) // 2
    angles = rope_freqs(half_width)[:, None] * positions.astype(jnp.float32)[None, :]
    first_half = values[latent_width : latent_width + half_width]
    second_half = values[latent_width + half_width :]
    cosine = jnp.cos(angles)
    sine_value = jnp.sin(angles)
    return jnp.concatenate(
        [
            values[:latent_width],
            first_half * cosine - second_half * sine_value,
            first_half * sine_value + second_half * cosine,
        ],
        axis=0,
    ).astype(jnp.bfloat16)


def rope_tables(positions, half_width, lanes):
    angles = positions.astype(jnp.float32)[:, None] * rope_freqs(half_width)[None, :]
    cosine, sine_value = jnp.cos(angles), jnp.sin(angles)
    cos_part = jnp.concatenate([cosine, cosine], axis=1)
    sin_part = jnp.concatenate([-sine_value, sine_value], axis=1)
    rest = lanes - 2 * half_width
    ones = jnp.ones((angles.shape[0], rest), jnp.float32)
    zeros = jnp.zeros((angles.shape[0], rest), jnp.float32)
    return jnp.stack(
        [
            jnp.concatenate([cos_part, ones], axis=1),
            jnp.concatenate([sin_part, zeros], axis=1),
            jnp.concatenate([ones, cos_part], axis=1),
            jnp.concatenate([zeros, sin_part], axis=1),
        ]
    )


def attention_kernel(
    group, tables, starts, own_index, key_index, keys, queries, value_weight, out, even, odd, values, bias
):
    row_count = queries.shape[0]
    width = queries.shape[1] // group
    half_width = (width - LAT) // 2
    lanes = 2 * (width - LAT)

    @pl.when(pl.program_id(0) == 0)
    def prepare():
        all_keys = keys[...]
        pad = jnp.zeros((width - LAT, all_keys.shape[1]), jnp.bfloat16)
        even[:width] = all_keys
        even[width:] = pad
        odd[: width - LAT] = pad
        odd[width - LAT :] = all_keys
        values[...] = keys[:LAT].astype(jnp.float32).T.astype(jnp.bfloat16)
        allowed = (key_index[...] >= starts[...]) & (key_index[...] <= own_index[...])
        bias[...] = jnp.where(allowed, 0.0, masked_score)

    lane = lax.broadcasted_iota(jnp.int32, (row_count, lanes), 1)
    low = (lane & (2 * half_width - 1)) < half_width

    def turned(start, which):
        entry = queries[:, start : start + lanes].astype(jnp.float32)
        partner = jnp.where(
            low, pltpu.roll(entry, lanes - half_width, 1), pltpu.roll(entry, half_width, 1)
        )
        return (entry * tables[2 * which] + partner * tables[2 * which + 1]).astype(jnp.bfloat16)

    for which, key_rows in ((0, even), (1, odd)):
        rows = []
        for head in range(which, group, 2):
            base = (head - which) * width
            if which == 0:
                rows.append(
                    jnp.concatenate([queries[:, base : base + LAT], turned(base + LAT, 0)], axis=1)
                )
            else:
                first = base + LAT
                rows.append(
                    jnp.concatenate(
                        [queries[:, first : first + LAT], turned(first + LAT, 1)], axis=1
                    )
                )
        stacked = jnp.concatenate(rows, axis=0)
        scores = jnp.dot(stacked, key_rows[...], preferred_element_type=jnp.float32)
        scores = scores.reshape(len(rows), row_count, -1) + bias[...][None]
        top = jnp.max(scores, axis=2, keepdims=True)
        exponent = jnp.exp((scores - top) * score_scale)
        total = jnp.sum(exponent, axis=2, keepdims=True).reshape(len(rows) * row_count, 1)
        weights = exponent.astype(jnp.bfloat16).reshape(len(rows) * row_count, -1)
        mixed = jnp.dot(weights, values[...], preferred_element_type=jnp.float32)
        mixed = (mixed / total).astype(jnp.bfloat16)
        for i in range(len(rows)):
            head = 2 * i + which
            out[:, head * VHEAD : (head + 1) * VHEAD] = jnp.dot(
                mixed[i * row_count : (i + 1) * row_count],
                value_weight[:, head * VHEAD : (head + 1) * VHEAD],
                preferred_element_type=jnp.float32,
            ).astype(jnp.bfloat16)


def attention(queries, keys, key_index, own_index, own_position, value_weight):
    row_count, query_width = queries.shape
    local_heads = value_weight.shape[1] // VHEAD
    width = query_width // local_heads
    group = 4 if local_heads % 4 == 0 else 2
    key_count = keys.shape[1]
    tables = rope_tables(own_position, (width - LAT) // 2, 2 * (width - LAT))
    whole = lambda shape: pl.BlockSpec(shape, lambda i: (0,) * len(shape))
    deep = 2 * width - LAT
    return pl.pallas_call(
        functools.partial(attention_kernel, group),
        grid=(local_heads // group,),
        in_specs=[
            whole(tables.shape),
            whole((row_count, 1)),
            whole((row_count, 1)),
            whole((1, key_count)),
            whole(keys.shape),
            pl.BlockSpec((row_count, group * width), lambda i: (0, i)),
            pl.BlockSpec((LAT, group * VHEAD), lambda i: (0, i)),
        ],
        out_specs=pl.BlockSpec((row_count, group * VHEAD), lambda i: (0, i)),
        out_shape=jax.ShapeDtypeStruct((row_count, local_heads * VHEAD), jnp.bfloat16),
        scratch_shapes=[
            pltpu.VMEM((deep, key_count), jnp.bfloat16),
            pltpu.VMEM((deep, key_count), jnp.bfloat16),
            pltpu.VMEM((key_count, LAT), jnp.bfloat16),
            pltpu.VMEM((row_count, key_count), jnp.float32),
        ],
        compiler_params=pltpu.CompilerParams(vmem_limit_bytes=40 * 1024 * 1024),
        cost_estimate=pl.CostEstimate(
            flops=2 * row_count * local_heads * (key_count * (deep + LAT) + LAT * VHEAD),
            bytes_accessed=2 * (queries.size + keys.size + value_weight.size),
            transcendentals=row_count * local_heads * key_count,
        ),
    )(
        tables,
        (own_index - own_position)[:, None],
        own_index[:, None],
        key_index[None, :],
        keys,
        queries,
        value_weight,
    )


def swap(value, axis_name, bit):
    width = lax.axis_size(axis_name)
    return lax.ppermute(value, axis_name, [(i, i ^ bit) for i in range(width)])


def pick(value, index):
    return lax.dynamic_index_in_dim(value, index, 0, keepdims=False)


def wide(value):
    return value.astype(jnp.float32)


def matmul(a, b):
    return jnp.dot(a, b, preferred_element_type=jnp.float32).astype(jnp.bfloat16)


def gather_keys(rotated_keys, n_ctx):
    rows = rotated_keys.shape[0] // 2
    core = lax.axis_index("tp") & 1
    half = lax.dynamic_slice_in_dim(rotated_keys, core * rows, rows, 0)
    came = [
        lax.ppermute(half, "ctx", [(c, c + d) for c in range(n_ctx - d)])
        for d in range(n_ctx - 1, 0, -1)
    ]
    mine = jnp.concatenate(came, axis=1)
    other = swap(mine, "tp", 1)
    before = jnp.concatenate(
        [jnp.where(core == 0, mine, other), jnp.where(core == 0, other, mine)], axis=0
    )
    return jnp.concatenate([before, rotated_keys], axis=1)


def spread_heads(heads_out, n_ctx, n_tp):
    pieces = heads_out.reshape(n_ctx, heads_out.shape[0] // n_ctx, heads_out.shape[1])
    return [
        lax.ppermute(
            pieces[s],
            ("ctx", "tp"),
            [(c * n_tp + t, t * n_tp + (c ^ s)) for c in range(n_ctx) for t in range(n_tp)],
        )
        for s in range(n_ctx)
    ]


def pair_rows(first, second):
    return jnp.concatenate(
        [first[0], second[1], second[0], first[1], first[2], second[3], second[2], first[3]], axis=0
    )


def reduce_ctx(kept, sent):
    came = swap(sent, "ctx", 1)
    mine = wide(kept[0]) + wide(came[0])
    other = (wide(kept[1]) + wide(came[1])).astype(jnp.bfloat16)
    return mine + wide(swap(other, "ctx", 2))


def gather_ctx(rows):
    pair = jnp.concatenate([rows, swap(rows, "ctx", 2)], axis=0)
    return jnp.concatenate([pair, swap(pair, "ctx", 1)], axis=0)


def paired_tail(
    heads_out, residual, output_weight, norm_gain, gate_weight, up_weight, down_weight, n_ctx, n_tp
):
    row_count, width = residual.shape
    half = row_count // 2
    model_width = width * n_tp
    c = lax.axis_index("ctx")
    t = lax.axis_index("tp")
    core = t & 1
    first_half = (t >> 1) ^ (c >> 1)
    own = spread_heads(heads_out, n_ctx, n_tp)
    own_all = jnp.stack(own)
    far = swap(own_all, "tp", 2)
    near = swap(own_all, "tp", 1)
    far_near = swap(far, "tp", 1)
    rows_a = pair_rows(own_all, near)
    order = [2, 3, 0, 1]
    rows_b = pair_rows([far[i] for i in order], [far_near[i] for i in order])
    residual_halves = residual.reshape(2, half, width)

    def project(rows, which):
        blocks = matmul(rows, output_weight).reshape(n_ctx, half, width)
        place = t ^ c
        head_sum = reduce_ctx(
            (pick(blocks, place), pick(blocks, place ^ 2)),
            jnp.stack([pick(blocks, place ^ 1), pick(blocks, place ^ 3)]),
        )
        attended = (wide(pick(residual_halves, which)) + head_sum).astype(jnp.bfloat16)
        return attended, gather_ctx(attended)

    attended_a, all_a = project(rows_a, first_half)
    attended_b, all_b = project(rows_b, 1 - first_half)

    def gate_up(all_rows):
        values = wide(all_rows)
        squares = jnp.sum(values * values, axis=1).reshape(2, 2 * half)
        scaled = (values * norm_gain[None, :]).astype(jnp.bfloat16)
        sums = [matmul(scaled, w).reshape(2, 2 * half, -1) for w in (gate_weight, up_weight)]
        kept, came = [], []
        for term in sums + [squares]:
            came.append(swap(pick(term, 1 - core), "tp", 1))
            kept.append(pick(term, core))
        return kept, came

    kept_a, came_a = gate_up(all_a)
    across = [
        swap((wide(k) + wide(r)).astype(k.dtype), "tp", 2) for k, r in zip(kept_a, came_a)
    ]
    kept_b, came_b = gate_up(all_b)
    gate, up, squares = [wide(k) + wide(r) + wide(x) for k, r, x in zip(kept_b, came_b, across)]
    inverse_rms = lax.rsqrt(squares / model_width + norm_eps)[:, None]
    hidden = (jax.nn.silu(gate * inverse_rms) * (up * inverse_rms)).astype(jnp.bfloat16)
    hidden_far = swap(hidden, "tp", 2)
    hidden_near = swap(hidden, "tp", 1)
    hidden_far_near = swap(hidden_far, "tp", 1)

    def down(mine, other, attended):
        blocks = matmul(jnp.concatenate([mine, other], axis=0), down_weight)
        blocks = blocks.reshape(2, 2, half, width)
        total = reduce_ctx(pick(blocks, core), pick(blocks, 1 - core))
        return (wide(attended) + total).astype(jnp.bfloat16)

    out_b = down(hidden, hidden_near, attended_b)
    out_a = down(hidden_far, hidden_far_near, attended_a)

    def in_order(a, b):
        first = first_half == 0
        return jnp.concatenate([jnp.where(first, a, b), jnp.where(first, b, a)], axis=0)

    return in_order(attended_a, attended_b), in_order(out_a, out_b)


def on_device(
    residual,
    latent,
    queries,
    lengths,
    value_weight,
    output_weight,
    norm_gain,
    gate_weight,
    up_weight,
    down_weight,
):
    row_count = residual.shape[0]
    ctx_place = lax.axis_index("ctx")
    n_ctx, n_tp = lax.axis_size("ctx"), lax.axis_size("tp")
    paired = n_ctx == 4 and n_tp == 4 and row_count % 64 == 0
    own_index = ctx_place * row_count + jnp.arange(row_count, dtype=jnp.int32)
    _, own_position = trace_info(own_index, lengths)
    rotated_keys = rope_keys(latent, own_position, LAT)
    key_order = jnp.arange(n_ctx * row_count, dtype=jnp.int32)
    if paired:
        keys = gather_keys(rotated_keys, n_ctx)
        key_index = key_order + (ctx_place - (n_ctx - 1)) * row_count
    else:
        keys = lax.all_gather(rotated_keys, "ctx", axis=1, tiled=True)
        key_index = key_order
    heads_out = attention(queries, keys, key_index, own_index, own_position, value_weight)
    if paired:
        return paired_tail(
            heads_out,
            residual,
            output_weight,
            norm_gain,
            gate_weight,
            up_weight,
            down_weight,
            n_ctx,
            n_tp,
        )
    all_heads = lax.all_gather(heads_out, "tp", axis=1, tiled=True)
    head_block = lax.all_to_all(all_heads, "ctx", split_axis=1, concat_axis=0, tiled=True)
    head_sum = lax.psum_scatter(
        jnp.dot(head_block, output_weight, preferred_element_type=jnp.float32).astype(jnp.bfloat16),
        "ctx",
        scatter_dimension=0,
        tiled=True,
    ).astype(jnp.float32)
    attended = (residual.astype(jnp.float32) + head_sum).astype(jnp.bfloat16)
    attended_float = attended.astype(jnp.float32)
    squares = lax.psum(jnp.sum(attended_float * attended_float, axis=1), "tp")
    inverse_rms = lax.rsqrt(squares / D + norm_eps)
    scaled = (attended_float * inverse_rms[:, None] * norm_gain[None, :]).astype(jnp.bfloat16)
    scaled_all = lax.all_gather(scaled, "ctx", axis=0, tiled=True)
    unit_count = gate_weight.shape[1]
    gate_up = jnp.concatenate([gate_weight, up_weight], axis=1)
    summed = lax.psum_scatter(
        jnp.dot(scaled_all, gate_up, preferred_element_type=jnp.float32).astype(jnp.bfloat16),
        "tp",
        scatter_dimension=0,
        tiled=True,
    ).astype(jnp.float32)
    hidden_share = (jax.nn.silu(summed[:, :unit_count]) * summed[:, unit_count:]).astype(
        jnp.bfloat16
    )
    hidden_all = lax.all_gather(hidden_share, "tp", axis=0, tiled=True)
    down_sum = lax.psum_scatter(
        jnp.dot(hidden_all, down_weight, preferred_element_type=jnp.float32).astype(jnp.bfloat16),
        "ctx",
        scatter_dimension=0,
        tiled=True,
    ).astype(jnp.float32)
    layer_out = (attended_float + down_sum).astype(jnp.bfloat16)
    return (attended, layer_out)


def solution(mesh):
    in_specs = (
        P(("grp", "ctx"), "tp"),
        P(None, ("grp", "ctx")),
        P(("grp", "ctx"), "tp"),
        P("grp"),
        P(None, "tp"),
        P("ctx", "tp"),
        P("tp"),
        P("tp", "ctx"),
        P("tp", "ctx"),
        P("ctx", "tp"),
    )
    out_specs = (P(("grp", "ctx"), "tp"), P(("grp", "ctx"), "tp"))
    return jax.shard_map(
        on_device, mesh=mesh, in_specs=in_specs, out_specs=out_specs, check_vma=False
    )
```

```python
import functools

import jax
import jax.numpy as jnp
from jax import lax
from jax.experimental import pallas as pl
from jax.experimental.pallas import tpu as pltpu
from jax.sharding import PartitionSpec as P

D = 7168
LAT = 512
ROPE = 64
VHEAD = 128


score_scale = 192.0 ** (-0.5)
rope_base = 10000.0
norm_eps = 1e-06
masked_score = -1e30


def rope_freqs(half_width):
    return rope_base ** (-jnp.arange(half_width, dtype=jnp.float32) / half_width)


def trace_info(token_index, lengths):
    trace_ends = jnp.cumsum(lengths)
    starts = trace_ends - lengths
    trace_ids = jnp.sum((token_index[:, None] >= trace_ends[None, :]).astype(jnp.int32), axis=1)
    member = trace_ids[:, None] == jnp.arange(lengths.shape[0], dtype=jnp.int32)[None, :]
    pos_shift = jnp.sum(jnp.where(member, (0 - starts)[None, :], 0), axis=1)
    return (trace_ids, token_index + pos_shift)


def rope_keys(latent, positions, latent_width):
    values = latent.astype(jnp.float32)
    half_width = (values.shape[0] - latent_width) // 2
    angles = rope_freqs(half_width)[:, None] * positions.astype(jnp.float32)[None, :]
    first_half = values[latent_width : latent_width + half_width]
    second_half = values[latent_width + half_width :]
    cosine = jnp.cos(angles)
    sine_value = jnp.sin(angles)
    return jnp.concatenate(
        [
            values[:latent_width],
            first_half * cosine - second_half * sine_value,
            first_half * sine_value + second_half * cosine,
        ],
        axis=0,
    ).astype(jnp.bfloat16)


def rope_tables(positions, half_width, lanes):
    angles = positions.astype(jnp.float32)[:, None] * rope_freqs(half_width)[None, :]
    cosine, sine_value = jnp.cos(angles), jnp.sin(angles)
    cos_part = jnp.concatenate([cosine, cosine], axis=1)
    sin_part = jnp.concatenate([-sine_value, sine_value], axis=1)
    rest = lanes - 2 * half_width
    ones = jnp.ones((angles.shape[0], rest), jnp.float32)
    zeros = jnp.zeros((angles.shape[0], rest), jnp.float32)
    return jnp.stack(
        [
            jnp.concatenate([cos_part, ones], axis=1),
            jnp.concatenate([sin_part, zeros], axis=1),
            jnp.concatenate([ones, cos_part], axis=1),
            jnp.concatenate([zeros, sin_part], axis=1),
        ]
    )


def attention_kernel(
    group, tables, starts, own_index, key_index, keys, queries, value_weight, out, even, odd, values, bias
):
    row_count = queries.shape[0]
    width = queries.shape[1] // group
    half_width = (width - LAT) // 2
    lanes = 2 * (width - LAT)

    @pl.when(pl.program_id(0) == 0)
    def prepare():
        all_keys = keys[...]
        pad = jnp.zeros((width - LAT, all_keys.shape[1]), jnp.bfloat16)
        even[:width] = all_keys
        even[width:] = pad
        odd[: width - LAT] = pad
        odd[width - LAT :] = all_keys
        values[...] = keys[:LAT].astype(jnp.float32).T.astype(jnp.bfloat16)
        allowed = (key_index[...] >= starts[...]) & (key_index[...] <= own_index[...])
        bias[...] = jnp.where(allowed, 0.0, masked_score)

    lane = lax.broadcasted_iota(jnp.int32, (row_count, lanes), 1)
    low = (lane & (2 * half_width - 1)) < half_width

    def turned(start, which):
        entry = queries[:, start : start + lanes].astype(jnp.float32)
        partner = jnp.where(
            low, pltpu.roll(entry, lanes - half_width, 1), pltpu.roll(entry, half_width, 1)
        )
        return (entry * tables[2 * which] + partner * tables[2 * which + 1]).astype(jnp.bfloat16)

    for which, key_rows in ((0, even), (1, odd)):
        rows = []
        for head in range(which, group, 2):
            base = (head - which) * width
            if which == 0:
                rows.append(
                    jnp.concatenate([queries[:, base : base + LAT], turned(base + LAT, 0)], axis=1)
                )
            else:
                first = base + LAT
                rows.append(
                    jnp.concatenate(
                        [queries[:, first : first + LAT], turned(first + LAT, 1)], axis=1
                    )
                )
        stacked = jnp.concatenate(rows, axis=0)
        scores = jnp.dot(stacked, key_rows[...], preferred_element_type=jnp.float32)
        scores = scores.reshape(len(rows), row_count, -1) + bias[...][None]
        top = jnp.max(scores, axis=2, keepdims=True)
        exponent = jnp.exp((scores - top) * score_scale)
        total = jnp.sum(exponent, axis=2, keepdims=True).reshape(len(rows) * row_count, 1)
        weights = exponent.astype(jnp.bfloat16).reshape(len(rows) * row_count, -1)
        mixed = jnp.dot(weights, values[...], preferred_element_type=jnp.float32)
        mixed = (mixed / total).astype(jnp.bfloat16)
        for i in range(len(rows)):
            head = 2 * i + which
            out[:, head * VHEAD : (head + 1) * VHEAD] = jnp.dot(
                mixed[i * row_count : (i + 1) * row_count],
                value_weight[:, head * VHEAD : (head + 1) * VHEAD],
                preferred_element_type=jnp.float32,
            ).astype(jnp.bfloat16)


def attention(queries, keys, key_index, own_index, own_position, value_weight):
    row_count, query_width = queries.shape
    local_heads = value_weight.shape[1] // VHEAD
    width = query_width // local_heads
    group = 4 if local_heads % 4 == 0 else 2
    key_count = keys.shape[1]
    tables = rope_tables(own_position, (width - LAT) // 2, 2 * (width - LAT))
    whole = lambda shape: pl.BlockSpec(shape, lambda i: (0,) * len(shape))
    deep = 2 * width - LAT
    return pl.pallas_call(
        functools.partial(attention_kernel, group),
        grid=(local_heads // group,),
        in_specs=[
            whole(tables.shape),
            whole((row_count, 1)),
            whole((row_count, 1)),
            whole((1, key_count)),
            whole(keys.shape),
            pl.BlockSpec((row_count, group * width), lambda i: (0, i)),
            pl.BlockSpec((LAT, group * VHEAD), lambda i: (0, i)),
        ],
        out_specs=pl.BlockSpec((row_count, group * VHEAD), lambda i: (0, i)),
        out_shape=jax.ShapeDtypeStruct((row_count, local_heads * VHEAD), jnp.bfloat16),
        scratch_shapes=[
            pltpu.VMEM((deep, key_count), jnp.bfloat16),
            pltpu.VMEM((deep, key_count), jnp.bfloat16),
            pltpu.VMEM((key_count, LAT), jnp.bfloat16),
            pltpu.VMEM((row_count, key_count), jnp.float32),
        ],
        compiler_params=pltpu.CompilerParams(vmem_limit_bytes=40 * 1024 * 1024),
        cost_estimate=pl.CostEstimate(
            flops=2 * row_count * local_heads * (key_count * (deep + LAT) + LAT * VHEAD),
            bytes_accessed=2 * (queries.size + keys.size + value_weight.size),
            transcendentals=row_count * local_heads * key_count,
        ),
    )(
        tables,
        (own_index - own_position)[:, None],
        own_index[:, None],
        key_index[None, :],
        keys,
        queries,
        value_weight,
    )


def swap(value, axis_name, bit):
    width = lax.axis_size(axis_name)
    return lax.ppermute(value, axis_name, [(i, i ^ bit) for i in range(width)])


def pick(value, index):
    return lax.dynamic_index_in_dim(value, index, 0, keepdims=False)


def wide(value):
    return value.astype(jnp.float32)


def matmul(a, b):
    return jnp.dot(a, b, preferred_element_type=jnp.float32).astype(jnp.bfloat16)


def gather_keys(rotated_keys, n_ctx):
    rows = rotated_keys.shape[0] // 2
    core = lax.axis_index("tp") & 1
    half = lax.dynamic_slice_in_dim(rotated_keys, core * rows, rows, 0)
    came = [
        lax.ppermute(half, "ctx", [(c, c + d) for c in range(n_ctx - d)])
        for d in range(n_ctx - 1, 0, -1)
    ]
    mine = jnp.concatenate(came, axis=1)
    other = swap(mine, "tp", 1)
    before = jnp.concatenate(
        [jnp.where(core == 0, mine, other), jnp.where(core == 0, other, mine)], axis=0
    )
    return jnp.concatenate([before, rotated_keys], axis=1)


def spread_heads(heads_out, n_ctx, n_tp):
    pieces = heads_out.reshape(n_ctx, heads_out.shape[0] // n_ctx, heads_out.shape[1])
    return [
        lax.ppermute(
            pieces[s],
            ("ctx", "tp"),
            [(c * n_tp + t, t * n_tp + (c ^ s)) for c in range(n_ctx) for t in range(n_tp)],
        )
        for s in range(n_ctx)
    ]


def pair_rows(first, second):
    return jnp.concatenate(
        [first[0], second[1], second[0], first[1], first[2], second[3], second[2], first[3]], axis=0
    )


def after(value, earlier):
    return lax.optimization_barrier((value, earlier))[0]


def reduce_ctx(block_of, n_ctx):
    c = lax.axis_index("ctx")
    right = left = None
    hops = []
    for s in range(1, n_ctx):
        to_right = block_of(jnp.minimum(n_ctx + c - s, n_ctx - 1))
        to_left = block_of(jnp.maximum(c + s - n_ctx, 0))
        if s > 1:
            to_right = (wide(to_right) + wide(right)).astype(jnp.bfloat16)
            to_left = (wide(to_left) + wide(left)).astype(jnp.bfloat16)
        right = lax.ppermute(to_right, "ctx", [(i, i + 1) for i in range(s)])
        left = lax.ppermute(to_left, "ctx", [(i, i - 1) for i in range(n_ctx - s, n_ctx)])
        hops.append(right)
    return wide(block_of(c)) + wide(right) + wide(left), hops


def gather_ctx(rows, n_ctx):
    c = lax.axis_index("ctx")
    right = left = rows
    from_left, from_right = [], []
    for s in range(1, n_ctx):
        right = lax.ppermute(right, "ctx", [(i, i + 1) for i in range(s - 1, n_ctx - 1)])
        left = lax.ppermute(left, "ctx", [(i, i - 1) for i in range(1, n_ctx - s + 1)])
        from_left.append(right)
        from_right.append(left)

    def block(place):
        return lax.select_n(
            c,
            *[
                rows if i == place else from_left[i - place - 1] if i > place else from_right[place - i - 1]
                for i in range(n_ctx)
            ],
        )

    return jnp.concatenate([block(i) for i in range(n_ctx)], axis=0)


def paired_tail(
    heads_out, residual, output_weight, norm_gain, gate_weight, up_weight, down_weight, n_ctx, n_tp
):
    row_count, width = residual.shape
    half = row_count // 2
    model_width = width * n_tp
    c = lax.axis_index("ctx")
    t = lax.axis_index("tp")
    core = t & 1
    first_half = (t >> 1) ^ (c >> 1)
    own = spread_heads(heads_out, n_ctx, n_tp)
    own_all = jnp.stack(own)
    near = swap(own_all, "tp", 1)
    far = swap(own_all, "tp", 2)
    residual_halves = residual.reshape(2, half, width)

    def sum_heads(blocks, which):
        head_sum, hops = reduce_ctx(lambda i: pick(blocks, t ^ i), n_ctx)
        return (wide(pick(residual_halves, which)) + head_sum).astype(jnp.bfloat16), hops

    blocks_a = matmul(pair_rows(own_all, near), output_weight).reshape(n_ctx, half, width)
    attended_a, hops_a = sum_heads(blocks_a, first_half)
    far = after(far, hops_a[0])
    far_near = swap(far, "tp", 1)
    order = [2, 3, 0, 1]
    rows_b = pair_rows([far[i] for i in order], [far_near[i] for i in order])
    blocks_b = matmul(rows_b, output_weight).reshape(n_ctx, half, width)
    all_a = gather_ctx(attended_a, n_ctx)
    attended_b, _ = sum_heads(after(blocks_b, attended_a), 1 - first_half)

    def gate_up(all_rows):
        values = wide(all_rows)
        squares = jnp.sum(values * values, axis=1).reshape(2, 2 * half)
        scaled = (values * norm_gain[None, :]).astype(jnp.bfloat16)
        sums = [matmul(scaled, w).reshape(2, 2 * half, -1) for w in (gate_weight, up_weight)]
        kept, came = [], []
        for term in sums + [squares]:
            came.append(swap(pick(term, 1 - core), "tp", 1))
            kept.append(pick(term, core))
        return kept, came

    kept_a, came_a = gate_up(all_a)
    across = [
        swap((wide(k) + wide(r)).astype(k.dtype), "tp", 2) for k, r in zip(kept_a, came_a)
    ]
    all_b = gather_ctx(attended_b, n_ctx)
    kept_b, came_b = gate_up(all_b)
    gate, up, squares = [wide(k) + wide(r) + wide(x) for k, r, x in zip(kept_b, came_b, across)]
    inverse_rms = lax.rsqrt(squares / model_width + norm_eps)[:, None]
    hidden = (jax.nn.silu(gate * inverse_rms) * (up * inverse_rms)).astype(jnp.bfloat16)
    hidden_near = swap(hidden, "tp", 1)
    hidden_far = swap(hidden, "tp", 2)

    def down(mine, other):
        return matmul(jnp.concatenate([mine, other], axis=0), down_weight).reshape(n_ctx, half, width)

    def finish(blocks, attended):
        total, hops = reduce_ctx(lambda i: pick(blocks, i ^ (2 * core)), n_ctx)
        return (wide(attended) + total).astype(jnp.bfloat16), hops

    down_b = down(hidden, hidden_near)
    out_b, hops_b = finish(down_b, attended_b)
    hidden_far = after(hidden_far, hops_b[0])
    hidden_far_near = swap(hidden_far, "tp", 1)
    out_a, _ = finish(down(hidden_far, hidden_far_near), attended_a)

    def in_order(a, b):
        first = first_half == 0
        return jnp.concatenate([jnp.where(first, a, b), jnp.where(first, b, a)], axis=0)

    return in_order(attended_a, attended_b), in_order(out_a, out_b)


def on_device(
    residual,
    latent,
    queries,
    lengths,
    value_weight,
    output_weight,
    norm_gain,
    gate_weight,
    up_weight,
    down_weight,
):
    row_count = residual.shape[0]
    ctx_place = lax.axis_index("ctx")
    n_ctx, n_tp = lax.axis_size("ctx"), lax.axis_size("tp")
    paired = n_ctx == 4 and n_tp == 4 and row_count % 64 == 0
    own_index = ctx_place * row_count + jnp.arange(row_count, dtype=jnp.int32)
    _, own_position = trace_info(own_index, lengths)
    rotated_keys = rope_keys(latent, own_position, LAT)
    key_order = jnp.arange(n_ctx * row_count, dtype=jnp.int32)
    if paired:
        keys = gather_keys(rotated_keys, n_ctx)
        key_index = key_order + (ctx_place - (n_ctx - 1)) * row_count
    else:
        keys = lax.all_gather(rotated_keys, "ctx", axis=1, tiled=True)
        key_index = key_order
    heads_out = attention(queries, keys, key_index, own_index, own_position, value_weight)
    if paired:
        return paired_tail(
            heads_out,
            residual,
            output_weight,
            norm_gain,
            gate_weight,
            up_weight,
            down_weight,
            n_ctx,
            n_tp,
        )
    all_heads = lax.all_gather(heads_out, "tp", axis=1, tiled=True)
    head_block = lax.all_to_all(all_heads, "ctx", split_axis=1, concat_axis=0, tiled=True)
    head_sum = lax.psum_scatter(
        jnp.dot(head_block, output_weight, preferred_element_type=jnp.float32).astype(jnp.bfloat16),
        "ctx",
        scatter_dimension=0,
        tiled=True,
    ).astype(jnp.float32)
    attended = (residual.astype(jnp.float32) + head_sum).astype(jnp.bfloat16)
    attended_float = attended.astype(jnp.float32)
    squares = lax.psum(jnp.sum(attended_float * attended_float, axis=1), "tp")
    inverse_rms = lax.rsqrt(squares / D + norm_eps)
    scaled = (attended_float * inverse_rms[:, None] * norm_gain[None, :]).astype(jnp.bfloat16)
    scaled_all = lax.all_gather(scaled, "ctx", axis=0, tiled=True)
    unit_count = gate_weight.shape[1]
    gate_up = jnp.concatenate([gate_weight, up_weight], axis=1)
    summed = lax.psum_scatter(
        jnp.dot(scaled_all, gate_up, preferred_element_type=jnp.float32).astype(jnp.bfloat16),
        "tp",
        scatter_dimension=0,
        tiled=True,
    ).astype(jnp.float32)
    hidden_share = (jax.nn.silu(summed[:, :unit_count]) * summed[:, unit_count:]).astype(
        jnp.bfloat16
    )
    hidden_all = lax.all_gather(hidden_share, "tp", axis=0, tiled=True)
    down_sum = lax.psum_scatter(
        jnp.dot(hidden_all, down_weight, preferred_element_type=jnp.float32).astype(jnp.bfloat16),
        "ctx",
        scatter_dimension=0,
        tiled=True,
    ).astype(jnp.float32)
    layer_out = (attended_float + down_sum).astype(jnp.bfloat16)
    return (attended, layer_out)


def solution(mesh):
    in_specs = (
        P(("grp", "ctx"), "tp"),
        P(None, ("grp", "ctx")),
        P(("grp", "ctx"), "tp"),
        P("grp"),
        P(None, "tp"),
        P("ctx", "tp"),
        P("tp"),
        P("tp", "ctx"),
        P("tp", "ctx"),
        P("ctx", "tp"),
    )
    out_specs = (P(("grp", "ctx"), "tp"), P(("grp", "ctx"), "tp"))
    return jax.shard_map(
        on_device, mesh=mesh, in_specs=in_specs, out_specs=out_specs, check_vma=False
    )
```

```python
import functools

import jax
import jax.numpy as jnp
from jax import lax
from jax.experimental import pallas as pl
from jax.experimental.pallas import tpu as pltpu
from jax.sharding import PartitionSpec as P

D = 7168
LAT = 512
ROPE = 64
VHEAD = 128


score_scale = 192.0 ** (-0.5)
rope_base = 10000.0
norm_eps = 1e-06
masked_score = -1e30


def rope_freqs(half_width):
    return rope_base ** (-jnp.arange(half_width, dtype=jnp.float32) / half_width)


def trace_info(token_index, lengths):
    trace_ends = jnp.cumsum(lengths)
    starts = trace_ends - lengths
    trace_ids = jnp.sum((token_index[:, None] >= trace_ends[None, :]).astype(jnp.int32), axis=1)
    member = trace_ids[:, None] == jnp.arange(lengths.shape[0], dtype=jnp.int32)[None, :]
    pos_shift = jnp.sum(jnp.where(member, (0 - starts)[None, :], 0), axis=1)
    return (trace_ids, token_index + pos_shift)


def rope_keys(latent, positions, latent_width):
    values = latent.astype(jnp.float32)
    half_width = (values.shape[0] - latent_width) // 2
    angles = rope_freqs(half_width)[:, None] * positions.astype(jnp.float32)[None, :]
    first_half = values[latent_width : latent_width + half_width]
    second_half = values[latent_width + half_width :]
    cosine = jnp.cos(angles)
    sine_value = jnp.sin(angles)
    return jnp.concatenate(
        [
            values[:latent_width],
            first_half * cosine - second_half * sine_value,
            first_half * sine_value + second_half * cosine,
        ],
        axis=0,
    ).astype(jnp.bfloat16)


def rope_tables(positions, half_width, lanes):
    angles = positions.astype(jnp.float32)[:, None] * rope_freqs(half_width)[None, :]
    cosine, sine_value = jnp.cos(angles), jnp.sin(angles)
    cos_part = jnp.concatenate([cosine, cosine], axis=1)
    sin_part = jnp.concatenate([-sine_value, sine_value], axis=1)
    rest = lanes - 2 * half_width
    ones = jnp.ones((angles.shape[0], rest), jnp.float32)
    zeros = jnp.zeros((angles.shape[0], rest), jnp.float32)
    return jnp.stack(
        [
            jnp.concatenate([cos_part, ones], axis=1),
            jnp.concatenate([sin_part, zeros], axis=1),
            jnp.concatenate([ones, cos_part], axis=1),
            jnp.concatenate([zeros, sin_part], axis=1),
        ]
    )


def attention_kernel(
    group, tables, starts, own_index, key_index, keys, queries, value_weight, out, even, odd, values, bias
):
    row_count = queries.shape[0]
    width = queries.shape[1] // group
    half_width = (width - LAT) // 2
    lanes = 2 * (width - LAT)

    @pl.when(pl.program_id(0) == 0)
    def prepare():
        all_keys = keys[...]
        pad = jnp.zeros((width - LAT, all_keys.shape[1]), jnp.bfloat16)
        even[:width] = all_keys
        even[width:] = pad
        odd[: width - LAT] = pad
        odd[width - LAT :] = all_keys
        values[...] = keys[:LAT].astype(jnp.float32).T.astype(jnp.bfloat16)
        allowed = (key_index[...] >= starts[...]) & (key_index[...] <= own_index[...])
        bias[...] = jnp.where(allowed, 0.0, masked_score)

    lane = lax.broadcasted_iota(jnp.int32, (row_count, lanes), 1)
    low = (lane & (2 * half_width - 1)) < half_width

    def turned(start, which):
        entry = queries[:, start : start + lanes].astype(jnp.float32)
        partner = jnp.where(
            low, pltpu.roll(entry, lanes - half_width, 1), pltpu.roll(entry, half_width, 1)
        )
        return (entry * tables[2 * which] + partner * tables[2 * which + 1]).astype(jnp.bfloat16)

    for which, key_rows in ((0, even), (1, odd)):
        rows = []
        for head in range(which, group, 2):
            base = (head - which) * width
            if which == 0:
                rows.append(
                    jnp.concatenate([queries[:, base : base + LAT], turned(base + LAT, 0)], axis=1)
                )
            else:
                first = base + LAT
                rows.append(
                    jnp.concatenate(
                        [queries[:, first : first + LAT], turned(first + LAT, 1)], axis=1
                    )
                )
        stacked = jnp.concatenate(rows, axis=0)
        scores = jnp.dot(stacked, key_rows[...], preferred_element_type=jnp.float32)
        scores = scores.reshape(len(rows), row_count, -1) + bias[...][None]
        top = jnp.max(scores, axis=2, keepdims=True)
        exponent = jnp.exp((scores - top) * score_scale)
        total = jnp.sum(exponent, axis=2, keepdims=True).reshape(len(rows) * row_count, 1)
        weights = exponent.astype(jnp.bfloat16).reshape(len(rows) * row_count, -1)
        mixed = jnp.dot(weights, values[...], preferred_element_type=jnp.float32)
        mixed = (mixed / total).astype(jnp.bfloat16)
        for i in range(len(rows)):
            head = 2 * i + which
            out[:, head * VHEAD : (head + 1) * VHEAD] = jnp.dot(
                mixed[i * row_count : (i + 1) * row_count],
                value_weight[:, head * VHEAD : (head + 1) * VHEAD],
                preferred_element_type=jnp.float32,
            ).astype(jnp.bfloat16)


def attention(queries, keys, key_index, own_index, own_position, value_weight):
    row_count, query_width = queries.shape
    local_heads = value_weight.shape[1] // VHEAD
    width = query_width // local_heads
    group = 4 if local_heads % 4 == 0 else 2
    key_count = keys.shape[1]
    tables = rope_tables(own_position, (width - LAT) // 2, 2 * (width - LAT))
    whole = lambda shape: pl.BlockSpec(shape, lambda i: (0,) * len(shape))
    deep = 2 * width - LAT
    return pl.pallas_call(
        functools.partial(attention_kernel, group),
        grid=(local_heads // group,),
        in_specs=[
            whole(tables.shape),
            whole((row_count, 1)),
            whole((row_count, 1)),
            whole((1, key_count)),
            whole(keys.shape),
            pl.BlockSpec((row_count, group * width), lambda i: (0, i)),
            pl.BlockSpec((LAT, group * VHEAD), lambda i: (0, i)),
        ],
        out_specs=pl.BlockSpec((row_count, group * VHEAD), lambda i: (0, i)),
        out_shape=jax.ShapeDtypeStruct((row_count, local_heads * VHEAD), jnp.bfloat16),
        scratch_shapes=[
            pltpu.VMEM((deep, key_count), jnp.bfloat16),
            pltpu.VMEM((deep, key_count), jnp.bfloat16),
            pltpu.VMEM((key_count, LAT), jnp.bfloat16),
            pltpu.VMEM((row_count, key_count), jnp.float32),
        ],
        compiler_params=pltpu.CompilerParams(vmem_limit_bytes=40 * 1024 * 1024),
        cost_estimate=pl.CostEstimate(
            flops=2 * row_count * local_heads * (key_count * (deep + LAT) + LAT * VHEAD),
            bytes_accessed=2 * (queries.size + keys.size + value_weight.size),
            transcendentals=row_count * local_heads * key_count,
        ),
    )(
        tables,
        (own_index - own_position)[:, None],
        own_index[:, None],
        key_index[None, :],
        keys,
        queries,
        value_weight,
    )


def swap(value, axis_name, bit):
    width = lax.axis_size(axis_name)
    return lax.ppermute(value, axis_name, [(i, i ^ bit) for i in range(width)])


def pick(value, index):
    return lax.dynamic_index_in_dim(value, index, 0, keepdims=False)


def wide(value):
    return value.astype(jnp.float32)


def matmul(a, b):
    return jnp.dot(a, b, preferred_element_type=jnp.float32).astype(jnp.bfloat16)


def gather_keys(rotated_keys, n_ctx):
    rows = rotated_keys.shape[0] // 2
    core = lax.axis_index("tp") & 1
    half = lax.dynamic_slice_in_dim(rotated_keys, core * rows, rows, 0)
    came = [
        lax.ppermute(half, "ctx", [(c, c + d) for c in range(n_ctx - d)])
        for d in range(n_ctx - 1, 0, -1)
    ]
    mine = jnp.concatenate(came, axis=1)
    other = swap(mine, "tp", 1)
    before = jnp.concatenate(
        [jnp.where(core == 0, mine, other), jnp.where(core == 0, other, mine)], axis=0
    )
    return jnp.concatenate([before, rotated_keys], axis=1)


def spread_heads(heads_out, n_ctx, n_tp):
    pieces = heads_out.reshape(n_ctx, heads_out.shape[0] // n_ctx, heads_out.shape[1])
    return [
        lax.ppermute(
            pieces[s],
            ("ctx", "tp"),
            [(c * n_tp + t, t * n_tp + (c ^ s)) for c in range(n_ctx) for t in range(n_tp)],
        )
        for s in range(n_ctx)
    ]


def pair_rows(first, second):
    return jnp.concatenate(
        [first[0], second[1], second[0], first[1], first[2], second[3], second[2], first[3]], axis=0
    )


def after(value, earlier):
    return lax.optimization_barrier((value, earlier))[0]


def reduce_ctx(blocks):
    flat = blocks.reshape(-1, blocks.shape[-1])
    return wide(lax.psum_scatter(flat, "ctx", scatter_dimension=0, tiled=True))


def gather_ctx(rows):
    return lax.all_gather(rows, "ctx", axis=0, tiled=True)


def paired_tail(
    heads_out, residual, output_weight, norm_gain, gate_weight, up_weight, down_weight, n_ctx, n_tp
):
    row_count, width = residual.shape
    half = row_count // 2
    model_width = width * n_tp
    c = lax.axis_index("ctx")
    t = lax.axis_index("tp")
    core = t & 1
    first_half = (t >> 1) ^ (c >> 1)
    own = spread_heads(heads_out, n_ctx, n_tp)
    own_all = jnp.stack(own)
    near = swap(own_all, "tp", 1)
    far = swap(own_all, "tp", 2)
    residual_halves = residual.reshape(2, half, width)

    def sum_heads(blocks, which):
        head_sum = reduce_ctx(jnp.stack([pick(blocks, t ^ i) for i in range(n_ctx)]))
        return (wide(pick(residual_halves, which)) + head_sum).astype(jnp.bfloat16)

    blocks_a = matmul(pair_rows(own_all, near), output_weight).reshape(n_ctx, half, width)
    far = after(far, blocks_a)
    far_near = swap(far, "tp", 1)
    order = [2, 3, 0, 1]
    rows_b = pair_rows([far[i] for i in order], [far_near[i] for i in order])
    blocks_b = matmul(rows_b, output_weight).reshape(n_ctx, half, width)
    attended_a = sum_heads(blocks_a, first_half)
    all_a = gather_ctx(attended_a)
    attended_b = sum_heads(after(blocks_b, attended_a), 1 - first_half)

    def gate_up(all_rows):
        values = wide(all_rows)
        squares = jnp.sum(values * values, axis=1).reshape(2, 2 * half)
        scaled = (values * norm_gain[None, :]).astype(jnp.bfloat16)
        sums = [matmul(scaled, w).reshape(2, 2 * half, -1) for w in (gate_weight, up_weight)]
        kept, came = [], []
        for term in sums + [squares]:
            came.append(swap(pick(term, 1 - core), "tp", 1))
            kept.append(pick(term, core))
        return kept, came

    kept_a, came_a = gate_up(all_a)
    chip_a = [(wide(k) + wide(r)).astype(k.dtype) for k, r in zip(kept_a, came_a)]
    across = [swap(term, "tp", 2) for term in chip_a]
    all_b = after(gather_ctx(attended_b), chip_a)
    kept_b, came_b = gate_up(all_b)
    gate, up, squares = [wide(k) + wide(r) + wide(x) for k, r, x in zip(kept_b, came_b, across)]
    inverse_rms = lax.rsqrt(squares / model_width + norm_eps)[:, None]
    hidden = (jax.nn.silu(gate * inverse_rms) * (up * inverse_rms)).astype(jnp.bfloat16)
    hidden_near = swap(hidden, "tp", 1)
    hidden_far = swap(hidden, "tp", 2)

    def down(mine, other):
        blocks = matmul(jnp.concatenate([mine, other], axis=0), down_weight)
        blocks = blocks.reshape(n_ctx, half, width)
        return jnp.stack([pick(blocks, i ^ (2 * core)) for i in range(n_ctx)])

    down_b = down(hidden, hidden_near)
    out_b = (wide(attended_b) + reduce_ctx(down_b)).astype(jnp.bfloat16)
    hidden_far = after(hidden_far, down_b)
    hidden_far_near = swap(hidden_far, "tp", 1)
    down_a = down(hidden_far, hidden_far_near)
    out_a = (wide(attended_a) + reduce_ctx(down_a)).astype(jnp.bfloat16)

    def in_order(a, b):
        first = first_half == 0
        return jnp.concatenate([jnp.where(first, a, b), jnp.where(first, b, a)], axis=0)

    return in_order(attended_a, attended_b), in_order(out_a, out_b)


def on_device(
    residual,
    latent,
    queries,
    lengths,
    value_weight,
    output_weight,
    norm_gain,
    gate_weight,
    up_weight,
    down_weight,
):
    row_count = residual.shape[0]
    ctx_place = lax.axis_index("ctx")
    n_ctx, n_tp = lax.axis_size("ctx"), lax.axis_size("tp")
    paired = n_ctx == 4 and n_tp == 4 and row_count % 64 == 0
    own_index = ctx_place * row_count + jnp.arange(row_count, dtype=jnp.int32)
    _, own_position = trace_info(own_index, lengths)
    rotated_keys = rope_keys(latent, own_position, LAT)
    key_order = jnp.arange(n_ctx * row_count, dtype=jnp.int32)
    if paired:
        keys = gather_keys(rotated_keys, n_ctx)
        key_index = key_order + (ctx_place - (n_ctx - 1)) * row_count
    else:
        keys = lax.all_gather(rotated_keys, "ctx", axis=1, tiled=True)
        key_index = key_order
    heads_out = attention(queries, keys, key_index, own_index, own_position, value_weight)
    if paired:
        return paired_tail(
            heads_out,
            residual,
            output_weight,
            norm_gain,
            gate_weight,
            up_weight,
            down_weight,
            n_ctx,
            n_tp,
        )
    all_heads = lax.all_gather(heads_out, "tp", axis=1, tiled=True)
    head_block = lax.all_to_all(all_heads, "ctx", split_axis=1, concat_axis=0, tiled=True)
    head_sum = lax.psum_scatter(
        jnp.dot(head_block, output_weight, preferred_element_type=jnp.float32).astype(jnp.bfloat16),
        "ctx",
        scatter_dimension=0,
        tiled=True,
    ).astype(jnp.float32)
    attended = (residual.astype(jnp.float32) + head_sum).astype(jnp.bfloat16)
    attended_float = attended.astype(jnp.float32)
    squares = lax.psum(jnp.sum(attended_float * attended_float, axis=1), "tp")
    inverse_rms = lax.rsqrt(squares / D + norm_eps)
    scaled = (attended_float * inverse_rms[:, None] * norm_gain[None, :]).astype(jnp.bfloat16)
    scaled_all = lax.all_gather(scaled, "ctx", axis=0, tiled=True)
    unit_count = gate_weight.shape[1]
    gate_up = jnp.concatenate([gate_weight, up_weight], axis=1)
    summed = lax.psum_scatter(
        jnp.dot(scaled_all, gate_up, preferred_element_type=jnp.float32).astype(jnp.bfloat16),
        "tp",
        scatter_dimension=0,
        tiled=True,
    ).astype(jnp.float32)
    hidden_share = (jax.nn.silu(summed[:, :unit_count]) * summed[:, unit_count:]).astype(
        jnp.bfloat16
    )
    hidden_all = lax.all_gather(hidden_share, "tp", axis=0, tiled=True)
    down_sum = lax.psum_scatter(
        jnp.dot(hidden_all, down_weight, preferred_element_type=jnp.float32).astype(jnp.bfloat16),
        "ctx",
        scatter_dimension=0,
        tiled=True,
    ).astype(jnp.float32)
    layer_out = (attended_float + down_sum).astype(jnp.bfloat16)
    return (attended, layer_out)


def solution(mesh):
    in_specs = (
        P(("grp", "ctx"), "tp"),
        P(None, ("grp", "ctx")),
        P(("grp", "ctx"), "tp"),
        P("grp"),
        P(None, "tp"),
        P("ctx", "tp"),
        P("tp"),
        P("tp", "ctx"),
        P("tp", "ctx"),
        P("ctx", "tp"),
    )
    out_specs = (P(("grp", "ctx"), "tp"), P(("grp", "ctx"), "tp"))
    return jax.shard_map(
        on_device, mesh=mesh, in_specs=in_specs, out_specs=out_specs, check_vma=False
    )
```

```python
import functools

import jax
import jax.numpy as jnp
from jax import lax
from jax.experimental import pallas as pl
from jax.experimental.pallas import tpu as pltpu
from jax.sharding import PartitionSpec as P

D = 7168
LAT = 512
ROPE = 64
VHEAD = 128


score_scale = 192.0 ** (-0.5)
rope_base = 10000.0
norm_eps = 1e-06
masked_score = -1e30


def rope_freqs(half_width):
    return rope_base ** (-jnp.arange(half_width, dtype=jnp.float32) / half_width)


def trace_info(token_index, lengths):
    trace_ends = jnp.cumsum(lengths)
    starts = trace_ends - lengths
    trace_ids = jnp.sum((token_index[:, None] >= trace_ends[None, :]).astype(jnp.int32), axis=1)
    member = trace_ids[:, None] == jnp.arange(lengths.shape[0], dtype=jnp.int32)[None, :]
    pos_shift = jnp.sum(jnp.where(member, (0 - starts)[None, :], 0), axis=1)
    return (trace_ids, token_index + pos_shift)


def rope_keys(latent, positions, latent_width):
    values = latent.astype(jnp.float32)
    half_width = (values.shape[0] - latent_width) // 2
    angles = rope_freqs(half_width)[:, None] * positions.astype(jnp.float32)[None, :]
    first_half = values[latent_width : latent_width + half_width]
    second_half = values[latent_width + half_width :]
    cosine = jnp.cos(angles)
    sine_value = jnp.sin(angles)
    return jnp.concatenate(
        [
            values[:latent_width],
            first_half * cosine - second_half * sine_value,
            first_half * sine_value + second_half * cosine,
        ],
        axis=0,
    ).astype(jnp.bfloat16)


def rope_tables(positions, half_width, lanes):
    angles = positions.astype(jnp.float32)[:, None] * rope_freqs(half_width)[None, :]
    cosine, sine_value = jnp.cos(angles), jnp.sin(angles)
    cos_part = jnp.concatenate([cosine, cosine], axis=1)
    sin_part = jnp.concatenate([-sine_value, sine_value], axis=1)
    rest = lanes - 2 * half_width
    ones = jnp.ones((angles.shape[0], rest), jnp.float32)
    zeros = jnp.zeros((angles.shape[0], rest), jnp.float32)
    return jnp.stack(
        [
            jnp.concatenate([cos_part, ones], axis=1),
            jnp.concatenate([sin_part, zeros], axis=1),
            jnp.concatenate([ones, cos_part], axis=1),
            jnp.concatenate([zeros, sin_part], axis=1),
        ]
    )


def attention_kernel(
    group, tables, starts, own_index, key_index, keys, queries, value_weight, out, even, odd, values, bias
):
    row_count = queries.shape[0]
    width = queries.shape[1] // group
    half_width = (width - LAT) // 2
    lanes = 2 * (width - LAT)

    @pl.when(pl.program_id(0) == 0)
    def prepare():
        all_keys = keys[...]
        pad = jnp.zeros((width - LAT, all_keys.shape[1]), jnp.bfloat16)
        even[:width] = all_keys
        even[width:] = pad
        odd[: width - LAT] = pad
        odd[width - LAT :] = all_keys
        values[...] = keys[:LAT].astype(jnp.float32).T.astype(jnp.bfloat16)
        allowed = (key_index[...] >= starts[...]) & (key_index[...] <= own_index[...])
        bias[...] = jnp.where(allowed, 0.0, masked_score)

    lane = lax.broadcasted_iota(jnp.int32, (row_count, lanes), 1)
    low = (lane & (2 * half_width - 1)) < half_width

    def turned(start, which):
        entry = queries[:, start : start + lanes].astype(jnp.float32)
        partner = jnp.where(
            low, pltpu.roll(entry, lanes - half_width, 1), pltpu.roll(entry, half_width, 1)
        )
        return (entry * tables[2 * which] + partner * tables[2 * which + 1]).astype(jnp.bfloat16)

    for which, key_rows in ((0, even), (1, odd)):
        rows = []
        for head in range(which, group, 2):
            base = (head - which) * width
            if which == 0:
                rows.append(
                    jnp.concatenate([queries[:, base : base + LAT], turned(base + LAT, 0)], axis=1)
                )
            else:
                first = base + LAT
                rows.append(
                    jnp.concatenate(
                        [queries[:, first : first + LAT], turned(first + LAT, 1)], axis=1
                    )
                )
        stacked = jnp.concatenate(rows, axis=0)
        scores = jnp.dot(stacked, key_rows[...], preferred_element_type=jnp.float32)
        scores = scores.reshape(len(rows), row_count, -1) + bias[...][None]
        top = jnp.max(scores, axis=2, keepdims=True)
        exponent = jnp.exp((scores - top) * score_scale)
        total = jnp.sum(exponent, axis=2, keepdims=True).reshape(len(rows) * row_count, 1)
        weights = exponent.astype(jnp.bfloat16).reshape(len(rows) * row_count, -1)
        mixed = jnp.dot(weights, values[...], preferred_element_type=jnp.float32)
        mixed = (mixed / total).astype(jnp.bfloat16)
        for i in range(len(rows)):
            head = 2 * i + which
            out[:, head * VHEAD : (head + 1) * VHEAD] = jnp.dot(
                mixed[i * row_count : (i + 1) * row_count],
                value_weight[:, head * VHEAD : (head + 1) * VHEAD],
                preferred_element_type=jnp.float32,
            ).astype(jnp.bfloat16)


def attention(queries, keys, key_index, own_index, own_position, value_weight):
    row_count, query_width = queries.shape
    local_heads = value_weight.shape[1] // VHEAD
    width = query_width // local_heads
    group = 4 if local_heads % 4 == 0 else 2
    key_count = keys.shape[1]
    tables = rope_tables(own_position, (width - LAT) // 2, 2 * (width - LAT))
    whole = lambda shape: pl.BlockSpec(shape, lambda i: (0,) * len(shape))
    deep = 2 * width - LAT
    return pl.pallas_call(
        functools.partial(attention_kernel, group),
        grid=(local_heads // group,),
        in_specs=[
            whole(tables.shape),
            whole((row_count, 1)),
            whole((row_count, 1)),
            whole((1, key_count)),
            whole(keys.shape),
            pl.BlockSpec((row_count, group * width), lambda i: (0, i)),
            pl.BlockSpec((LAT, group * VHEAD), lambda i: (0, i)),
        ],
        out_specs=pl.BlockSpec((row_count, group * VHEAD), lambda i: (0, i)),
        out_shape=jax.ShapeDtypeStruct((row_count, local_heads * VHEAD), jnp.bfloat16),
        scratch_shapes=[
            pltpu.VMEM((deep, key_count), jnp.bfloat16),
            pltpu.VMEM((deep, key_count), jnp.bfloat16),
            pltpu.VMEM((key_count, LAT), jnp.bfloat16),
            pltpu.VMEM((row_count, key_count), jnp.float32),
        ],
        compiler_params=pltpu.CompilerParams(vmem_limit_bytes=40 * 1024 * 1024),
        cost_estimate=pl.CostEstimate(
            flops=2 * row_count * local_heads * (key_count * (deep + LAT) + LAT * VHEAD),
            bytes_accessed=2 * (queries.size + keys.size + value_weight.size),
            transcendentals=row_count * local_heads * key_count,
        ),
    )(
        tables,
        (own_index - own_position)[:, None],
        own_index[:, None],
        key_index[None, :],
        keys,
        queries,
        value_weight,
    )


def swap(value, axis_name, bit):
    width = lax.axis_size(axis_name)
    return lax.ppermute(value, axis_name, [(i, i ^ bit) for i in range(width)])


def pick(value, index):
    return lax.dynamic_index_in_dim(value, index, 0, keepdims=False)


def wide(value):
    return value.astype(jnp.float32)


def matmul_kernel(rows, weight, out):
    out[...] = jnp.dot(rows[...], weight[...], preferred_element_type=jnp.float32).astype(out.dtype)


def matmul(rows, weight):
    row_count, depth = rows.shape
    columns = weight.shape[1]
    block = 256
    return pl.pallas_call(
        matmul_kernel,
        grid=(columns // block,),
        in_specs=[
            pl.BlockSpec((row_count, depth), lambda i: (0, 0)),
            pl.BlockSpec((depth, block), lambda i: (0, i)),
        ],
        out_specs=pl.BlockSpec((row_count, block), lambda i: (0, i)),
        out_shape=jax.ShapeDtypeStruct((row_count, columns), jnp.bfloat16),
        compiler_params=pltpu.CompilerParams(vmem_limit_bytes=16 * 1024 * 1024),
        cost_estimate=pl.CostEstimate(
            flops=2 * row_count * depth * columns,
            bytes_accessed=2 * weight.size,
            transcendentals=0,
        ),
    )(rows, weight)


def gather_keys(rotated_keys, n_ctx):
    rows = rotated_keys.shape[0] // 2
    core = lax.axis_index("tp") & 1
    half = lax.dynamic_slice_in_dim(rotated_keys, core * rows, rows, 0)
    came = [
        lax.ppermute(half, "ctx", [(c, c + d) for c in range(n_ctx - d)])
        for d in range(n_ctx - 1, 0, -1)
    ]
    mine = jnp.concatenate(came, axis=1)
    other = swap(mine, "tp", 1)
    before = jnp.concatenate(
        [jnp.where(core == 0, mine, other), jnp.where(core == 0, other, mine)], axis=0
    )
    return jnp.concatenate([before, rotated_keys], axis=1)


def spread_heads(heads_out, n_ctx, n_tp):
    pieces = heads_out.reshape(n_ctx, heads_out.shape[0] // n_ctx, heads_out.shape[1])
    return [
        lax.ppermute(
            pieces[s],
            ("ctx", "tp"),
            [(c * n_tp + t, t * n_tp + (c ^ s)) for c in range(n_ctx) for t in range(n_tp)],
        )
        for s in range(n_ctx)
    ]


def pair_rows(first, second):
    return jnp.concatenate(
        [first[0], second[1], second[0], first[1], first[2], second[3], second[2], first[3]], axis=0
    )


def after(value, earlier):
    return lax.optimization_barrier((value, earlier))[0]


def paired_tail(
    heads_out, residual, output_weight, norm_gain, gate_weight, up_weight, down_weight, n_ctx, n_tp
):
    row_count, width = residual.shape
    half = row_count // 2
    model_width = width * n_tp
    c = lax.axis_index("ctx")
    t = lax.axis_index("tp")
    core = t & 1
    first_half = (t >> 1) ^ (c >> 1)
    own = spread_heads(heads_out, n_ctx, n_tp)
    own_all = jnp.stack(own)
    near = swap(own_all, "tp", 1)
    residual_halves = residual.reshape(2, half, width)

    def sum_heads(blocks, which):
        place = t ^ c
        sent = jnp.stack([pick(blocks, place ^ 1), pick(blocks, place ^ 3)])
        came = swap(sent, "ctx", 1)
        mine = wide(pick(blocks, place)) + wide(came[0])
        other = (wide(pick(blocks, place ^ 2)) + wide(came[1])).astype(jnp.bfloat16)
        total = wide(pick(residual_halves, which)) + mine + wide(swap(other, "ctx", 2))
        return total.astype(jnp.bfloat16), sent, came

    def gather_ctx(rows):
        pair = jnp.concatenate([rows, swap(rows, "ctx", 2)], axis=0)
        return pair, swap(pair, "ctx", 1)

    blocks_a = matmul(pair_rows(own_all, near), output_weight).reshape(n_ctx, half, width)
    attended_a, sent_a, came_a = sum_heads(blocks_a, first_half)
    far = after(swap(after(own_all, sent_a), "tp", 2), came_a)
    far_near = swap(far, "tp", 1)
    order = [2, 3, 0, 1]
    rows_b = pair_rows([far[i] for i in order], [far_near[i] for i in order])
    blocks_b = matmul(rows_b, output_weight).reshape(n_ctx, half, width)
    near_a, far_a = gather_ctx(attended_a)
    attended_b, _, _ = sum_heads(after(blocks_b, attended_a), 1 - first_half)

    def gate_up(rows):
        values = wide(rows)
        squares = jnp.sum(values * values, axis=1).reshape(-1, 2, half)
        scaled = (values * norm_gain[None, :]).astype(jnp.bfloat16)
        terms = [
            matmul(scaled, weight).reshape(-1, 2, half, weight.shape[1])
            for weight in (gate_weight, up_weight)
        ]

        def side(value, which):
            return lax.dynamic_index_in_dim(value, which, 1, keepdims=False)

        kept = jnp.stack([side(term, core) for term in terms])
        came = swap(jnp.stack([side(term, 1 - core) for term in terms]), "tp", 1)
        total = wide(kept) + wide(came)
        came_squares = swap(side(squares, 1 - core), "tp", 1)
        return total, side(squares, core) + came_squares

    sums_a, squares_a = [], []
    for rows in (near_a, far_a):
        total, squares = gate_up(rows)
        sums_a.append(total.astype(jnp.bfloat16))
        squares_a.append(squares)
    across = [swap(total, "tp", 2) for total in sums_a]
    across_squares = swap(jnp.concatenate(squares_a, axis=0), "tp", 2)
    all_b = jnp.concatenate(gather_ctx(attended_b), axis=0)
    sums_b, squares_b = gate_up(after(all_b, sums_a))
    inverse_rms = lax.rsqrt((squares_b + across_squares) / model_width + norm_eps)[:, :, None]
    gate, up = (sums_b + wide(jnp.concatenate(across, axis=1))) * inverse_rms[None]
    hidden = (jax.nn.silu(gate) * up).astype(jnp.bfloat16).reshape(2 * half, -1)
    hidden_near = swap(hidden, "tp", 1)
    hidden_far = swap(hidden, "tp", 2)

    def sum_down(mine, other):
        blocks = matmul(jnp.concatenate([mine, other], axis=0), down_weight)
        blocks = blocks.reshape(2, 2, half, width)
        came = swap(blocks[:, 1], "ctx", 1)
        pair = wide(blocks[:, 0]) + wide(came)
        other_place = pick(pair, 1 - core).astype(jnp.bfloat16)
        return pick(pair, core) + wide(swap(other_place, "ctx", 2)), came

    down_b, came_b = sum_down(hidden, hidden_near)
    hidden_far = after(hidden_far, came_b)
    down_a, _ = sum_down(hidden_far, swap(hidden_far, "tp", 1))
    out_a = (wide(attended_a) + down_a).astype(jnp.bfloat16)
    out_b = (wide(attended_b) + down_b).astype(jnp.bfloat16)

    def in_order(a, b):
        first = first_half == 0
        return jnp.concatenate([jnp.where(first, a, b), jnp.where(first, b, a)], axis=0)

    return in_order(attended_a, attended_b), in_order(out_a, out_b)


def on_device(
    residual,
    latent,
    queries,
    lengths,
    value_weight,
    output_weight,
    norm_gain,
    gate_weight,
    up_weight,
    down_weight,
):
    row_count = residual.shape[0]
    ctx_place = lax.axis_index("ctx")
    n_ctx, n_tp = lax.axis_size("ctx"), lax.axis_size("tp")
    paired = n_ctx == 4 and n_tp == 4 and row_count % 64 == 0 and residual.shape[1] % 256 == 0
    own_index = ctx_place * row_count + jnp.arange(row_count, dtype=jnp.int32)
    _, own_position = trace_info(own_index, lengths)
    rotated_keys = rope_keys(latent, own_position, LAT)
    key_order = jnp.arange(n_ctx * row_count, dtype=jnp.int32)
    if paired:
        keys = gather_keys(rotated_keys, n_ctx)
        key_index = key_order + (ctx_place - (n_ctx - 1)) * row_count
    else:
        keys = lax.all_gather(rotated_keys, "ctx", axis=1, tiled=True)
        key_index = key_order
    heads_out = attention(queries, keys, key_index, own_index, own_position, value_weight)
    if paired:
        return paired_tail(
            heads_out,
            residual,
            output_weight,
            norm_gain,
            gate_weight,
            up_weight,
            down_weight,
            n_ctx,
            n_tp,
        )
    all_heads = lax.all_gather(heads_out, "tp", axis=1, tiled=True)
    head_block = lax.all_to_all(all_heads, "ctx", split_axis=1, concat_axis=0, tiled=True)
    head_sum = lax.psum_scatter(
        jnp.dot(head_block, output_weight, preferred_element_type=jnp.float32).astype(jnp.bfloat16),
        "ctx",
        scatter_dimension=0,
        tiled=True,
    ).astype(jnp.float32)
    attended = (residual.astype(jnp.float32) + head_sum).astype(jnp.bfloat16)
    attended_float = attended.astype(jnp.float32)
    squares = lax.psum(jnp.sum(attended_float * attended_float, axis=1), "tp")
    inverse_rms = lax.rsqrt(squares / D + norm_eps)
    scaled = (attended_float * inverse_rms[:, None] * norm_gain[None, :]).astype(jnp.bfloat16)
    scaled_all = lax.all_gather(scaled, "ctx", axis=0, tiled=True)
    unit_count = gate_weight.shape[1]
    gate_up = jnp.concatenate([gate_weight, up_weight], axis=1)
    summed = lax.psum_scatter(
        jnp.dot(scaled_all, gate_up, preferred_element_type=jnp.float32).astype(jnp.bfloat16),
        "tp",
        scatter_dimension=0,
        tiled=True,
    ).astype(jnp.float32)
    hidden_share = (jax.nn.silu(summed[:, :unit_count]) * summed[:, unit_count:]).astype(
        jnp.bfloat16
    )
    hidden_all = lax.all_gather(hidden_share, "tp", axis=0, tiled=True)
    down_sum = lax.psum_scatter(
        jnp.dot(hidden_all, down_weight, preferred_element_type=jnp.float32).astype(jnp.bfloat16),
        "ctx",
        scatter_dimension=0,
        tiled=True,
    ).astype(jnp.float32)
    layer_out = (attended_float + down_sum).astype(jnp.bfloat16)
    return (attended, layer_out)


def solution(mesh):
    in_specs = (
        P(("grp", "ctx"), "tp"),
        P(None, ("grp", "ctx")),
        P(("grp", "ctx"), "tp"),
        P("grp"),
        P(None, "tp"),
        P("ctx", "tp"),
        P("tp"),
        P("tp", "ctx"),
        P("tp", "ctx"),
        P("ctx", "tp"),
    )
    out_specs = (P(("grp", "ctx"), "tp"), P(("grp", "ctx"), "tp"))
    return jax.shard_map(
        on_device, mesh=mesh, in_specs=in_specs, out_specs=out_specs, check_vma=False
    )
```

```python
import functools

import jax
import jax.numpy as jnp
from jax import lax
from jax.experimental import pallas as pl
from jax.experimental.pallas import tpu as pltpu
from jax.sharding import PartitionSpec as P

D = 7168
LAT = 512
ROPE = 64
VHEAD = 128


score_scale = 192.0 ** (-0.5)
rope_base = 10000.0
norm_eps = 1e-06
masked_score = -1e30


def rope_freqs(half_width):
    return rope_base ** (-jnp.arange(half_width, dtype=jnp.float32) / half_width)


def trace_info(token_index, lengths):
    trace_ends = jnp.cumsum(lengths)
    starts = trace_ends - lengths
    trace_ids = jnp.sum((token_index[:, None] >= trace_ends[None, :]).astype(jnp.int32), axis=1)
    member = trace_ids[:, None] == jnp.arange(lengths.shape[0], dtype=jnp.int32)[None, :]
    pos_shift = jnp.sum(jnp.where(member, (0 - starts)[None, :], 0), axis=1)
    return (trace_ids, token_index + pos_shift)


def rope_keys(latent, positions, latent_width):
    values = latent.astype(jnp.float32)
    half_width = (values.shape[0] - latent_width) // 2
    angles = rope_freqs(half_width)[:, None] * positions.astype(jnp.float32)[None, :]
    first_half = values[latent_width : latent_width + half_width]
    second_half = values[latent_width + half_width :]
    cosine = jnp.cos(angles)
    sine_value = jnp.sin(angles)
    return jnp.concatenate(
        [
            values[:latent_width],
            first_half * cosine - second_half * sine_value,
            first_half * sine_value + second_half * cosine,
        ],
        axis=0,
    ).astype(jnp.bfloat16)


def rope_tables(positions, half_width, lanes):
    angles = positions.astype(jnp.float32)[:, None] * rope_freqs(half_width)[None, :]
    cosine, sine_value = jnp.cos(angles), jnp.sin(angles)
    cos_part = jnp.concatenate([cosine, cosine], axis=1)
    sin_part = jnp.concatenate([-sine_value, sine_value], axis=1)
    rest = lanes - 2 * half_width
    ones = jnp.ones((angles.shape[0], rest), jnp.float32)
    zeros = jnp.zeros((angles.shape[0], rest), jnp.float32)
    return jnp.stack(
        [
            jnp.concatenate([cos_part, ones], axis=1),
            jnp.concatenate([sin_part, zeros], axis=1),
            jnp.concatenate([ones, cos_part], axis=1),
            jnp.concatenate([zeros, sin_part], axis=1),
        ]
    )


def attention_kernel(
    group, tables, starts, own_index, key_index, keys, queries, value_weight, out, even, odd, values, bias
):
    row_count = queries.shape[0]
    width = queries.shape[1] // group
    half_width = (width - LAT) // 2
    lanes = 2 * (width - LAT)

    @pl.when(pl.program_id(0) == 0)
    def prepare():
        all_keys = keys[...]
        pad = jnp.zeros((width - LAT, all_keys.shape[1]), jnp.bfloat16)
        even[:width] = all_keys
        even[width:] = pad
        odd[: width - LAT] = pad
        odd[width - LAT :] = all_keys
        values[...] = keys[:LAT].astype(jnp.float32).T.astype(jnp.bfloat16)
        allowed = (key_index[...] >= starts[...]) & (key_index[...] <= own_index[...])
        bias[...] = jnp.where(allowed, 0.0, masked_score)

    lane = lax.broadcasted_iota(jnp.int32, (row_count, lanes), 1)
    low = (lane & (2 * half_width - 1)) < half_width

    def turned(start, which):
        entry = queries[:, start : start + lanes].astype(jnp.float32)
        partner = jnp.where(
            low, pltpu.roll(entry, lanes - half_width, 1), pltpu.roll(entry, half_width, 1)
        )
        return (entry * tables[2 * which] + partner * tables[2 * which + 1]).astype(jnp.bfloat16)

    for which, key_rows in ((0, even), (1, odd)):
        rows = []
        for head in range(which, group, 2):
            base = (head - which) * width
            if which == 0:
                rows.append(
                    jnp.concatenate([queries[:, base : base + LAT], turned(base + LAT, 0)], axis=1)
                )
            else:
                first = base + LAT
                rows.append(
                    jnp.concatenate(
                        [queries[:, first : first + LAT], turned(first + LAT, 1)], axis=1
                    )
                )
        stacked = jnp.concatenate(rows, axis=0)
        scores = jnp.dot(stacked, key_rows[...], preferred_element_type=jnp.float32)
        scores = scores.reshape(len(rows), row_count, -1) + bias[...][None]
        top = jnp.max(scores, axis=2, keepdims=True)
        exponent = jnp.exp((scores - top) * score_scale)
        total = jnp.sum(exponent, axis=2, keepdims=True).reshape(len(rows) * row_count, 1)
        weights = exponent.astype(jnp.bfloat16).reshape(len(rows) * row_count, -1)
        mixed = jnp.dot(weights, values[...], preferred_element_type=jnp.float32)
        mixed = (mixed / total).astype(jnp.bfloat16)
        for i in range(len(rows)):
            head = 2 * i + which
            out[:, head * VHEAD : (head + 1) * VHEAD] = jnp.dot(
                mixed[i * row_count : (i + 1) * row_count],
                value_weight[:, head * VHEAD : (head + 1) * VHEAD],
                preferred_element_type=jnp.float32,
            ).astype(jnp.bfloat16)


def attention(queries, keys, key_index, own_index, own_position, value_weight):
    row_count, query_width = queries.shape
    local_heads = value_weight.shape[1] // VHEAD
    width = query_width // local_heads
    group = 4 if local_heads % 4 == 0 else 2
    key_count = keys.shape[1]
    tables = rope_tables(own_position, (width - LAT) // 2, 2 * (width - LAT))
    whole = lambda shape: pl.BlockSpec(shape, lambda i: (0,) * len(shape))
    deep = 2 * width - LAT
    return pl.pallas_call(
        functools.partial(attention_kernel, group),
        grid=(local_heads // group,),
        in_specs=[
            whole(tables.shape),
            whole((row_count, 1)),
            whole((row_count, 1)),
            whole((1, key_count)),
            whole(keys.shape),
            pl.BlockSpec((row_count, group * width), lambda i: (0, i)),
            pl.BlockSpec((LAT, group * VHEAD), lambda i: (0, i)),
        ],
        out_specs=pl.BlockSpec((row_count, group * VHEAD), lambda i: (0, i)),
        out_shape=jax.ShapeDtypeStruct((row_count, local_heads * VHEAD), jnp.bfloat16),
        scratch_shapes=[
            pltpu.VMEM((deep, key_count), jnp.bfloat16),
            pltpu.VMEM((deep, key_count), jnp.bfloat16),
            pltpu.VMEM((key_count, LAT), jnp.bfloat16),
            pltpu.VMEM((row_count, key_count), jnp.float32),
        ],
        compiler_params=pltpu.CompilerParams(vmem_limit_bytes=40 * 1024 * 1024),
        cost_estimate=pl.CostEstimate(
            flops=2 * row_count * local_heads * (key_count * (deep + LAT) + LAT * VHEAD),
            bytes_accessed=2 * (queries.size + keys.size + value_weight.size),
            transcendentals=row_count * local_heads * key_count,
        ),
    )(
        tables,
        (own_index - own_position)[:, None],
        own_index[:, None],
        key_index[None, :],
        keys,
        queries,
        value_weight,
    )


def swap(value, axis_name, bit):
    width = lax.axis_size(axis_name)
    return lax.ppermute(value, axis_name, [(i, i ^ bit) for i in range(width)])


def pick(value, index):
    return lax.dynamic_index_in_dim(value, index, 0, keepdims=False)


def wide(value):
    return value.astype(jnp.float32)


def streamed_kernel(count, *refs):
    rows, weights, outs = refs[0], refs[1 : 1 + count], refs[1 + count :]
    for weight, out in zip(weights, outs):
        out[...] = jnp.dot(rows[...], weight[...], preferred_element_type=jnp.float32).astype(out.dtype)


def matmuls(rows, weights):
    row_count, depth = rows.shape
    columns = weights[0].shape[1]
    block = 256
    return pl.pallas_call(
        functools.partial(streamed_kernel, len(weights)),
        grid=(columns // block,),
        in_specs=[pl.BlockSpec((row_count, depth), lambda i: (0, 0))]
        + [pl.BlockSpec((depth, block), lambda i: (0, i)) for _ in weights],
        out_specs=[pl.BlockSpec((row_count, block), lambda i: (0, i)) for _ in weights],
        out_shape=[jax.ShapeDtypeStruct((row_count, columns), jnp.bfloat16) for _ in weights],
        compiler_params=pltpu.CompilerParams(vmem_limit_bytes=50 * 1024 * 1024),
        cost_estimate=pl.CostEstimate(flops=1024, bytes_accessed=1024, transcendentals=0),
    )(rows, *weights)


def gather_keys(rotated_keys, n_ctx):
    rows = rotated_keys.shape[0] // 2
    core = lax.axis_index("tp") & 1
    half = lax.dynamic_slice_in_dim(rotated_keys, core * rows, rows, 0)
    came = [
        lax.ppermute(half, "ctx", [(c, c + d) for c in range(n_ctx - d)])
        for d in range(n_ctx - 1, 0, -1)
    ]
    mine = jnp.concatenate(came, axis=1)
    other = swap(mine, "tp", 1)
    before = jnp.concatenate(
        [jnp.where(core == 0, mine, other), jnp.where(core == 0, other, mine)], axis=0
    )
    return jnp.concatenate([before, rotated_keys], axis=1)


def spread_heads(heads_out, n_ctx, n_tp):
    pieces = heads_out.reshape(n_ctx, heads_out.shape[0] // n_ctx, heads_out.shape[1])
    return [
        lax.ppermute(
            pieces[s],
            ("ctx", "tp"),
            [(c * n_tp + t, t * n_tp + (c ^ s)) for c in range(n_ctx) for t in range(n_tp)],
        )
        for s in range(n_ctx)
    ]


def pair_rows(first, second):
    return jnp.concatenate(
        [first[0], second[1], second[0], first[1], first[2], second[3], second[2], first[3]], axis=0
    )


def after(value, earlier):
    return lax.optimization_barrier((value, earlier))[0]


def paired_tail(
    heads_out, residual, output_weight, norm_gain, gate_weight, up_weight, down_weight, n_ctx, n_tp
):
    row_count, width = residual.shape
    half = row_count // 2
    model_width = width * n_tp
    c = lax.axis_index("ctx")
    t = lax.axis_index("tp")
    core = t & 1
    first_half = (t >> 1) ^ (c >> 1)
    own = spread_heads(heads_out, n_ctx, n_tp)
    own_all = jnp.stack(own)
    near = swap(own_all, "tp", 1)
    residual_halves = residual.reshape(2, half, width)

    def first_hop(rows):
        blocks = matmuls(rows, [output_weight])[0].reshape(n_ctx, half, width)
        place = t ^ c
        sent = jnp.stack([pick(blocks, place ^ 1), pick(blocks, place ^ 3)])
        kept = [pick(blocks, place), pick(blocks, place ^ 2)]
        return kept, sent, swap(sent, "ctx", 1)

    def second_hop(kept, came):
        other = (wide(kept[1]) + wide(came[1])).astype(jnp.bfloat16)
        return wide(kept[0]) + wide(came[0]), other, swap(other, "ctx", 2)

    def attend(mine, came, which):
        return (wide(pick(residual_halves, which)) + mine + wide(came)).astype(jnp.bfloat16)

    def side(value, which):
        return lax.dynamic_index_in_dim(value, which, 1, keepdims=False)

    def gate_up(rows):
        values = wide(rows)
        squares = jnp.sum(values * values, axis=1).reshape(-1, 2, half)
        scaled = (values * norm_gain[None, :]).astype(jnp.bfloat16)
        terms = [
            term.reshape(-1, 2, half, term.shape[1])
            for term in matmuls(scaled, [gate_weight, up_weight])
        ]
        sent = jnp.stack([side(term, 1 - core) for term in terms])
        kept = jnp.stack([side(term, core) for term in terms])
        return kept, sent, squares

    kept_a, sent_a, came_a = first_hop(pair_rows(own_all, near))
    far = swap(after(own_all, sent_a), "tp", 2)
    mine_a, other_a, last_a = second_hop(kept_a, came_a)
    far = after(far, other_a)
    far_near = swap(far, "tp", 1)
    attended_a = attend(mine_a, last_a, first_half)
    twin_a = swap(attended_a, "ctx", 2)
    order = [2, 3, 0, 1]
    rows_b = pair_rows([far[i] for i in order], [far_near[i] for i in order])
    kept_b, sent_b, came_b = first_hop(after(rows_b, attended_a))
    pair_a = jnp.concatenate([attended_a, after(twin_a, sent_b)], axis=0)
    rest_a = swap(pair_a, "ctx", 1)
    kept_p, sent_p, squares_p = gate_up(pair_a)
    came_p = swap(sent_p, "tp", 1)
    mine_b, other_b, last_b = second_hop(kept_b, after(came_b, sent_p))
    sums_p = (wide(kept_p) + wide(after(came_p, other_b))).astype(jnp.bfloat16)
    across_p = swap(sums_p, "tp", 2)
    kept_q, sent_q, squares_q = gate_up(after(rest_a, sums_p))
    across_p, last_b, sent_q = lax.optimization_barrier((across_p, last_b, sent_q))
    attended_b = attend(mine_b, last_b, 1 - first_half)
    sums_q = (wide(kept_q) + wide(swap(sent_q, "tp", 1))).astype(jnp.bfloat16)
    across_q = swap(sums_q, "tp", 2)
    pair_b = jnp.concatenate([attended_b, swap(attended_b, "ctx", 2)], axis=0)
    all_b = jnp.concatenate([pair_b, swap(pair_b, "ctx", 1)], axis=0)
    all_b, across_q = lax.optimization_barrier((all_b, across_q))
    kept, sent, squares_b = gate_up(all_b)
    came = swap(sent, "tp", 1)
    squares = jnp.stack([jnp.concatenate([squares_p, squares_q], axis=0), squares_b])
    chip_squares = lax.dynamic_index_in_dim(squares, core, 2, keepdims=False) + swap(
        lax.dynamic_index_in_dim(squares, 1 - core, 2, keepdims=False), "tp", 1
    )
    total_squares = chip_squares[1] + swap(chip_squares[0], "tp", 2)
    inverse_rms = lax.rsqrt(total_squares / model_width + norm_eps)[:, :, None]
    across = jnp.concatenate([across_p, across_q], axis=1)
    gate = (wide(kept[0]) + wide(came[0]) + wide(across[0])) * inverse_rms
    up = (wide(kept[1]) + wide(came[1]) + wide(across[1])) * inverse_rms
    hidden = (jax.nn.silu(gate) * up).astype(jnp.bfloat16).reshape(2 * half, -1)
    hidden_near = swap(hidden, "tp", 1)
    hidden_far = swap(hidden, "tp", 2)

    def down_hop(mine, other):
        blocks = matmuls(jnp.concatenate([mine, other], axis=0), [down_weight])[0]
        blocks = blocks.reshape(2, 2, half, width)
        return blocks[:, 0], swap(blocks[:, 1], "ctx", 1)

    def down_second(kept, came):
        pair = wide(kept) + wide(came)
        other = pick(pair, 1 - core).astype(jnp.bfloat16)
        return pick(pair, core), other, swap(other, "ctx", 2)

    kept_b, came_b = down_hop(hidden, hidden_near)
    hidden_far = after(hidden_far, kept_b)
    hidden_far_near = swap(hidden_far, "tp", 1)
    down_b, other_b, last_b = down_second(kept_b, after(came_b, hidden_far))
    down_a, _, last_a = down_second(*down_hop(hidden_far, after(hidden_far_near, other_b)))
    out_b = (wide(attended_b) + down_b + wide(last_b)).astype(jnp.bfloat16)
    out_a = (wide(attended_a) + down_a + wide(last_a)).astype(jnp.bfloat16)

    def in_order(a, b):
        first = first_half == 0
        return jnp.concatenate([jnp.where(first, a, b), jnp.where(first, b, a)], axis=0)

    return in_order(attended_a, attended_b), in_order(out_a, out_b)


def on_device(
    residual,
    latent,
    queries,
    lengths,
    value_weight,
    output_weight,
    norm_gain,
    gate_weight,
    up_weight,
    down_weight,
):
    row_count = residual.shape[0]
    ctx_place = lax.axis_index("ctx")
    n_ctx, n_tp = lax.axis_size("ctx"), lax.axis_size("tp")
    paired = n_ctx == 4 and n_tp == 4 and row_count % 64 == 0 and residual.shape[1] % 256 == 0
    own_index = ctx_place * row_count + jnp.arange(row_count, dtype=jnp.int32)
    _, own_position = trace_info(own_index, lengths)
    rotated_keys = rope_keys(latent, own_position, LAT)
    key_order = jnp.arange(n_ctx * row_count, dtype=jnp.int32)
    if paired:
        keys = gather_keys(rotated_keys, n_ctx)
        key_index = key_order + (ctx_place - (n_ctx - 1)) * row_count
    else:
        keys = lax.all_gather(rotated_keys, "ctx", axis=1, tiled=True)
        key_index = key_order
    heads_out = attention(queries, keys, key_index, own_index, own_position, value_weight)
    if paired:
        return paired_tail(
            heads_out,
            residual,
            output_weight,
            norm_gain,
            gate_weight,
            up_weight,
            down_weight,
            n_ctx,
            n_tp,
        )
    all_heads = lax.all_gather(heads_out, "tp", axis=1, tiled=True)
    head_block = lax.all_to_all(all_heads, "ctx", split_axis=1, concat_axis=0, tiled=True)
    head_sum = lax.psum_scatter(
        jnp.dot(head_block, output_weight, preferred_element_type=jnp.float32).astype(jnp.bfloat16),
        "ctx",
        scatter_dimension=0,
        tiled=True,
    ).astype(jnp.float32)
    attended = (residual.astype(jnp.float32) + head_sum).astype(jnp.bfloat16)
    attended_float = attended.astype(jnp.float32)
    squares = lax.psum(jnp.sum(attended_float * attended_float, axis=1), "tp")
    inverse_rms = lax.rsqrt(squares / D + norm_eps)
    scaled = (attended_float * inverse_rms[:, None] * norm_gain[None, :]).astype(jnp.bfloat16)
    scaled_all = lax.all_gather(scaled, "ctx", axis=0, tiled=True)
    unit_count = gate_weight.shape[1]
    gate_up = jnp.concatenate([gate_weight, up_weight], axis=1)
    summed = lax.psum_scatter(
        jnp.dot(scaled_all, gate_up, preferred_element_type=jnp.float32).astype(jnp.bfloat16),
        "tp",
        scatter_dimension=0,
        tiled=True,
    ).astype(jnp.float32)
    hidden_share = (jax.nn.silu(summed[:, :unit_count]) * summed[:, unit_count:]).astype(
        jnp.bfloat16
    )
    hidden_all = lax.all_gather(hidden_share, "tp", axis=0, tiled=True)
    down_sum = lax.psum_scatter(
        jnp.dot(hidden_all, down_weight, preferred_element_type=jnp.float32).astype(jnp.bfloat16),
        "ctx",
        scatter_dimension=0,
        tiled=True,
    ).astype(jnp.float32)
    layer_out = (attended_float + down_sum).astype(jnp.bfloat16)
    return (attended, layer_out)


def solution(mesh):
    in_specs = (
        P(("grp", "ctx"), "tp"),
        P(None, ("grp", "ctx")),
        P(("grp", "ctx"), "tp"),
        P("grp"),
        P(None, "tp"),
        P("ctx", "tp"),
        P("tp"),
        P("tp", "ctx"),
        P("tp", "ctx"),
        P("ctx", "tp"),
    )
    out_specs = (P(("grp", "ctx"), "tp"), P(("grp", "ctx"), "tp"))
    return jax.shard_map(
        on_device, mesh=mesh, in_specs=in_specs, out_specs=out_specs, check_vma=False
    )
```

```python
import functools

import jax
import jax.numpy as jnp
from jax import lax
from jax.experimental import pallas as pl
from jax.experimental.pallas import tpu as pltpu
from jax.sharding import PartitionSpec as P

D = 7168
LAT = 512
ROPE = 64
VHEAD = 128


score_scale = 192.0 ** (-0.5)
rope_base = 10000.0
norm_eps = 1e-06
masked_score = -1e30


def rope_freqs(half_width):
    return rope_base ** (-jnp.arange(half_width, dtype=jnp.float32) / half_width)


def trace_info(token_index, lengths):
    trace_ends = jnp.cumsum(lengths)
    starts = trace_ends - lengths
    trace_ids = jnp.sum((token_index[:, None] >= trace_ends[None, :]).astype(jnp.int32), axis=1)
    member = trace_ids[:, None] == jnp.arange(lengths.shape[0], dtype=jnp.int32)[None, :]
    pos_shift = jnp.sum(jnp.where(member, (0 - starts)[None, :], 0), axis=1)
    return (trace_ids, token_index + pos_shift)


def rope_keys(latent, positions, latent_width):
    values = latent.astype(jnp.float32)
    half_width = (values.shape[0] - latent_width) // 2
    angles = rope_freqs(half_width)[:, None] * positions.astype(jnp.float32)[None, :]
    first_half = values[latent_width : latent_width + half_width]
    second_half = values[latent_width + half_width :]
    cosine = jnp.cos(angles)
    sine_value = jnp.sin(angles)
    return jnp.concatenate(
        [
            values[:latent_width],
            first_half * cosine - second_half * sine_value,
            first_half * sine_value + second_half * cosine,
        ],
        axis=0,
    ).astype(jnp.bfloat16)


def rope_tables(positions, half_width, lanes):
    angles = positions.astype(jnp.float32)[:, None] * rope_freqs(half_width)[None, :]
    cosine, sine_value = jnp.cos(angles), jnp.sin(angles)
    cos_part = jnp.concatenate([cosine, cosine], axis=1)
    sin_part = jnp.concatenate([-sine_value, sine_value], axis=1)
    rest = lanes - 2 * half_width
    ones = jnp.ones((angles.shape[0], rest), jnp.float32)
    zeros = jnp.zeros((angles.shape[0], rest), jnp.float32)
    return jnp.stack(
        [
            jnp.concatenate([cos_part, ones], axis=1),
            jnp.concatenate([sin_part, zeros], axis=1),
            jnp.concatenate([ones, cos_part], axis=1),
            jnp.concatenate([zeros, sin_part], axis=1),
        ]
    )


def attention_kernel(
    group, tables, starts, own_index, key_index, keys, queries, value_weight, out, even, odd, values, bias
):
    row_count = queries.shape[0]
    width = queries.shape[1] // group
    half_width = (width - LAT) // 2
    lanes = 2 * (width - LAT)

    @pl.when(pl.program_id(0) == 0)
    def prepare():
        all_keys = keys[...]
        pad = jnp.zeros((width - LAT, all_keys.shape[1]), jnp.bfloat16)
        even[:width] = all_keys
        even[width:] = pad
        odd[: width - LAT] = pad
        odd[width - LAT :] = all_keys
        values[...] = keys[:LAT].astype(jnp.float32).T.astype(jnp.bfloat16)
        allowed = (key_index[...] >= starts[...]) & (key_index[...] <= own_index[...])
        bias[...] = jnp.where(allowed, 0.0, masked_score)

    lane = lax.broadcasted_iota(jnp.int32, (row_count, lanes), 1)
    low = (lane & (2 * half_width - 1)) < half_width

    def turned(start, which):
        entry = queries[:, start : start + lanes].astype(jnp.float32)
        partner = jnp.where(
            low, pltpu.roll(entry, lanes - half_width, 1), pltpu.roll(entry, half_width, 1)
        )
        return (entry * tables[2 * which] + partner * tables[2 * which + 1]).astype(jnp.bfloat16)

    for which, key_rows in ((0, even), (1, odd)):
        rows = []
        for head in range(which, group, 2):
            base = (head - which) * width
            if which == 0:
                rows.append(
                    jnp.concatenate([queries[:, base : base + LAT], turned(base + LAT, 0)], axis=1)
                )
            else:
                first = base + LAT
                rows.append(
                    jnp.concatenate(
                        [queries[:, first : first + LAT], turned(first + LAT, 1)], axis=1
                    )
                )
        stacked = jnp.concatenate(rows, axis=0)
        scores = jnp.dot(stacked, key_rows[...], preferred_element_type=jnp.float32)
        scores = scores.reshape(len(rows), row_count, -1) + bias[...][None]
        top = jnp.max(scores, axis=2, keepdims=True)
        exponent = jnp.exp((scores - top) * score_scale)
        total = jnp.sum(exponent, axis=2, keepdims=True).reshape(len(rows) * row_count, 1)
        weights = exponent.astype(jnp.bfloat16).reshape(len(rows) * row_count, -1)
        mixed = jnp.dot(weights, values[...], preferred_element_type=jnp.float32)
        mixed = (mixed / total).astype(jnp.bfloat16)
        for i in range(len(rows)):
            head = 2 * i + which
            out[:, head * VHEAD : (head + 1) * VHEAD] = jnp.dot(
                mixed[i * row_count : (i + 1) * row_count],
                value_weight[:, head * VHEAD : (head + 1) * VHEAD],
                preferred_element_type=jnp.float32,
            ).astype(jnp.bfloat16)


def attention(queries, keys, key_index, own_index, own_position, value_weight):
    row_count, query_width = queries.shape
    local_heads = value_weight.shape[1] // VHEAD
    width = query_width // local_heads
    group = 4 if local_heads % 4 == 0 else 2
    key_count = keys.shape[1]
    tables = rope_tables(own_position, (width - LAT) // 2, 2 * (width - LAT))
    whole = lambda shape: pl.BlockSpec(shape, lambda i: (0,) * len(shape))
    deep = 2 * width - LAT
    return pl.pallas_call(
        functools.partial(attention_kernel, group),
        grid=(local_heads // group,),
        in_specs=[
            whole(tables.shape),
            whole((row_count, 1)),
            whole((row_count, 1)),
            whole((1, key_count)),
            whole(keys.shape),
            pl.BlockSpec((row_count, group * width), lambda i: (0, i)),
            pl.BlockSpec((LAT, group * VHEAD), lambda i: (0, i)),
        ],
        out_specs=pl.BlockSpec((row_count, group * VHEAD), lambda i: (0, i)),
        out_shape=jax.ShapeDtypeStruct((row_count, local_heads * VHEAD), jnp.bfloat16),
        scratch_shapes=[
            pltpu.VMEM((deep, key_count), jnp.bfloat16),
            pltpu.VMEM((deep, key_count), jnp.bfloat16),
            pltpu.VMEM((key_count, LAT), jnp.bfloat16),
            pltpu.VMEM((row_count, key_count), jnp.float32),
        ],
        compiler_params=pltpu.CompilerParams(vmem_limit_bytes=(6 + key_count // 64) * 1024 * 1024),
        cost_estimate=pl.CostEstimate(
            flops=2 * row_count * local_heads * (key_count * (deep + LAT) + LAT * VHEAD),
            bytes_accessed=2 * (queries.size + keys.size + value_weight.size),
            transcendentals=row_count * local_heads * key_count,
        ),
    )(
        tables,
        (own_index - own_position)[:, None],
        own_index[:, None],
        key_index[None, :],
        keys,
        queries,
        value_weight,
    )


def swap(value, axis_name, bit):
    width = lax.axis_size(axis_name)
    return lax.ppermute(value, axis_name, [(i, i ^ bit) for i in range(width)])


def pick(value, index):
    return lax.dynamic_index_in_dim(value, index, 0, keepdims=False)


def wide(value):
    return value.astype(jnp.float32)


def matmul(a, b):
    return jnp.dot(a, b, preferred_element_type=jnp.float32).astype(jnp.bfloat16)


def load_kernel(chunks, weight, out, sems):
    rows = weight.shape[0] // chunks
    copies = [
        pltpu.make_async_copy(
            weight.at[pl.ds(i * rows, rows)], out.at[pl.ds(i * rows, rows)], sems.at[i]
        )
        for i in range(chunks)
    ]
    for copy in copies:
        copy.start()
    for copy in copies:
        copy.wait()


def load(weight, grant):
    chunks = 8
    return pl.pallas_call(
        functools.partial(load_kernel, chunks),
        in_specs=[pl.BlockSpec(memory_space=pltpu.HBM)],
        out_specs=pl.BlockSpec(memory_space=pltpu.VMEM),
        out_shape=pltpu.VMEM(weight.shape, weight.dtype),
        scratch_shapes=[pltpu.SemaphoreType.DMA((chunks,))],
        compiler_params=pltpu.CompilerParams(vmem_limit_bytes=grant * 1024 * 1024),
        cost_estimate=pl.CostEstimate(flops=0, bytes_accessed=1024, transcendentals=0),
    )(weight)


def after(value, earlier):
    return lax.optimization_barrier((value, earlier))[0]


def gather_keys(rotated_keys, n_ctx):
    rows = rotated_keys.shape[0] // 2
    core = lax.axis_index("tp") & 1
    half = lax.dynamic_slice_in_dim(rotated_keys, core * rows, rows, 0)
    came = [
        lax.ppermute(half, "ctx", [(c, c + d) for c in range(n_ctx - d)])
        for d in range(n_ctx - 1, 0, -1)
    ]
    mine = jnp.concatenate(came, axis=1)
    other = swap(mine, "tp", 1)
    before = jnp.concatenate(
        [jnp.where(core == 0, mine, other), jnp.where(core == 0, other, mine)], axis=0
    )
    return jnp.concatenate([before, rotated_keys], axis=1)


def spread_heads(heads_out, n_ctx, n_tp):
    pieces = heads_out.reshape(n_ctx, heads_out.shape[0] // n_ctx, heads_out.shape[1])
    return [
        lax.ppermute(
            pieces[s],
            ("ctx", "tp"),
            [(c * n_tp + t, t * n_tp + (c ^ s)) for c in range(n_ctx) for t in range(n_tp)],
        )
        for s in range(n_ctx)
    ]


def pair_rows(first, second):
    return jnp.concatenate(
        [first[0], second[1], second[0], first[1], first[2], second[3], second[2], first[3]], axis=0
    )


def paired_tail(
    heads_out, residual, output_weight, norm_gain, gate_weight, up_weight, down_weight, n_ctx, n_tp
):
    row_count, width = residual.shape
    half = row_count // 2
    model_width = width * n_tp
    c = lax.axis_index("ctx")
    t = lax.axis_index("tp")
    core = t & 1
    first_half = (t >> 1) ^ (c >> 1)
    own = spread_heads(heads_out, n_ctx, n_tp)
    gate_weight = load(after(gate_weight, heads_out), 44)
    up_weight = load(after(up_weight, gate_weight), 34)
    own_all = jnp.stack(after(own, up_weight))
    near = swap(own_all, "tp", 1)
    residual_halves = residual.reshape(2, half, width)

    def first_hop(rows):
        blocks = matmul(rows, output_weight).reshape(n_ctx, half, width)
        place = t ^ c
        sent = jnp.stack([pick(blocks, place ^ 1), pick(blocks, place ^ 3)])
        kept = [pick(blocks, place), pick(blocks, place ^ 2)]
        return kept, sent, swap(sent, "ctx", 1)

    def second_hop(kept, came):
        other = (wide(kept[1]) + wide(came[1])).astype(jnp.bfloat16)
        return wide(kept[0]) + wide(came[0]), other, swap(other, "ctx", 2)

    def attend(mine, came, which):
        return (wide(pick(residual_halves, which)) + mine + wide(came)).astype(jnp.bfloat16)

    def side(value, which):
        return lax.dynamic_index_in_dim(value, which, 1, keepdims=False)

    def gate_up(rows):
        values = wide(rows)
        squares = jnp.sum(values * values, axis=1).reshape(-1, 2, half)
        scaled = (values * norm_gain[None, :]).astype(jnp.bfloat16)
        terms = [
            term.reshape(-1, 2, half, term.shape[1])
            for term in [matmul(scaled, weight) for weight in (gate_weight, up_weight)]
        ]
        sent = jnp.stack([side(term, 1 - core) for term in terms])
        kept = jnp.stack([side(term, core) for term in terms])
        return kept, sent, squares

    kept_a, sent_a, came_a = first_hop(pair_rows(own_all, near))
    far = swap(after(own_all, sent_a), "tp", 2)
    mine_a, other_a, last_a = second_hop(kept_a, came_a)
    far = after(far, other_a)
    far_near = swap(far, "tp", 1)
    attended_a = attend(mine_a, last_a, first_half)
    twin_a = swap(attended_a, "ctx", 2)
    order = [2, 3, 0, 1]
    rows_b = pair_rows([far[i] for i in order], [far_near[i] for i in order])
    kept_b, sent_b, came_b = first_hop(after(rows_b, attended_a))
    pair_a = jnp.concatenate([attended_a, after(twin_a, sent_b)], axis=0)
    rest_a = swap(pair_a, "ctx", 1)
    kept_p, sent_p, squares_p = gate_up(pair_a)
    came_p = swap(sent_p, "tp", 1)
    mine_b, other_b, last_b = second_hop(kept_b, after(came_b, sent_p))
    sums_p = (wide(kept_p) + wide(after(came_p, other_b))).astype(jnp.bfloat16)
    across_p = swap(sums_p, "tp", 2)
    kept_q, sent_q, squares_q = gate_up(after(rest_a, sums_p))
    across_p, last_b, sent_q = lax.optimization_barrier((across_p, last_b, sent_q))
    attended_b = attend(mine_b, last_b, 1 - first_half)
    sums_q = (wide(kept_q) + wide(swap(sent_q, "tp", 1))).astype(jnp.bfloat16)
    across_q = swap(sums_q, "tp", 2)
    down_weight = load(after(down_weight, attended_b), 24)
    twin_b = after(swap(attended_b, "ctx", 2), down_weight)
    pair_b = jnp.concatenate([attended_b, twin_b], axis=0)
    all_b = jnp.concatenate([pair_b, swap(pair_b, "ctx", 1)], axis=0)
    all_b, across_q = lax.optimization_barrier((all_b, across_q))
    kept, sent, squares_b = gate_up(all_b)
    came = swap(sent, "tp", 1)
    squares = jnp.stack([jnp.concatenate([squares_p, squares_q], axis=0), squares_b])
    chip_squares = lax.dynamic_index_in_dim(squares, core, 2, keepdims=False) + swap(
        lax.dynamic_index_in_dim(squares, 1 - core, 2, keepdims=False), "tp", 1
    )
    total_squares = chip_squares[1] + swap(chip_squares[0], "tp", 2)
    inverse_rms = lax.rsqrt(total_squares / model_width + norm_eps)[:, :, None]
    across = jnp.concatenate([across_p, across_q], axis=1)
    gate = (wide(kept[0]) + wide(came[0]) + wide(across[0])) * inverse_rms
    up = (wide(kept[1]) + wide(came[1]) + wide(across[1])) * inverse_rms
    hidden = (jax.nn.silu(gate) * up).astype(jnp.bfloat16).reshape(2 * half, -1)
    hidden_near = swap(hidden, "tp", 1)
    hidden_far = swap(hidden, "tp", 2)

    def down_hop(mine, other):
        blocks = matmul(jnp.concatenate([mine, other], axis=0), down_weight)
        blocks = blocks.reshape(2, 2, half, width)
        return blocks[:, 0], swap(blocks[:, 1], "ctx", 1)

    def down_second(kept, came):
        pair = wide(kept) + wide(came)
        other = pick(pair, 1 - core).astype(jnp.bfloat16)
        return pick(pair, core), other, swap(other, "ctx", 2)

    kept_b, came_b = down_hop(hidden, hidden_near)
    hidden_far = after(hidden_far, kept_b)
    hidden_far_near = swap(hidden_far, "tp", 1)
    down_b, other_b, last_b = down_second(kept_b, after(came_b, hidden_far))
    down_a, _, last_a = down_second(*down_hop(hidden_far, after(hidden_far_near, other_b)))
    out_b = (wide(attended_b) + down_b + wide(last_b)).astype(jnp.bfloat16)
    out_a = (wide(attended_a) + down_a + wide(last_a)).astype(jnp.bfloat16)

    def in_order(a, b):
        first = first_half == 0
        return jnp.concatenate([jnp.where(first, a, b), jnp.where(first, b, a)], axis=0)

    return in_order(attended_a, attended_b), in_order(out_a, out_b)


def on_device(
    residual,
    latent,
    queries,
    lengths,
    value_weight,
    output_weight,
    norm_gain,
    gate_weight,
    up_weight,
    down_weight,
):
    row_count = residual.shape[0]
    ctx_place = lax.axis_index("ctx")
    n_ctx, n_tp = lax.axis_size("ctx"), lax.axis_size("tp")
    paired = n_ctx == 4 and n_tp == 4 and row_count % 64 == 0 and residual.shape[1] % 256 == 0
    own_index = ctx_place * row_count + jnp.arange(row_count, dtype=jnp.int32)
    _, own_position = trace_info(own_index, lengths)
    rotated_keys = rope_keys(latent, own_position, LAT)
    key_order = jnp.arange(n_ctx * row_count, dtype=jnp.int32)
    if paired:
        keys = gather_keys(rotated_keys, n_ctx)
        key_index = key_order + (ctx_place - (n_ctx - 1)) * row_count
    else:
        keys = lax.all_gather(rotated_keys, "ctx", axis=1, tiled=True)
        key_index = key_order
    heads_out = attention(queries, keys, key_index, own_index, own_position, value_weight)
    if paired:
        return paired_tail(
            heads_out,
            residual,
            output_weight,
            norm_gain,
            gate_weight,
            up_weight,
            down_weight,
            n_ctx,
            n_tp,
        )
    all_heads = lax.all_gather(heads_out, "tp", axis=1, tiled=True)
    head_block = lax.all_to_all(all_heads, "ctx", split_axis=1, concat_axis=0, tiled=True)
    head_sum = lax.psum_scatter(
        jnp.dot(head_block, output_weight, preferred_element_type=jnp.float32).astype(jnp.bfloat16),
        "ctx",
        scatter_dimension=0,
        tiled=True,
    ).astype(jnp.float32)
    attended = (residual.astype(jnp.float32) + head_sum).astype(jnp.bfloat16)
    attended_float = attended.astype(jnp.float32)
    squares = lax.psum(jnp.sum(attended_float * attended_float, axis=1), "tp")
    inverse_rms = lax.rsqrt(squares / D + norm_eps)
    scaled = (attended_float * inverse_rms[:, None] * norm_gain[None, :]).astype(jnp.bfloat16)
    scaled_all = lax.all_gather(scaled, "ctx", axis=0, tiled=True)
    unit_count = gate_weight.shape[1]
    gate_up = jnp.concatenate([gate_weight, up_weight], axis=1)
    summed = lax.psum_scatter(
        jnp.dot(scaled_all, gate_up, preferred_element_type=jnp.float32).astype(jnp.bfloat16),
        "tp",
        scatter_dimension=0,
        tiled=True,
    ).astype(jnp.float32)
    hidden_share = (jax.nn.silu(summed[:, :unit_count]) * summed[:, unit_count:]).astype(
        jnp.bfloat16
    )
    hidden_all = lax.all_gather(hidden_share, "tp", axis=0, tiled=True)
    down_sum = lax.psum_scatter(
        jnp.dot(hidden_all, down_weight, preferred_element_type=jnp.float32).astype(jnp.bfloat16),
        "ctx",
        scatter_dimension=0,
        tiled=True,
    ).astype(jnp.float32)
    layer_out = (attended_float + down_sum).astype(jnp.bfloat16)
    return (attended, layer_out)


def solution(mesh):
    in_specs = (
        P(("grp", "ctx"), "tp"),
        P(None, ("grp", "ctx")),
        P(("grp", "ctx"), "tp"),
        P("grp"),
        P(None, "tp"),
        P("ctx", "tp"),
        P("tp"),
        P("tp", "ctx"),
        P("tp", "ctx"),
        P("ctx", "tp"),
    )
    out_specs = (P(("grp", "ctx"), "tp"), P(("grp", "ctx"), "tp"))
    return jax.shard_map(
        on_device, mesh=mesh, in_specs=in_specs, out_specs=out_specs, check_vma=False
    )
```

```python
import functools

import jax
import jax.numpy as jnp
from jax import lax
from jax.experimental import pallas as pl
from jax.experimental.pallas import tpu as pltpu
from jax.sharding import PartitionSpec as P

D = 7168
LAT = 512
ROPE = 64
VHEAD = 128


score_scale = 192.0 ** (-0.5)
rope_base = 10000.0
norm_eps = 1e-06
masked_score = -1e30


def rope_freqs(half_width):
    return rope_base ** (-jnp.arange(half_width, dtype=jnp.float32) / half_width)


def trace_info(token_index, lengths):
    trace_ends = jnp.cumsum(lengths)
    starts = trace_ends - lengths
    trace_ids = jnp.sum((token_index[:, None] >= trace_ends[None, :]).astype(jnp.int32), axis=1)
    member = trace_ids[:, None] == jnp.arange(lengths.shape[0], dtype=jnp.int32)[None, :]
    pos_shift = jnp.sum(jnp.where(member, (0 - starts)[None, :], 0), axis=1)
    return (trace_ids, token_index + pos_shift)


def rope_keys(latent, positions, latent_width):
    values = latent.astype(jnp.float32)
    half_width = (values.shape[0] - latent_width) // 2
    angles = rope_freqs(half_width)[:, None] * positions.astype(jnp.float32)[None, :]
    first_half = values[latent_width : latent_width + half_width]
    second_half = values[latent_width + half_width :]
    cosine = jnp.cos(angles)
    sine_value = jnp.sin(angles)
    return jnp.concatenate(
        [
            values[:latent_width],
            first_half * cosine - second_half * sine_value,
            first_half * sine_value + second_half * cosine,
        ],
        axis=0,
    ).astype(jnp.bfloat16)


def rope_tables(positions, half_width, lanes):
    angles = positions.astype(jnp.float32)[:, None] * rope_freqs(half_width)[None, :]
    cosine, sine_value = jnp.cos(angles), jnp.sin(angles)
    cos_part = jnp.concatenate([cosine, cosine], axis=1)
    sin_part = jnp.concatenate([-sine_value, sine_value], axis=1)
    rest = lanes - 2 * half_width
    ones = jnp.ones((angles.shape[0], rest), jnp.float32)
    zeros = jnp.zeros((angles.shape[0], rest), jnp.float32)
    return jnp.stack(
        [
            jnp.concatenate([cos_part, ones], axis=1),
            jnp.concatenate([sin_part, zeros], axis=1),
            jnp.concatenate([ones, cos_part], axis=1),
            jnp.concatenate([zeros, sin_part], axis=1),
        ]
    )


def attention_kernel(
    group, tables, starts, own_index, key_index, keys, queries, value_weight, out, even, odd, values, bias
):
    row_count = queries.shape[0]
    width = queries.shape[1] // group
    half_width = (width - LAT) // 2
    lanes = 2 * (width - LAT)

    @pl.when(pl.program_id(0) == 0)
    def prepare():
        all_keys = keys[...]
        pad = jnp.zeros((width - LAT, all_keys.shape[1]), jnp.bfloat16)
        even[:width] = all_keys
        even[width:] = pad
        odd[: width - LAT] = pad
        odd[width - LAT :] = all_keys
        values[...] = keys[:LAT].astype(jnp.float32).T.astype(jnp.bfloat16)
        allowed = (key_index[...] >= starts[...]) & (key_index[...] <= own_index[...])
        bias[...] = jnp.where(allowed, 0.0, masked_score)

    lane = lax.broadcasted_iota(jnp.int32, (row_count, lanes), 1)
    low = (lane & (2 * half_width - 1)) < half_width

    def turned(start, which):
        entry = queries[:, start : start + lanes].astype(jnp.float32)
        partner = jnp.where(
            low, pltpu.roll(entry, lanes - half_width, 1), pltpu.roll(entry, half_width, 1)
        )
        return (entry * tables[2 * which] + partner * tables[2 * which + 1]).astype(jnp.bfloat16)

    for which, key_rows in ((0, even), (1, odd)):
        rows = []
        for head in range(which, group, 2):
            base = (head - which) * width
            if which == 0:
                rows.append(
                    jnp.concatenate([queries[:, base : base + LAT], turned(base + LAT, 0)], axis=1)
                )
            else:
                first = base + LAT
                rows.append(
                    jnp.concatenate(
                        [queries[:, first : first + LAT], turned(first + LAT, 1)], axis=1
                    )
                )
        stacked = jnp.concatenate(rows, axis=0)
        scores = jnp.dot(stacked, key_rows[...], preferred_element_type=jnp.float32)
        scores = scores.reshape(len(rows), row_count, -1) + bias[...][None]
        top = jnp.max(scores, axis=2, keepdims=True)
        exponent = jnp.exp((scores - top) * score_scale)
        total = jnp.sum(exponent, axis=2, keepdims=True).reshape(len(rows) * row_count, 1)
        weights = exponent.astype(jnp.bfloat16).reshape(len(rows) * row_count, -1)
        mixed = jnp.dot(weights, values[...], preferred_element_type=jnp.float32)
        mixed = (mixed / total).astype(jnp.bfloat16)
        for i in range(len(rows)):
            head = 2 * i + which
            out[:, head * VHEAD : (head + 1) * VHEAD] = jnp.dot(
                mixed[i * row_count : (i + 1) * row_count],
                value_weight[:, head * VHEAD : (head + 1) * VHEAD],
                preferred_element_type=jnp.float32,
            ).astype(jnp.bfloat16)


def attention(queries, keys, key_index, own_index, own_position, value_weight):
    row_count, query_width = queries.shape
    local_heads = value_weight.shape[1] // VHEAD
    width = query_width // local_heads
    group = 4 if local_heads % 4 == 0 else 2
    key_count = keys.shape[1]
    tables = rope_tables(own_position, (width - LAT) // 2, 2 * (width - LAT))
    whole = lambda shape: pl.BlockSpec(shape, lambda i: (0,) * len(shape))
    deep = 2 * width - LAT
    return pl.pallas_call(
        functools.partial(attention_kernel, group),
        grid=(local_heads // group,),
        in_specs=[
            whole(tables.shape),
            whole((row_count, 1)),
            whole((row_count, 1)),
            whole((1, key_count)),
            whole(keys.shape),
            pl.BlockSpec((row_count, group * width), lambda i: (0, i)),
            pl.BlockSpec((LAT, group * VHEAD), lambda i: (0, i)),
        ],
        out_specs=pl.BlockSpec((row_count, group * VHEAD), lambda i: (0, i)),
        out_shape=jax.ShapeDtypeStruct((row_count, local_heads * VHEAD), jnp.bfloat16),
        scratch_shapes=[
            pltpu.VMEM((deep, key_count), jnp.bfloat16),
            pltpu.VMEM((deep, key_count), jnp.bfloat16),
            pltpu.VMEM((key_count, LAT), jnp.bfloat16),
            pltpu.VMEM((row_count, key_count), jnp.float32),
        ],
        compiler_params=pltpu.CompilerParams(vmem_limit_bytes=(6 + key_count // 64) * 1024 * 1024),
        cost_estimate=pl.CostEstimate(
            flops=2 * row_count * local_heads * (key_count * (deep + LAT) + LAT * VHEAD),
            bytes_accessed=2 * (queries.size + keys.size + value_weight.size),
            transcendentals=row_count * local_heads * key_count,
        ),
    )(
        tables,
        (own_index - own_position)[:, None],
        own_index[:, None],
        key_index[None, :],
        keys,
        queries,
        value_weight,
    )


def swap(value, axis_name, bit):
    width = lax.axis_size(axis_name)
    return lax.ppermute(value, axis_name, [(i, i ^ bit) for i in range(width)])


def pick(value, index):
    return lax.dynamic_index_in_dim(value, index, 0, keepdims=False)


def wide(value):
    return value.astype(jnp.float32)


def matmul(a, b):
    return jnp.dot(a, b, preferred_element_type=jnp.float32).astype(jnp.bfloat16)


def load_kernel(chunks, weight, out, sems):
    rows = weight.shape[0] // chunks
    copies = [
        pltpu.make_async_copy(
            weight.at[pl.ds(i * rows, rows)], out.at[pl.ds(i * rows, rows)], sems.at[i]
        )
        for i in range(chunks)
    ]
    for copy in copies:
        copy.start()
    for copy in copies:
        copy.wait()


def load(weight, grant):
    chunks = 8
    return pl.pallas_call(
        functools.partial(load_kernel, chunks),
        in_specs=[pl.BlockSpec(memory_space=pltpu.HBM)],
        out_specs=pl.BlockSpec(memory_space=pltpu.VMEM),
        out_shape=pltpu.VMEM(weight.shape, weight.dtype),
        scratch_shapes=[pltpu.SemaphoreType.DMA((chunks,))],
        compiler_params=pltpu.CompilerParams(vmem_limit_bytes=grant * 1024 * 1024),
        cost_estimate=pl.CostEstimate(flops=0, bytes_accessed=1024, transcendentals=0),
    )(weight)


def after(value, earlier):
    return lax.optimization_barrier((value, earlier))[0]


def gather_keys(rotated_keys, n_ctx):
    rows = rotated_keys.shape[0] // 2
    core = lax.axis_index("tp") & 1
    half = lax.dynamic_slice_in_dim(rotated_keys, core * rows, rows, 0)
    came = [
        lax.ppermute(half, "ctx", [(c, c + d) for c in range(n_ctx - d)])
        for d in range(n_ctx - 1, 0, -1)
    ]
    mine = jnp.concatenate(came, axis=1)
    other = swap(mine, "tp", 1)
    before = jnp.concatenate(
        [jnp.where(core == 0, mine, other), jnp.where(core == 0, other, mine)], axis=0
    )
    return jnp.concatenate([before, rotated_keys], axis=1)


def spread_heads(heads_out, n_ctx, n_tp):
    pieces = heads_out.reshape(n_ctx, heads_out.shape[0] // n_ctx, heads_out.shape[1])
    return [
        lax.ppermute(
            pieces[s],
            ("ctx", "tp"),
            [(c * n_tp + t, t * n_tp + (c ^ s)) for c in range(n_ctx) for t in range(n_tp)],
        )
        for s in range(n_ctx)
    ]


def pair_rows(first, second):
    return jnp.concatenate(
        [first[0], second[1], second[0], first[1], first[2], second[3], second[2], first[3]], axis=0
    )


def paired_tail(
    heads_out, residual, output_weight, norm_gain, gate_weight, up_weight, down_weight, n_ctx, n_tp
):
    row_count, width = residual.shape
    half = row_count // 2
    model_width = width * n_tp
    c = lax.axis_index("ctx")
    t = lax.axis_index("tp")
    core = t & 1
    first_half = (t >> 1) ^ (c >> 1)
    own = spread_heads(heads_out, n_ctx, n_tp)
    gate_weight = load(after(gate_weight, heads_out), 44)
    up_weight = load(after(up_weight, gate_weight), 34)
    own_all = jnp.stack(after(own, up_weight))
    near = swap(own_all, "tp", 1)
    residual_halves = residual.reshape(2, half, width)

    def first_hop(rows):
        blocks = matmul(rows, output_weight).reshape(n_ctx, half, width)
        place = t ^ c
        sent = jnp.stack([pick(blocks, place ^ 1), pick(blocks, place ^ 3)])
        kept = [pick(blocks, place), pick(blocks, place ^ 2)]
        return kept, sent, swap(sent, "ctx", 1)

    def second_hop(kept, came):
        other = (wide(kept[1]) + wide(came[1])).astype(jnp.bfloat16)
        return wide(kept[0]) + wide(came[0]), other, swap(other, "ctx", 2)

    def attend(mine, came, which):
        return (wide(pick(residual_halves, which)) + mine + wide(came)).astype(jnp.bfloat16)

    def gate_up(rows):
        values = wide(rows)
        scaled = (values * norm_gain[None, :]).astype(jnp.bfloat16)
        terms = [matmul(scaled, gate_weight), matmul(scaled, up_weight)]

        def side(which):
            return jnp.concatenate(
                [lax.dynamic_slice_in_dim(term, which * half, half, 0) for term in terms], axis=0
            )

        return side(core), side(1 - core), jnp.sum(values * values, axis=1)

    def chip_sum(kept, sent):
        return wide(kept) + wide(swap(sent, "tp", 1))

    kept_a, sent_a, came_a = first_hop(pair_rows(own_all, near))
    far = swap(after(own_all, sent_a), "tp", 2)
    mine_a, other_a, last_a = second_hop(kept_a, came_a)
    far = after(far, other_a)
    far_near = swap(far, "tp", 1)
    order = [2, 3, 0, 1]
    rows_b = pair_rows([far[i] for i in order], [far_near[i] for i in order])
    kept_b, sent_b, came_b = first_hop(rows_b)
    attended_a = attend(mine_a, after(last_a, sent_b), first_half)
    twin_a = swap(attended_a, "ctx", 2)
    mine_b, other_b, last_b = second_hop(kept_b, after(came_b, attended_a))
    pair_a = jnp.concatenate([attended_a, after(twin_a, other_b)], axis=0)
    rest_a = swap(pair_a, "ctx", 1)
    kept, sent, squares_p = gate_up(pair_a)
    sums_p = chip_sum(kept, sent).astype(jnp.bfloat16)
    across_p = swap(sums_p, "tp", 2)
    attended_b = attend(mine_b, after(last_b, sums_p), 1 - first_half)
    twin_b = swap(attended_b, "ctx", 2)
    rest_a, across_p, _ = lax.optimization_barrier((rest_a, across_p, attended_b))
    kept, sent, squares_q = gate_up(rest_a)
    sums_q = chip_sum(kept, sent).astype(jnp.bfloat16)
    across_q = swap(sums_q, "tp", 2)
    squares_a = jnp.concatenate([squares_p, squares_q])
    across_squares = swap(squares_a + swap(squares_a, "tp", 1), "tp", 2)
    pair_b = jnp.concatenate([attended_b, after(twin_b, sums_q)], axis=0)
    rest_b = swap(pair_b, "ctx", 1)

    def hide(chip_terms, squares, across, across_squares):
        squares = squares + swap(squares, "tp", 1) + across_squares
        squares = lax.dynamic_slice_in_dim(squares, core * half, half, 0)
        inverse_rms = lax.rsqrt(squares / model_width + norm_eps)[:, None]
        gate = (chip_terms[:half] + wide(across[:half])) * inverse_rms
        up = (chip_terms[half:] + wide(across[half:])) * inverse_rms
        return (jax.nn.silu(gate) * up).astype(jnp.bfloat16)

    kept, sent, squares_p = gate_up(pair_b)
    terms_p = chip_sum(kept, sent)
    down_weight = load(after(down_weight, sums_q), 24)
    rest_b, across_q, _, _ = lax.optimization_barrier((rest_b, across_q, sent, down_weight))
    kept, sent, squares_q = gate_up(rest_b)
    terms_q = chip_sum(kept, sent)
    hidden = jnp.concatenate(
        [
            hide(terms_p, squares_p, across_p, across_squares[: 2 * half]),
            hide(terms_q, squares_q, across_q, across_squares[2 * half :]),
        ],
        axis=0,
    )
    hidden_near = swap(hidden, "tp", 1)
    hidden_far = swap(hidden, "tp", 2)

    def down_hop(mine, other):
        blocks = matmul(jnp.concatenate([mine, other], axis=0), down_weight)
        blocks = blocks.reshape(2, 2, half, width)
        return blocks[:, 0], swap(blocks[:, 1], "ctx", 1)

    def down_second(kept, came):
        pair = wide(kept) + wide(came)
        other = pick(pair, 1 - core).astype(jnp.bfloat16)
        return pick(pair, core), other, swap(other, "ctx", 2)

    kept_b, came_b = down_hop(hidden, hidden_near)
    hidden_far = after(hidden_far, kept_b)
    hidden_far_near = swap(hidden_far, "tp", 1)
    down_b, other_b, last_b = down_second(kept_b, after(came_b, hidden_far))
    down_a, _, last_a = down_second(*down_hop(hidden_far, after(hidden_far_near, other_b)))
    out_b = (wide(attended_b) + down_b + wide(last_b)).astype(jnp.bfloat16)
    out_a = (wide(attended_a) + down_a + wide(last_a)).astype(jnp.bfloat16)

    def in_order(a, b):
        first = first_half == 0
        return jnp.concatenate([jnp.where(first, a, b), jnp.where(first, b, a)], axis=0)

    return in_order(attended_a, attended_b), in_order(out_a, out_b)


def on_device(
    residual,
    latent,
    queries,
    lengths,
    value_weight,
    output_weight,
    norm_gain,
    gate_weight,
    up_weight,
    down_weight,
):
    row_count = residual.shape[0]
    ctx_place = lax.axis_index("ctx")
    n_ctx, n_tp = lax.axis_size("ctx"), lax.axis_size("tp")
    paired = n_ctx == 4 and n_tp == 4 and row_count % 64 == 0 and residual.shape[1] % 256 == 0
    own_index = ctx_place * row_count + jnp.arange(row_count, dtype=jnp.int32)
    _, own_position = trace_info(own_index, lengths)
    rotated_keys = rope_keys(latent, own_position, LAT)
    key_order = jnp.arange(n_ctx * row_count, dtype=jnp.int32)
    if paired:
        keys = gather_keys(rotated_keys, n_ctx)
        key_index = key_order + (ctx_place - (n_ctx - 1)) * row_count
    else:
        keys = lax.all_gather(rotated_keys, "ctx", axis=1, tiled=True)
        key_index = key_order
    heads_out = attention(queries, keys, key_index, own_index, own_position, value_weight)
    if paired:
        return paired_tail(
            heads_out,
            residual,
            output_weight,
            norm_gain,
            gate_weight,
            up_weight,
            down_weight,
            n_ctx,
            n_tp,
        )
    all_heads = lax.all_gather(heads_out, "tp", axis=1, tiled=True)
    head_block = lax.all_to_all(all_heads, "ctx", split_axis=1, concat_axis=0, tiled=True)
    head_sum = lax.psum_scatter(
        jnp.dot(head_block, output_weight, preferred_element_type=jnp.float32).astype(jnp.bfloat16),
        "ctx",
        scatter_dimension=0,
        tiled=True,
    ).astype(jnp.float32)
    attended = (residual.astype(jnp.float32) + head_sum).astype(jnp.bfloat16)
    attended_float = attended.astype(jnp.float32)
    squares = lax.psum(jnp.sum(attended_float * attended_float, axis=1), "tp")
    inverse_rms = lax.rsqrt(squares / D + norm_eps)
    scaled = (attended_float * inverse_rms[:, None] * norm_gain[None, :]).astype(jnp.bfloat16)
    scaled_all = lax.all_gather(scaled, "ctx", axis=0, tiled=True)
    unit_count = gate_weight.shape[1]
    gate_up = jnp.concatenate([gate_weight, up_weight], axis=1)
    summed = lax.psum_scatter(
        jnp.dot(scaled_all, gate_up, preferred_element_type=jnp.float32).astype(jnp.bfloat16),
        "tp",
        scatter_dimension=0,
        tiled=True,
    ).astype(jnp.float32)
    hidden_share = (jax.nn.silu(summed[:, :unit_count]) * summed[:, unit_count:]).astype(
        jnp.bfloat16
    )
    hidden_all = lax.all_gather(hidden_share, "tp", axis=0, tiled=True)
    down_sum = lax.psum_scatter(
        jnp.dot(hidden_all, down_weight, preferred_element_type=jnp.float32).astype(jnp.bfloat16),
        "ctx",
        scatter_dimension=0,
        tiled=True,
    ).astype(jnp.float32)
    layer_out = (attended_float + down_sum).astype(jnp.bfloat16)
    return (attended, layer_out)


def solution(mesh):
    in_specs = (
        P(("grp", "ctx"), "tp"),
        P(None, ("grp", "ctx")),
        P(("grp", "ctx"), "tp"),
        P("grp"),
        P(None, "tp"),
        P("ctx", "tp"),
        P("tp"),
        P("tp", "ctx"),
        P("tp", "ctx"),
        P("ctx", "tp"),
    )
    out_specs = (P(("grp", "ctx"), "tp"), P(("grp", "ctx"), "tp"))
    return jax.shard_map(
        on_device, mesh=mesh, in_specs=in_specs, out_specs=out_specs, check_vma=False
    )
```

```python
import functools

import jax
import jax.numpy as jnp
from jax import lax
from jax.experimental import pallas as pl
from jax.experimental.pallas import tpu as pltpu
from jax.sharding import PartitionSpec as P

D = 7168
LAT = 512
ROPE = 64
VHEAD = 128


score_scale = 192.0 ** (-0.5)
rope_base = 10000.0
norm_eps = 1e-06
masked_score = -1e30


def rope_freqs(half_width):
    return rope_base ** (-jnp.arange(half_width, dtype=jnp.float32) / half_width)


def trace_info(token_index, lengths):
    trace_ends = jnp.cumsum(lengths)
    starts = trace_ends - lengths
    trace_ids = jnp.sum((token_index[:, None] >= trace_ends[None, :]).astype(jnp.int32), axis=1)
    member = trace_ids[:, None] == jnp.arange(lengths.shape[0], dtype=jnp.int32)[None, :]
    pos_shift = jnp.sum(jnp.where(member, (0 - starts)[None, :], 0), axis=1)
    return (trace_ids, token_index + pos_shift)


def rope_keys(latent, positions, latent_width):
    values = latent.astype(jnp.float32)
    half_width = (values.shape[0] - latent_width) // 2
    angles = rope_freqs(half_width)[:, None] * positions.astype(jnp.float32)[None, :]
    first_half = values[latent_width : latent_width + half_width]
    second_half = values[latent_width + half_width :]
    cosine = jnp.cos(angles)
    sine_value = jnp.sin(angles)
    return jnp.concatenate(
        [
            values[:latent_width],
            first_half * cosine - second_half * sine_value,
            first_half * sine_value + second_half * cosine,
        ],
        axis=0,
    ).astype(jnp.bfloat16)


def rope_tables(positions, half_width, lanes):
    angles = positions.astype(jnp.float32)[:, None] * rope_freqs(half_width)[None, :]
    cosine, sine_value = jnp.cos(angles), jnp.sin(angles)
    cos_part = jnp.concatenate([cosine, cosine], axis=1)
    sin_part = jnp.concatenate([-sine_value, sine_value], axis=1)
    rest = lanes - 2 * half_width
    ones = jnp.ones((angles.shape[0], rest), jnp.float32)
    zeros = jnp.zeros((angles.shape[0], rest), jnp.float32)
    return jnp.stack(
        [
            jnp.concatenate([cos_part, ones], axis=1),
            jnp.concatenate([sin_part, zeros], axis=1),
            jnp.concatenate([ones, cos_part], axis=1),
            jnp.concatenate([zeros, sin_part], axis=1),
        ]
    )


def attention_kernel(
    group, tables, starts, own_index, key_index, keys, queries, value_weight, out, even, odd, values, bias
):
    row_count = queries.shape[0]
    width = queries.shape[1] // group
    half_width = (width - LAT) // 2
    lanes = 2 * (width - LAT)

    @pl.when(pl.program_id(0) == 0)
    def prepare():
        all_keys = keys[...]
        pad = jnp.zeros((width - LAT, all_keys.shape[1]), jnp.bfloat16)
        even[:width] = all_keys
        even[width:] = pad
        odd[: width - LAT] = pad
        odd[width - LAT :] = all_keys
        values[...] = keys[:LAT].astype(jnp.float32).T.astype(jnp.bfloat16)
        allowed = (key_index[...] >= starts[...]) & (key_index[...] <= own_index[...])
        bias[...] = jnp.where(allowed, 0.0, masked_score)

    lane = lax.broadcasted_iota(jnp.int32, (row_count, lanes), 1)
    low = (lane & (2 * half_width - 1)) < half_width

    def turned(start, which):
        entry = queries[:, start : start + lanes].astype(jnp.float32)
        partner = jnp.where(
            low, pltpu.roll(entry, lanes - half_width, 1), pltpu.roll(entry, half_width, 1)
        )
        return (entry * tables[2 * which] + partner * tables[2 * which + 1]).astype(jnp.bfloat16)

    for which, key_rows in ((0, even), (1, odd)):
        rows = []
        for head in range(which, group, 2):
            base = (head - which) * width
            if which == 0:
                rows.append(
                    jnp.concatenate([queries[:, base : base + LAT], turned(base + LAT, 0)], axis=1)
                )
            else:
                first = base + LAT
                rows.append(
                    jnp.concatenate(
                        [queries[:, first : first + LAT], turned(first + LAT, 1)], axis=1
                    )
                )
        stacked = jnp.concatenate(rows, axis=0)
        scores = jnp.dot(stacked, key_rows[...], preferred_element_type=jnp.float32)
        scores = scores.reshape(len(rows), row_count, -1) + bias[...][None]
        top = jnp.max(scores, axis=2, keepdims=True)
        exponent = jnp.exp((scores - top) * score_scale)
        total = jnp.sum(exponent, axis=2, keepdims=True).reshape(len(rows) * row_count, 1)
        weights = exponent.astype(jnp.bfloat16).reshape(len(rows) * row_count, -1)
        mixed = jnp.dot(weights, values[...], preferred_element_type=jnp.float32)
        mixed = (mixed / total).astype(jnp.bfloat16)
        for i in range(len(rows)):
            head = 2 * i + which
            out[:, head * VHEAD : (head + 1) * VHEAD] = jnp.dot(
                mixed[i * row_count : (i + 1) * row_count],
                value_weight[:, head * VHEAD : (head + 1) * VHEAD],
                preferred_element_type=jnp.float32,
            ).astype(jnp.bfloat16)


def attention(queries, keys, key_index, own_index, own_position, value_weight):
    row_count, query_width = queries.shape
    local_heads = value_weight.shape[1] // VHEAD
    width = query_width // local_heads
    group = 4 if local_heads % 4 == 0 else 2
    key_count = keys.shape[1]
    tables = rope_tables(own_position, (width - LAT) // 2, 2 * (width - LAT))
    whole = lambda shape: pl.BlockSpec(shape, lambda i: (0,) * len(shape))
    deep = 2 * width - LAT
    return pl.pallas_call(
        functools.partial(attention_kernel, group),
        grid=(local_heads // group,),
        in_specs=[
            whole(tables.shape),
            whole((row_count, 1)),
            whole((row_count, 1)),
            whole((1, key_count)),
            whole(keys.shape),
            pl.BlockSpec((row_count, group * width), lambda i: (0, i)),
            pl.BlockSpec((LAT, group * VHEAD), lambda i: (0, i)),
        ],
        out_specs=pl.BlockSpec((row_count, group * VHEAD), lambda i: (0, i)),
        out_shape=jax.ShapeDtypeStruct((row_count, local_heads * VHEAD), jnp.bfloat16),
        scratch_shapes=[
            pltpu.VMEM((deep, key_count), jnp.bfloat16),
            pltpu.VMEM((deep, key_count), jnp.bfloat16),
            pltpu.VMEM((key_count, LAT), jnp.bfloat16),
            pltpu.VMEM((row_count, key_count), jnp.float32),
        ],
        compiler_params=pltpu.CompilerParams(vmem_limit_bytes=(6 + key_count // 64) * 1024 * 1024),
        cost_estimate=pl.CostEstimate(
            flops=2 * row_count * local_heads * (key_count * (deep + LAT) + LAT * VHEAD),
            bytes_accessed=2 * (queries.size + keys.size + value_weight.size),
            transcendentals=row_count * local_heads * key_count,
        ),
    )(
        tables,
        (own_index - own_position)[:, None],
        own_index[:, None],
        key_index[None, :],
        keys,
        queries,
        value_weight,
    )


def swap(value, axis_name, bit):
    width = lax.axis_size(axis_name)
    return lax.ppermute(value, axis_name, [(i, i ^ bit) for i in range(width)])


def pick(value, index):
    return lax.dynamic_index_in_dim(value, index, 0, keepdims=False)


def wide(value):
    return value.astype(jnp.float32)


def matmul(a, b):
    return jnp.dot(a, b, preferred_element_type=jnp.float32).astype(jnp.bfloat16)


def load_kernel(chunks, weight, out, sems):
    rows = weight.shape[0] // chunks
    copies = [
        pltpu.make_async_copy(
            weight.at[pl.ds(i * rows, rows)], out.at[pl.ds(i * rows, rows)], sems.at[i]
        )
        for i in range(chunks)
    ]
    for copy in copies:
        copy.start()
    for copy in copies:
        copy.wait()


def load(weight, grant):
    chunks = 8
    return pl.pallas_call(
        functools.partial(load_kernel, chunks),
        in_specs=[pl.BlockSpec(memory_space=pltpu.HBM)],
        out_specs=pl.BlockSpec(memory_space=pltpu.VMEM),
        out_shape=pltpu.VMEM(weight.shape, weight.dtype),
        scratch_shapes=[pltpu.SemaphoreType.DMA((chunks,))],
        compiler_params=pltpu.CompilerParams(vmem_limit_bytes=grant * 1024 * 1024),
        cost_estimate=pl.CostEstimate(flops=0, bytes_accessed=1024, transcendentals=0),
    )(weight)


def after(value, earlier):
    return lax.optimization_barrier((value, earlier))[0]


def gather_keys(rotated_keys, n_ctx):
    rows = rotated_keys.shape[0] // 2
    core = lax.axis_index("tp") & 1
    half = lax.dynamic_slice_in_dim(rotated_keys, core * rows, rows, 0)
    came = [
        lax.ppermute(half, "ctx", [(c, c + d) for c in range(n_ctx - d)])
        for d in range(n_ctx - 1, 0, -1)
    ]
    mine = jnp.concatenate(came, axis=1)
    other = swap(mine, "tp", 1)
    before = jnp.concatenate(
        [jnp.where(core == 0, mine, other), jnp.where(core == 0, other, mine)], axis=0
    )
    return jnp.concatenate([before, rotated_keys], axis=1)


def spread_heads(heads_out, n_ctx, n_tp):
    pieces = heads_out.reshape(n_ctx, heads_out.shape[0] // n_ctx, heads_out.shape[1])
    return [
        lax.ppermute(
            pieces[s],
            ("ctx", "tp"),
            [(c * n_tp + t, t * n_tp + (c ^ s)) for c in range(n_ctx) for t in range(n_tp)],
        )
        for s in range(n_ctx)
    ]


def pair_rows(first, second):
    return jnp.concatenate(
        [first[0], second[1], second[0], first[1], first[2], second[3], second[2], first[3]], axis=0
    )


def paired_tail(
    heads_out, residual, output_weight, norm_gain, gate_weight, up_weight, down_weight, n_ctx, n_tp
):
    row_count, width = residual.shape
    half = row_count // 2
    model_width = width * n_tp
    c = lax.axis_index("ctx")
    t = lax.axis_index("tp")
    core = t & 1
    first_half = (t >> 1) ^ (c >> 1)
    own = spread_heads(heads_out, n_ctx, n_tp)
    gate_weight = load(after(gate_weight, heads_out), 44)
    up_weight = load(after(up_weight, gate_weight), 34)
    own_all = jnp.stack(after(own, up_weight))
    near = swap(own_all, "tp", 1)
    residual_halves = residual.reshape(2, half, width)

    def first_hop(rows):
        blocks = matmul(rows, output_weight).reshape(n_ctx, half, width)
        place = t ^ c
        sent = jnp.stack([pick(blocks, place ^ 1), pick(blocks, place ^ 3)])
        kept = [pick(blocks, place), pick(blocks, place ^ 2)]
        return kept, sent, swap(sent, "ctx", 1)

    def second_hop(kept, came):
        other = (wide(kept[1]) + wide(came[1])).astype(jnp.bfloat16)
        return wide(kept[0]) + wide(came[0]), other, swap(other, "ctx", 2)

    def attend(mine, came, which):
        return (wide(pick(residual_halves, which)) + mine + wide(came)).astype(jnp.bfloat16)

    def gate_up(rows):
        values = wide(rows)
        scaled = (values * norm_gain[None, :]).astype(jnp.bfloat16)
        terms = [matmul(scaled, gate_weight), matmul(scaled, up_weight)]

        def side(which):
            return jnp.concatenate(
                [lax.dynamic_slice_in_dim(term, which * half, half, 0) for term in terms], axis=0
            )

        return side(core), side(1 - core), jnp.sum(values * values, axis=1)

    def chip_sum(kept, sent):
        return wide(kept) + wide(swap(sent, "tp", 1))

    kept_a, sent_a, came_a = first_hop(pair_rows(own_all, near))
    far = swap(after(own_all, sent_a), "tp", 2)
    mine_a, other_a, last_a = second_hop(kept_a, came_a)
    far = after(far, other_a)
    far_near = swap(far, "tp", 1)
    attended_a = attend(mine_a, after(last_a, far), first_half)
    twin_a = swap(attended_a, "ctx", 2)
    far_near = after(far_near, attended_a)
    order = [2, 3, 0, 1]
    rows_b = pair_rows([far[i] for i in order], [far_near[i] for i in order])
    kept_b, sent_b, came_b = first_hop(rows_b)
    mine_b, other_b, last_b = second_hop(kept_b, came_b)
    pair_a = jnp.concatenate([attended_a, after(twin_a, other_b)], axis=0)
    rest_a = swap(pair_a, "ctx", 1)
    kept, sent, squares_p = gate_up(pair_a)
    sums_p = chip_sum(kept, sent).astype(jnp.bfloat16)
    across_p = swap(sums_p, "tp", 2)
    attended_b = attend(mine_b, after(last_b, sums_p), 1 - first_half)
    twin_b = swap(attended_b, "ctx", 2)
    rest_a, across_p, twin_b = lax.optimization_barrier((rest_a, across_p, twin_b))
    kept, sent, squares_q = gate_up(rest_a)
    sums_q = chip_sum(kept, sent).astype(jnp.bfloat16)
    across_q = swap(sums_q, "tp", 2)
    squares_a = jnp.concatenate([squares_p, squares_q])
    across_squares = swap(squares_a + swap(squares_a, "tp", 1), "tp", 2)
    pair_b = jnp.concatenate([attended_b, twin_b], axis=0)
    rest_b = swap(pair_b, "ctx", 1)

    def hide(chip_terms, squares, across, across_squares):
        squares = squares + swap(squares, "tp", 1) + across_squares
        squares = lax.dynamic_slice_in_dim(squares, core * half, half, 0)
        inverse_rms = lax.rsqrt(squares / model_width + norm_eps)[:, None]
        gate = (chip_terms[:half] + wide(across[:half])) * inverse_rms
        up = (chip_terms[half:] + wide(across[half:])) * inverse_rms
        return (jax.nn.silu(gate) * up).astype(jnp.bfloat16)

    kept, sent, squares_p = gate_up(after(pair_b, sums_q))
    terms_p = chip_sum(kept, sent)
    down_weight = load(after(down_weight, sums_q), 24)
    rest_b, across_q, _, _ = lax.optimization_barrier((rest_b, across_q, sent, down_weight))
    kept, sent, squares_q = gate_up(rest_b)
    terms_q = chip_sum(kept, sent)
    hidden = jnp.concatenate(
        [
            hide(terms_p, squares_p, across_p, across_squares[: 2 * half]),
            hide(terms_q, squares_q, across_q, across_squares[2 * half :]),
        ],
        axis=0,
    )
    hidden_near = swap(hidden, "tp", 1)
    hidden_far = swap(hidden, "tp", 2)

    def down_hop(mine, other):
        blocks = matmul(jnp.concatenate([mine, other], axis=0), down_weight)
        blocks = blocks.reshape(2, 2, half, width)
        return blocks[:, 0], swap(blocks[:, 1], "ctx", 1)

    def down_second(kept, came):
        pair = wide(kept) + wide(came)
        other = pick(pair, 1 - core).astype(jnp.bfloat16)
        return pick(pair, core), other, swap(other, "ctx", 2)

    kept_b, came_b = down_hop(hidden, hidden_near)
    hidden_far = after(hidden_far, kept_b)
    hidden_far_near = swap(hidden_far, "tp", 1)
    down_b, other_b, last_b = down_second(kept_b, after(came_b, hidden_far))
    down_a, _, last_a = down_second(*down_hop(hidden_far, after(hidden_far_near, other_b)))
    out_b = (wide(attended_b) + down_b + wide(last_b)).astype(jnp.bfloat16)
    out_a = (wide(attended_a) + down_a + wide(last_a)).astype(jnp.bfloat16)

    def in_order(a, b):
        first = first_half == 0
        return jnp.concatenate([jnp.where(first, a, b), jnp.where(first, b, a)], axis=0)

    return in_order(attended_a, attended_b), in_order(out_a, out_b)


def on_device(
    residual,
    latent,
    queries,
    lengths,
    value_weight,
    output_weight,
    norm_gain,
    gate_weight,
    up_weight,
    down_weight,
):
    row_count = residual.shape[0]
    ctx_place = lax.axis_index("ctx")
    n_ctx, n_tp = lax.axis_size("ctx"), lax.axis_size("tp")
    paired = n_ctx == 4 and n_tp == 4 and row_count % 64 == 0 and residual.shape[1] % 256 == 0
    own_index = ctx_place * row_count + jnp.arange(row_count, dtype=jnp.int32)
    _, own_position = trace_info(own_index, lengths)
    rotated_keys = rope_keys(latent, own_position, LAT)
    key_order = jnp.arange(n_ctx * row_count, dtype=jnp.int32)
    if paired:
        keys = gather_keys(rotated_keys, n_ctx)
        key_index = key_order + (ctx_place - (n_ctx - 1)) * row_count
    else:
        keys = lax.all_gather(rotated_keys, "ctx", axis=1, tiled=True)
        key_index = key_order
    heads_out = attention(queries, keys, key_index, own_index, own_position, value_weight)
    if paired:
        return paired_tail(
            heads_out,
            residual,
            output_weight,
            norm_gain,
            gate_weight,
            up_weight,
            down_weight,
            n_ctx,
            n_tp,
        )
    all_heads = lax.all_gather(heads_out, "tp", axis=1, tiled=True)
    head_block = lax.all_to_all(all_heads, "ctx", split_axis=1, concat_axis=0, tiled=True)
    head_sum = lax.psum_scatter(
        jnp.dot(head_block, output_weight, preferred_element_type=jnp.float32).astype(jnp.bfloat16),
        "ctx",
        scatter_dimension=0,
        tiled=True,
    ).astype(jnp.float32)
    attended = (residual.astype(jnp.float32) + head_sum).astype(jnp.bfloat16)
    attended_float = attended.astype(jnp.float32)
    squares = lax.psum(jnp.sum(attended_float * attended_float, axis=1), "tp")
    inverse_rms = lax.rsqrt(squares / D + norm_eps)
    scaled = (attended_float * inverse_rms[:, None] * norm_gain[None, :]).astype(jnp.bfloat16)
    scaled_all = lax.all_gather(scaled, "ctx", axis=0, tiled=True)
    unit_count = gate_weight.shape[1]
    gate_up = jnp.concatenate([gate_weight, up_weight], axis=1)
    summed = lax.psum_scatter(
        jnp.dot(scaled_all, gate_up, preferred_element_type=jnp.float32).astype(jnp.bfloat16),
        "tp",
        scatter_dimension=0,
        tiled=True,
    ).astype(jnp.float32)
    hidden_share = (jax.nn.silu(summed[:, :unit_count]) * summed[:, unit_count:]).astype(
        jnp.bfloat16
    )
    hidden_all = lax.all_gather(hidden_share, "tp", axis=0, tiled=True)
    down_sum = lax.psum_scatter(
        jnp.dot(hidden_all, down_weight, preferred_element_type=jnp.float32).astype(jnp.bfloat16),
        "ctx",
        scatter_dimension=0,
        tiled=True,
    ).astype(jnp.float32)
    layer_out = (attended_float + down_sum).astype(jnp.bfloat16)
    return (attended, layer_out)


def solution(mesh):
    in_specs = (
        P(("grp", "ctx"), "tp"),
        P(None, ("grp", "ctx")),
        P(("grp", "ctx"), "tp"),
        P("grp"),
        P(None, "tp"),
        P("ctx", "tp"),
        P("tp"),
        P("tp", "ctx"),
        P("tp", "ctx"),
        P("ctx", "tp"),
    )
    out_specs = (P(("grp", "ctx"), "tp"), P(("grp", "ctx"), "tp"))
    return jax.shard_map(
        on_device, mesh=mesh, in_specs=in_specs, out_specs=out_specs, check_vma=False
    )
```

```python
import functools

import jax
import jax.numpy as jnp
from jax import lax
from jax.experimental import pallas as pl
from jax.experimental.pallas import tpu as pltpu
from jax.sharding import PartitionSpec as P

D = 7168
LAT = 512
ROPE = 64
VHEAD = 128


score_scale = 192.0 ** (-0.5)
rope_base = 10000.0
norm_eps = 1e-06
masked_score = -1e30


def rope_freqs(half_width):
    return rope_base ** (-jnp.arange(half_width, dtype=jnp.float32) / half_width)


def trace_info(token_index, lengths):
    trace_ends = jnp.cumsum(lengths)
    starts = trace_ends - lengths
    trace_ids = jnp.sum((token_index[:, None] >= trace_ends[None, :]).astype(jnp.int32), axis=1)
    member = trace_ids[:, None] == jnp.arange(lengths.shape[0], dtype=jnp.int32)[None, :]
    pos_shift = jnp.sum(jnp.where(member, (0 - starts)[None, :], 0), axis=1)
    return (trace_ids, token_index + pos_shift)


def rope_keys(latent, positions, latent_width):
    values = latent.astype(jnp.float32)
    half_width = (values.shape[0] - latent_width) // 2
    angles = rope_freqs(half_width)[:, None] * positions.astype(jnp.float32)[None, :]
    first_half = values[latent_width : latent_width + half_width]
    second_half = values[latent_width + half_width :]
    cosine = jnp.cos(angles)
    sine_value = jnp.sin(angles)
    return jnp.concatenate(
        [
            values[:latent_width],
            first_half * cosine - second_half * sine_value,
            first_half * sine_value + second_half * cosine,
        ],
        axis=0,
    ).astype(jnp.bfloat16)


def rope_tables(positions, half_width, lanes):
    angles = positions.astype(jnp.float32)[:, None] * rope_freqs(half_width)[None, :]
    cosine, sine_value = jnp.cos(angles), jnp.sin(angles)
    cos_part = jnp.concatenate([cosine, cosine], axis=1)
    sin_part = jnp.concatenate([-sine_value, sine_value], axis=1)
    rest = lanes - 2 * half_width
    ones = jnp.ones((angles.shape[0], rest), jnp.float32)
    zeros = jnp.zeros((angles.shape[0], rest), jnp.float32)
    return jnp.stack(
        [
            jnp.concatenate([cos_part, ones], axis=1),
            jnp.concatenate([sin_part, zeros], axis=1),
            jnp.concatenate([ones, cos_part], axis=1),
            jnp.concatenate([zeros, sin_part], axis=1),
        ]
    )


def attention_kernel(
    group, tables, starts, own_index, key_index, keys, queries, value_weight, out, even, odd, values, bias
):
    row_count = queries.shape[0]
    width = queries.shape[1] // group
    half_width = (width - LAT) // 2
    lanes = 2 * (width - LAT)

    @pl.when(pl.program_id(0) == 0)
    def prepare():
        all_keys = keys[...]
        pad = jnp.zeros((width - LAT, all_keys.shape[1]), jnp.bfloat16)
        even[:width] = all_keys
        even[width:] = pad
        odd[: width - LAT] = pad
        odd[width - LAT :] = all_keys
        values[...] = keys[:LAT].astype(jnp.float32).T.astype(jnp.bfloat16)
        allowed = (key_index[...] >= starts[...]) & (key_index[...] <= own_index[...])
        bias[...] = jnp.where(allowed, 0.0, masked_score)

    lane = lax.broadcasted_iota(jnp.int32, (row_count, lanes), 1)
    low = (lane & (2 * half_width - 1)) < half_width

    def turned(start, which):
        entry = queries[:, start : start + lanes].astype(jnp.float32)
        partner = jnp.where(
            low, pltpu.roll(entry, lanes - half_width, 1), pltpu.roll(entry, half_width, 1)
        )
        return (entry * tables[2 * which] + partner * tables[2 * which + 1]).astype(jnp.bfloat16)

    for which, key_rows in ((0, even), (1, odd)):
        rows = []
        for head in range(which, group, 2):
            base = (head - which) * width
            if which == 0:
                rows.append(
                    jnp.concatenate([queries[:, base : base + LAT], turned(base + LAT, 0)], axis=1)
                )
            else:
                first = base + LAT
                rows.append(
                    jnp.concatenate(
                        [queries[:, first : first + LAT], turned(first + LAT, 1)], axis=1
                    )
                )
        stacked = jnp.concatenate(rows, axis=0)
        scores = jnp.dot(stacked, key_rows[...], preferred_element_type=jnp.float32)
        scores = scores.reshape(len(rows), row_count, -1) + bias[...][None]
        top = jnp.max(scores, axis=2, keepdims=True)
        exponent = jnp.exp((scores - top) * score_scale)
        total = jnp.sum(exponent, axis=2, keepdims=True).reshape(len(rows) * row_count, 1)
        weights = exponent.astype(jnp.bfloat16).reshape(len(rows) * row_count, -1)
        mixed = jnp.dot(weights, values[...], preferred_element_type=jnp.float32)
        mixed = (mixed / total).astype(jnp.bfloat16)
        for i in range(len(rows)):
            head = 2 * i + which
            out[:, head * VHEAD : (head + 1) * VHEAD] = jnp.dot(
                mixed[i * row_count : (i + 1) * row_count],
                value_weight[:, head * VHEAD : (head + 1) * VHEAD],
                preferred_element_type=jnp.float32,
            ).astype(jnp.bfloat16)


def attention(queries, keys, key_index, own_index, own_position, value_weight):
    row_count, query_width = queries.shape
    local_heads = value_weight.shape[1] // VHEAD
    width = query_width // local_heads
    group = 4 if local_heads % 4 == 0 else 2
    key_count = keys.shape[1]
    tables = rope_tables(own_position, (width - LAT) // 2, 2 * (width - LAT))
    whole = lambda shape: pl.BlockSpec(shape, lambda i: (0,) * len(shape))
    deep = 2 * width - LAT
    return pl.pallas_call(
        functools.partial(attention_kernel, group),
        grid=(local_heads // group,),
        in_specs=[
            whole(tables.shape),
            whole((row_count, 1)),
            whole((row_count, 1)),
            whole((1, key_count)),
            whole(keys.shape),
            pl.BlockSpec((row_count, group * width), lambda i: (0, i)),
            pl.BlockSpec((LAT, group * VHEAD), lambda i: (0, i)),
        ],
        out_specs=pl.BlockSpec((row_count, group * VHEAD), lambda i: (0, i)),
        out_shape=jax.ShapeDtypeStruct((row_count, local_heads * VHEAD), jnp.bfloat16),
        scratch_shapes=[
            pltpu.VMEM((deep, key_count), jnp.bfloat16),
            pltpu.VMEM((deep, key_count), jnp.bfloat16),
            pltpu.VMEM((key_count, LAT), jnp.bfloat16),
            pltpu.VMEM((row_count, key_count), jnp.float32),
        ],
        compiler_params=pltpu.CompilerParams(vmem_limit_bytes=(6 + key_count // 64) * 1024 * 1024),
        cost_estimate=pl.CostEstimate(
            flops=2 * row_count * local_heads * (key_count * (deep + LAT) + LAT * VHEAD),
            bytes_accessed=2 * (queries.size + keys.size + value_weight.size),
            transcendentals=row_count * local_heads * key_count,
        ),
    )(
        tables,
        (own_index - own_position)[:, None],
        own_index[:, None],
        key_index[None, :],
        keys,
        queries,
        value_weight,
    )


def swap(value, axis_name, bit):
    width = lax.axis_size(axis_name)
    return lax.ppermute(value, axis_name, [(i, i ^ bit) for i in range(width)])


def pick(value, index):
    return lax.dynamic_index_in_dim(value, index, 0, keepdims=False)


def wide(value):
    return value.astype(jnp.float32)


def matmul(a, b):
    return jnp.dot(a, b, preferred_element_type=jnp.float32).astype(jnp.bfloat16)


def streamed_kernel(depth, rows, weight, out, held, total, sems):
    steps = weight.shape[0] // depth
    copies = [
        pltpu.make_async_copy(
            weight.at[pl.ds(i * depth, depth)], held.at[pl.ds(i * depth, depth)], sems.at[i]
        )
        for i in range(steps)
    ]
    for copy in copies:
        copy.start()
    block = 256
    for i, copy in enumerate(copies):
        copy.wait()
        part = rows[:, i * depth : (i + 1) * depth]
        for start in range(0, weight.shape[1], block):
            columns = slice(start, start + block)
            term = jnp.dot(
                part,
                held[i * depth : (i + 1) * depth, columns],
                preferred_element_type=jnp.float32,
            )
            if i > 0:
                term = term + total[:, columns]
            if i < steps - 1:
                total[:, columns] = term
            else:
                out[:, columns] = term.astype(out.dtype)


def streamed_matmul(rows, weight):
    steps = weight.shape[0] // 512
    return pl.pallas_call(
        functools.partial(streamed_kernel, 512),
        in_specs=[
            pl.BlockSpec(memory_space=pltpu.VMEM),
            pl.BlockSpec(memory_space=pl.ANY),
        ],
        out_specs=pl.BlockSpec(memory_space=pltpu.VMEM),
        out_shape=jax.ShapeDtypeStruct((rows.shape[0], weight.shape[1]), jnp.bfloat16),
        scratch_shapes=[
            pltpu.VMEM(weight.shape, weight.dtype),
            pltpu.VMEM((rows.shape[0], weight.shape[1]), jnp.float32),
            pltpu.SemaphoreType.DMA((steps,)),
        ],
        compiler_params=pltpu.CompilerParams(vmem_limit_bytes=50 * 1024 * 1024),
        cost_estimate=pl.CostEstimate(flops=1024, bytes_accessed=1024, transcendentals=0),
    )(rows, weight)


def after(value, earlier):
    return lax.optimization_barrier((value, earlier))[0]


def gather_keys(rotated_keys, n_ctx):
    rows = rotated_keys.shape[0] // 2
    core = lax.axis_index("tp") & 1
    half = lax.dynamic_slice_in_dim(rotated_keys, core * rows, rows, 0)
    came = [
        lax.ppermute(half, "ctx", [(c, c + d) for c in range(n_ctx - d)])
        for d in range(n_ctx - 1, 0, -1)
    ]
    mine = jnp.concatenate(came, axis=1)
    other = swap(mine, "tp", 1)
    before = jnp.concatenate(
        [jnp.where(core == 0, mine, other), jnp.where(core == 0, other, mine)], axis=0
    )
    return jnp.concatenate([before, rotated_keys], axis=1)


def spread_heads(heads_out, n_ctx, n_tp):
    c, t = lax.axis_index("ctx"), lax.axis_index("tp")
    quarters = heads_out.reshape(n_tp, heads_out.shape[0] // n_tp, heads_out.shape[1])
    groups = jnp.stack(
        [pick(quarters, t)] + [swap(pick(quarters, t ^ m), "tp", m) for m in range(1, n_tp)]
    )
    return jnp.stack(
        [pick(groups, t ^ c)] + [swap(pick(groups, t ^ c ^ j), "ctx", j) for j in range(1, n_ctx)]
    )


def core_rows(mine, other):
    first = lax.axis_index("tp") & 1 == 0
    both = jnp.stack([jnp.where(first, mine, other), jnp.where(first, other, mine)], axis=1)
    return both.reshape(-1, mine.shape[-1])


def paired_tail(
    heads_out, residual, output_weight, norm_gain, gate_weight, up_weight, down_weight, n_ctx, n_tp
):
    row_count, width = residual.shape
    half = row_count // 2
    model_width = width * n_tp
    t = lax.axis_index("tp")
    core = t & 1
    first_half = t >> 1
    own = spread_heads(heads_out, n_ctx, n_tp)
    near = swap(own, "tp", 1)
    far = swap(own, "tp", 2)
    residual_halves = residual.reshape(2, half, width)

    def first_hop(rows):
        blocks = streamed_matmul(rows, output_weight).reshape(2, 2, half, width)
        sent = blocks[:, 1]
        return blocks[:, 0], sent, swap(sent, "ctx", 1)

    def second_hop(kept, came):
        other = (wide(kept[1]) + wide(came[1])).astype(jnp.bfloat16)
        return wide(kept[0]) + wide(came[0]), other, swap(other, "ctx", 2)

    def attend(mine, came, which):
        return (wide(pick(residual_halves, which)) + mine + wide(came)).astype(jnp.bfloat16)

    def gate_up(rows):
        values = wide(rows)
        scaled = (values * norm_gain[None, :]).astype(jnp.bfloat16)
        terms = [matmul(scaled, gate_weight), matmul(scaled, up_weight)]

        def side(which):
            return jnp.concatenate(
                [lax.dynamic_slice_in_dim(term, which * half, half, 0) for term in terms], axis=0
            )

        return side(core), side(1 - core), jnp.sum(values * values, axis=1)

    def chip_sum(kept, sent):
        return wide(kept) + wide(swap(sent, "tp", 1))

    kept_a, sent_a, came_a = first_hop(core_rows(own, near))
    far = after(far, sent_a)
    far_near = swap(far, "tp", 1)
    mine_a, other_a, last_a = second_hop(kept_a, came_a)
    kept_b, sent_b, came_b = first_hop(core_rows(far, after(far_near, other_a)))
    attended_a = attend(mine_a, after(last_a, sent_b), first_half)
    twin_a = swap(attended_a, "ctx", 2)
    mine_b, other_b, last_b = second_hop(kept_b, after(came_b, attended_a))
    pair_a = jnp.concatenate([attended_a, after(twin_a, other_b)], axis=0)
    rest_a = swap(pair_a, "ctx", 1)
    kept, sent, squares_p = gate_up(pair_a)
    sums_p = chip_sum(kept, sent).astype(jnp.bfloat16)
    across_p = swap(sums_p, "tp", 2)
    attended_b = attend(mine_b, after(last_b, sums_p), 1 - first_half)
    twin_b = swap(attended_b, "ctx", 2)
    rest_a, across_p, twin_b = lax.optimization_barrier((rest_a, across_p, twin_b))
    kept, sent, squares_q = gate_up(rest_a)
    sums_q = chip_sum(kept, sent).astype(jnp.bfloat16)
    across_q = swap(sums_q, "tp", 2)
    squares_a = jnp.concatenate([squares_p, squares_q])
    across_squares = swap(squares_a + swap(squares_a, "tp", 1), "tp", 2)
    pair_b = jnp.concatenate([attended_b, twin_b], axis=0)
    rest_b = swap(pair_b, "ctx", 1)

    def hide(chip_terms, squares, across, across_squares):
        squares = squares + swap(squares, "tp", 1) + across_squares
        squares = lax.dynamic_slice_in_dim(squares, core * half, half, 0)
        inverse_rms = lax.rsqrt(squares / model_width + norm_eps)[:, None]
        gate = (chip_terms[:half] + wide(across[:half])) * inverse_rms
        up = (chip_terms[half:] + wide(across[half:])) * inverse_rms
        return (jax.nn.silu(gate) * up).astype(jnp.bfloat16)

    kept, sent, squares_p = gate_up(after(pair_b, sums_q))
    terms_p = chip_sum(kept, sent)
    rest_b, across_q, _ = lax.optimization_barrier((rest_b, across_q, sent))
    kept, sent, squares_q = gate_up(rest_b)
    terms_q = chip_sum(kept, sent)
    hidden = jnp.concatenate(
        [
            hide(terms_p, squares_p, across_p, across_squares[: 2 * half]),
            hide(terms_q, squares_q, across_q, across_squares[2 * half :]),
        ],
        axis=0,
    )
    hidden_near = swap(hidden, "tp", 1)
    hidden_far = swap(hidden, "tp", 2)

    def down_hop(mine, other):
        blocks = streamed_matmul(jnp.concatenate([mine, other], axis=0), down_weight)
        blocks = blocks.reshape(2, 2, half, width)
        return blocks[:, 0], swap(blocks[:, 1], "ctx", 1)

    def down_second(kept, came):
        pair = wide(kept) + wide(came)
        other = pick(pair, 1 - core).astype(jnp.bfloat16)
        return pick(pair, core), other, swap(other, "ctx", 2)

    kept_b, came_b = down_hop(hidden, hidden_near)
    hidden_far = after(hidden_far, kept_b)
    hidden_far_near = swap(hidden_far, "tp", 1)
    down_b, other_b, last_b = down_second(kept_b, after(came_b, hidden_far))
    down_a, _, last_a = down_second(*down_hop(hidden_far, after(hidden_far_near, other_b)))
    out_b = (wide(attended_b) + down_b + wide(last_b)).astype(jnp.bfloat16)
    out_a = (wide(attended_a) + down_a + wide(last_a)).astype(jnp.bfloat16)

    def in_order(a, b):
        first = first_half == 0
        return jnp.concatenate([jnp.where(first, a, b), jnp.where(first, b, a)], axis=0)

    return in_order(attended_a, attended_b), in_order(out_a, out_b)


def on_device(
    residual,
    latent,
    queries,
    lengths,
    value_weight,
    output_weight,
    norm_gain,
    gate_weight,
    up_weight,
    down_weight,
):
    row_count = residual.shape[0]
    ctx_place = lax.axis_index("ctx")
    n_ctx, n_tp = lax.axis_size("ctx"), lax.axis_size("tp")
    paired = (
        n_ctx == 4
        and n_tp == 4
        and row_count % 64 == 0
        and residual.shape[1] % 256 == 0
        and output_weight.shape[0] % 512 == 0
        and down_weight.shape[0] % 512 == 0
    )
    own_index = ctx_place * row_count + jnp.arange(row_count, dtype=jnp.int32)
    _, own_position = trace_info(own_index, lengths)
    rotated_keys = rope_keys(latent, own_position, LAT)
    key_order = jnp.arange(n_ctx * row_count, dtype=jnp.int32)
    if paired:
        keys = gather_keys(rotated_keys, n_ctx)
        key_index = key_order + (ctx_place - (n_ctx - 1)) * row_count
    else:
        keys = lax.all_gather(rotated_keys, "ctx", axis=1, tiled=True)
        key_index = key_order
    heads_out = attention(queries, keys, key_index, own_index, own_position, value_weight)
    if paired:
        return paired_tail(
            heads_out,
            residual,
            output_weight,
            norm_gain,
            gate_weight,
            up_weight,
            down_weight,
            n_ctx,
            n_tp,
        )
    all_heads = lax.all_gather(heads_out, "tp", axis=1, tiled=True)
    head_block = lax.all_to_all(all_heads, "ctx", split_axis=1, concat_axis=0, tiled=True)
    head_sum = lax.psum_scatter(
        jnp.dot(head_block, output_weight, preferred_element_type=jnp.float32).astype(jnp.bfloat16),
        "ctx",
        scatter_dimension=0,
        tiled=True,
    ).astype(jnp.float32)
    attended = (residual.astype(jnp.float32) + head_sum).astype(jnp.bfloat16)
    attended_float = attended.astype(jnp.float32)
    squares = lax.psum(jnp.sum(attended_float * attended_float, axis=1), "tp")
    inverse_rms = lax.rsqrt(squares / D + norm_eps)
    scaled = (attended_float * inverse_rms[:, None] * norm_gain[None, :]).astype(jnp.bfloat16)
    scaled_all = lax.all_gather(scaled, "ctx", axis=0, tiled=True)
    unit_count = gate_weight.shape[1]
    gate_up = jnp.concatenate([gate_weight, up_weight], axis=1)
    summed = lax.psum_scatter(
        jnp.dot(scaled_all, gate_up, preferred_element_type=jnp.float32).astype(jnp.bfloat16),
        "tp",
        scatter_dimension=0,
        tiled=True,
    ).astype(jnp.float32)
    hidden_share = (jax.nn.silu(summed[:, :unit_count]) * summed[:, unit_count:]).astype(
        jnp.bfloat16
    )
    hidden_all = lax.all_gather(hidden_share, "tp", axis=0, tiled=True)
    down_sum = lax.psum_scatter(
        jnp.dot(hidden_all, down_weight, preferred_element_type=jnp.float32).astype(jnp.bfloat16),
        "ctx",
        scatter_dimension=0,
        tiled=True,
    ).astype(jnp.float32)
    layer_out = (attended_float + down_sum).astype(jnp.bfloat16)
    return (attended, layer_out)


def solution(mesh):
    in_specs = (
        P(("grp", "ctx"), "tp"),
        P(None, ("grp", "ctx")),
        P(("grp", "ctx"), "tp"),
        P("grp"),
        P(None, "tp"),
        P("ctx", "tp"),
        P("tp"),
        P("tp", "ctx"),
        P("tp", "ctx"),
        P("ctx", "tp"),
    )
    out_specs = (P(("grp", "ctx"), "tp"), P(("grp", "ctx"), "tp"))
    return jax.shard_map(
        on_device, mesh=mesh, in_specs=in_specs, out_specs=out_specs, check_vma=False
    )
```

```python
import functools

import jax
import jax.numpy as jnp
from jax import lax
from jax.experimental import pallas as pl
from jax.experimental.pallas import tpu as pltpu
from jax.sharding import PartitionSpec as P

D = 7168
LAT = 512
ROPE = 64
VHEAD = 128


score_scale = 192.0 ** (-0.5)
rope_base = 10000.0
norm_eps = 1e-06
masked_score = -1e30


def rope_freqs(half_width):
    return rope_base ** (-jnp.arange(half_width, dtype=jnp.float32) / half_width)


def trace_info(token_index, lengths):
    trace_ends = jnp.cumsum(lengths)
    starts = trace_ends - lengths
    trace_ids = jnp.sum((token_index[:, None] >= trace_ends[None, :]).astype(jnp.int32), axis=1)
    member = trace_ids[:, None] == jnp.arange(lengths.shape[0], dtype=jnp.int32)[None, :]
    pos_shift = jnp.sum(jnp.where(member, (0 - starts)[None, :], 0), axis=1)
    return (trace_ids, token_index + pos_shift)


def rope_keys(latent, positions, latent_width):
    values = latent.astype(jnp.float32)
    half_width = (values.shape[0] - latent_width) // 2
    angles = rope_freqs(half_width)[:, None] * positions.astype(jnp.float32)[None, :]
    first_half = values[latent_width : latent_width + half_width]
    second_half = values[latent_width + half_width :]
    cosine = jnp.cos(angles)
    sine_value = jnp.sin(angles)
    return jnp.concatenate(
        [
            values[:latent_width],
            first_half * cosine - second_half * sine_value,
            first_half * sine_value + second_half * cosine,
        ],
        axis=0,
    ).astype(jnp.bfloat16)


def rope_tables(positions, half_width, lanes):
    angles = positions.astype(jnp.float32)[:, None] * rope_freqs(half_width)[None, :]
    cosine, sine_value = jnp.cos(angles), jnp.sin(angles)
    cos_part = jnp.concatenate([cosine, cosine], axis=1)
    sin_part = jnp.concatenate([-sine_value, sine_value], axis=1)
    rest = lanes - 2 * half_width
    ones = jnp.ones((angles.shape[0], rest), jnp.float32)
    zeros = jnp.zeros((angles.shape[0], rest), jnp.float32)
    return jnp.stack(
        [
            jnp.concatenate([cos_part, ones], axis=1),
            jnp.concatenate([sin_part, zeros], axis=1),
            jnp.concatenate([ones, cos_part], axis=1),
            jnp.concatenate([zeros, sin_part], axis=1),
        ]
    )


def attention_kernel(
    group, tables, starts, own_index, key_index, keys, queries, value_weight, out, even, odd, values, bias
):
    row_count = queries.shape[0]
    width = queries.shape[1] // group
    half_width = (width - LAT) // 2
    lanes = 2 * (width - LAT)

    @pl.when(pl.program_id(0) == 0)
    def prepare():
        all_keys = keys[...]
        pad = jnp.zeros((width - LAT, all_keys.shape[1]), jnp.bfloat16)
        even[:width] = all_keys
        even[width:] = pad
        odd[: width - LAT] = pad
        odd[width - LAT :] = all_keys
        values[...] = keys[:LAT].astype(jnp.float32).T.astype(jnp.bfloat16)
        allowed = (key_index[...] >= starts[...]) & (key_index[...] <= own_index[...])
        bias[...] = jnp.where(allowed, 0.0, masked_score)

    lane = lax.broadcasted_iota(jnp.int32, (row_count, lanes), 1)
    low = (lane & (2 * half_width - 1)) < half_width

    def turned(start, which):
        entry = queries[:, start : start + lanes].astype(jnp.float32)
        partner = jnp.where(
            low, pltpu.roll(entry, lanes - half_width, 1), pltpu.roll(entry, half_width, 1)
        )
        return (entry * tables[2 * which] + partner * tables[2 * which + 1]).astype(jnp.bfloat16)

    for which, key_rows in ((0, even), (1, odd)):
        rows = []
        for head in range(which, group, 2):
            base = (head - which) * width
            if which == 0:
                rows.append(
                    jnp.concatenate([queries[:, base : base + LAT], turned(base + LAT, 0)], axis=1)
                )
            else:
                first = base + LAT
                rows.append(
                    jnp.concatenate(
                        [queries[:, first : first + LAT], turned(first + LAT, 1)], axis=1
                    )
                )
        stacked = jnp.concatenate(rows, axis=0)
        scores = jnp.dot(stacked, key_rows[...], preferred_element_type=jnp.float32)
        scores = scores.reshape(len(rows), row_count, -1) + bias[...][None]
        top = jnp.max(scores, axis=2, keepdims=True)
        exponent = jnp.exp((scores - top) * score_scale)
        total = jnp.sum(exponent, axis=2, keepdims=True).reshape(len(rows) * row_count, 1)
        weights = exponent.astype(jnp.bfloat16).reshape(len(rows) * row_count, -1)
        mixed = jnp.dot(weights, values[...], preferred_element_type=jnp.float32)
        mixed = (mixed / total).astype(jnp.bfloat16)
        for i in range(len(rows)):
            head = 2 * i + which
            out[:, head * VHEAD : (head + 1) * VHEAD] = jnp.dot(
                mixed[i * row_count : (i + 1) * row_count],
                value_weight[:, head * VHEAD : (head + 1) * VHEAD],
                preferred_element_type=jnp.float32,
            ).astype(jnp.bfloat16)


def attention(queries, keys, key_index, own_index, own_position, value_weight):
    row_count, query_width = queries.shape
    local_heads = value_weight.shape[1] // VHEAD
    width = query_width // local_heads
    group = 4 if local_heads % 4 == 0 else 2
    key_count = keys.shape[1]
    tables = rope_tables(own_position, (width - LAT) // 2, 2 * (width - LAT))
    whole = lambda shape: pl.BlockSpec(shape, lambda i: (0,) * len(shape))
    deep = 2 * width - LAT
    return pl.pallas_call(
        functools.partial(attention_kernel, group),
        grid=(local_heads // group,),
        in_specs=[
            whole(tables.shape),
            whole((row_count, 1)),
            whole((row_count, 1)),
            whole((1, key_count)),
            whole(keys.shape),
            pl.BlockSpec((row_count, group * width), lambda i: (0, i)),
            pl.BlockSpec((LAT, group * VHEAD), lambda i: (0, i)),
        ],
        out_specs=pl.BlockSpec((row_count, group * VHEAD), lambda i: (0, i)),
        out_shape=jax.ShapeDtypeStruct((row_count, local_heads * VHEAD), jnp.bfloat16),
        scratch_shapes=[
            pltpu.VMEM((deep, key_count), jnp.bfloat16),
            pltpu.VMEM((deep, key_count), jnp.bfloat16),
            pltpu.VMEM((key_count, LAT), jnp.bfloat16),
            pltpu.VMEM((row_count, key_count), jnp.float32),
        ],
        compiler_params=pltpu.CompilerParams(vmem_limit_bytes=(6 + key_count // 64) * 1024 * 1024),
        cost_estimate=pl.CostEstimate(
            flops=2 * row_count * local_heads * (key_count * (deep + LAT) + LAT * VHEAD),
            bytes_accessed=2 * (queries.size + keys.size + value_weight.size),
            transcendentals=row_count * local_heads * key_count,
        ),
    )(
        tables,
        (own_index - own_position)[:, None],
        own_index[:, None],
        key_index[None, :],
        keys,
        queries,
        value_weight,
    )


def swap(value, axis_name, bit):
    width = lax.axis_size(axis_name)
    return lax.ppermute(value, axis_name, [(i, i ^ bit) for i in range(width)])


def pick(value, index):
    return lax.dynamic_index_in_dim(value, index, 0, keepdims=False)


def wide(value):
    return value.astype(jnp.float32)


def matmul(a, b):
    return jnp.dot(a, b, preferred_element_type=jnp.float32).astype(jnp.bfloat16)


def streamed_kernel(depth, rows, weight, out, held, total, sems):
    steps = weight.shape[0] // depth
    copies = [
        pltpu.make_async_copy(
            weight.at[pl.ds(i * depth, depth)], held.at[pl.ds(i * depth, depth)], sems.at[i]
        )
        for i in range(steps)
    ]
    for copy in copies:
        copy.start()
    block = 256
    for i, copy in enumerate(copies):
        copy.wait()
        part = rows[:, i * depth : (i + 1) * depth]
        for start in range(0, weight.shape[1], block):
            columns = slice(start, start + block)
            term = jnp.dot(
                part,
                held[i * depth : (i + 1) * depth, columns],
                preferred_element_type=jnp.float32,
            )
            if i > 0:
                term = term + total[:, columns]
            if i < steps - 1:
                total[:, columns] = term
            else:
                out[:, columns] = term.astype(out.dtype)


def streamed_matmul(rows, weight):
    steps = weight.shape[0] // 512
    return pl.pallas_call(
        functools.partial(streamed_kernel, 512),
        in_specs=[
            pl.BlockSpec(memory_space=pltpu.VMEM),
            pl.BlockSpec(memory_space=pl.ANY),
        ],
        out_specs=pl.BlockSpec(memory_space=pltpu.VMEM),
        out_shape=jax.ShapeDtypeStruct((rows.shape[0], weight.shape[1]), jnp.bfloat16),
        scratch_shapes=[
            pltpu.VMEM(weight.shape, weight.dtype),
            pltpu.VMEM((rows.shape[0], weight.shape[1]), jnp.float32),
            pltpu.SemaphoreType.DMA((steps,)),
        ],
        compiler_params=pltpu.CompilerParams(vmem_limit_bytes=50 * 1024 * 1024),
        cost_estimate=pl.CostEstimate(flops=1024, bytes_accessed=1024, transcendentals=0),
    )(rows, weight)


def after(value, earlier):
    return lax.optimization_barrier((value, earlier))[0]


def gather_keys(latent, n_ctx):
    rows = latent.shape[0] // 2
    core = lax.axis_index("tp") & 1
    half = lax.dynamic_slice_in_dim(latent, core * rows, rows, 0)
    came = [
        lax.ppermute(half, "ctx", [(c, c + d) for c in range(n_ctx - d)])
        for d in range(n_ctx - 1, 0, -1)
    ]
    mine = jnp.concatenate(came, axis=1)
    other = swap(mine, "tp", 1)
    before = jnp.concatenate(
        [jnp.where(core == 0, mine, other), jnp.where(core == 0, other, mine)], axis=0
    )
    return jnp.concatenate([before, latent], axis=1)


def spread_heads(heads_out, n_ctx, n_tp):
    c, t = lax.axis_index("ctx"), lax.axis_index("tp")
    quarters = heads_out.reshape(n_tp, heads_out.shape[0] // n_tp, heads_out.shape[1])
    groups = jnp.stack(
        [pick(quarters, t)] + [swap(pick(quarters, t ^ m), "tp", m) for m in range(1, n_tp)]
    )
    return jnp.stack(
        [pick(groups, t ^ c)] + [swap(pick(groups, t ^ c ^ j), "ctx", j) for j in range(1, n_ctx)]
    )


def core_rows(mine, other):
    first = lax.axis_index("tp") & 1 == 0
    both = jnp.stack([jnp.where(first, mine, other), jnp.where(first, other, mine)], axis=1)
    return both.reshape(-1, mine.shape[-1])


def paired_tail(
    heads_out, residual, output_weight, norm_gain, gate_weight, up_weight, down_weight, n_ctx, n_tp
):
    row_count, width = residual.shape
    half = row_count // 2
    model_width = width * n_tp
    t = lax.axis_index("tp")
    core = t & 1
    first_half = t >> 1
    own = spread_heads(heads_out, n_ctx, n_tp)
    near = swap(own, "tp", 1)
    far = swap(own, "tp", 2)
    residual_halves = residual.reshape(2, half, width)

    def first_hop(rows):
        blocks = streamed_matmul(rows, output_weight).reshape(2, 2, half, width)
        sent = blocks[:, 1]
        return blocks[:, 0], sent, swap(sent, "ctx", 1)

    def second_hop(kept, came):
        other = (wide(kept[1]) + wide(came[1])).astype(jnp.bfloat16)
        return wide(kept[0]) + wide(came[0]), other, swap(other, "ctx", 2)

    def attend(mine, came, which):
        return (wide(pick(residual_halves, which)) + mine + wide(came)).astype(jnp.bfloat16)

    def scale(rows):
        values = wide(rows)
        scaled = (values * norm_gain[None, :]).astype(jnp.bfloat16)
        return jnp.sum(values * values, axis=1), scaled

    def gate_up(rows):
        squares, scaled = scale(rows)
        terms = [matmul(scaled, gate_weight), matmul(scaled, up_weight)]

        def side(which):
            return jnp.concatenate(
                [lax.dynamic_slice_in_dim(term, which * half, half, 0) for term in terms], axis=0
            )

        return side(core), side(1 - core), squares

    def chip_sum(kept, sent):
        return wide(kept) + wide(swap(sent, "tp", 1))

    kept_a, sent_a, came_a = first_hop(core_rows(own, near))
    far = after(far, sent_a)
    far_near = swap(far, "tp", 1)
    mine_a, other_a, last_a = second_hop(kept_a, came_a)
    kept_b, sent_b, came_b = first_hop(core_rows(far, after(far_near, other_a)))
    attended_a = attend(mine_a, after(last_a, sent_b), first_half)
    twin_a = swap(attended_a, "ctx", 2)
    pair_a = jnp.concatenate([attended_a, twin_a], axis=0)
    rest_a = swap(pair_a, "ctx", 1)
    mine_b, other_b, last_b = second_hop(kept_b, after(came_b, pair_a))
    rest_a, last_b = lax.optimization_barrier((rest_a, last_b))
    attended_b = attend(mine_b, last_b, 1 - first_half)
    twin_b = swap(attended_b, "ctx", 2)
    all_a = jnp.concatenate([pair_a, rest_a], axis=0)
    squares_a, scaled = scale(all_a)

    def cross(rows, weight):
        term = matmul(rows, weight).reshape(2, 2, half, -1)

        def side(which):
            return lax.dynamic_index_in_dim(term, which, 1, keepdims=False).reshape(2 * half, -1)

        sent = side(1 - core)
        total = chip_sum(side(core), sent).astype(jnp.bfloat16)
        return sent, total, swap(total, "tp", 2)

    sent_gate, _, across_gate = cross(scaled, gate_weight)
    _, sums_up, across_up = cross(after(scaled, sent_gate), up_weight)
    across_squares = swap(squares_a + swap(squares_a, "tp", 1), "tp", 2)
    pair_b = jnp.concatenate([attended_b, after(twin_b, across_gate)], axis=0)
    rest_b = swap(pair_b, "ctx", 1)

    def hide(chip_terms, squares, across_gate, across_up, across_squares):
        squares = squares + swap(squares, "tp", 1) + across_squares
        squares = lax.dynamic_slice_in_dim(squares, core * half, half, 0)
        inverse_rms = lax.rsqrt(squares / model_width + norm_eps)[:, None]
        gate = (chip_terms[:half] + wide(across_gate)) * inverse_rms
        up = (chip_terms[half:] + wide(across_up)) * inverse_rms
        return (jax.nn.silu(gate) * up).astype(jnp.bfloat16)

    kept, sent, squares_p = gate_up(after(pair_b, sums_up))
    terms_p = chip_sum(kept, sent)
    rest_b, across_up, _ = lax.optimization_barrier((rest_b, across_up, sent))
    kept, sent, squares_q = gate_up(rest_b)
    terms_q = chip_sum(kept, sent)
    parts = [
        hide(
            terms,
            squares,
            across_gate[i * half : (i + 1) * half],
            across_up[i * half : (i + 1) * half],
            across_squares[2 * i * half : 2 * (i + 1) * half],
        )
        for i, (terms, squares) in enumerate(((terms_p, squares_p), (terms_q, squares_q)))
    ]
    hidden = jnp.concatenate(parts, axis=0)
    hidden_near = swap(hidden, "tp", 1)
    hidden_far = swap(hidden, "tp", 2)

    def down_hop(mine, other):
        blocks = streamed_matmul(jnp.concatenate([mine, other], axis=0), down_weight)
        blocks = blocks.reshape(2, 2, half, width)
        return blocks[:, 0], swap(blocks[:, 1], "ctx", 1)

    def down_second(kept, came):
        pair = wide(kept) + wide(came)
        other = pick(pair, 1 - core).astype(jnp.bfloat16)
        return pick(pair, core), other, swap(other, "ctx", 2)

    def in_order(a, b):
        first = first_half == 0
        return jnp.concatenate([jnp.where(first, a, b), jnp.where(first, b, a)], axis=0)

    attended = in_order(attended_a, attended_b)
    kept_b, came_b = down_hop(hidden, hidden_near)
    hidden_far = after(hidden_far, (kept_b, attended))
    hidden_far_near = swap(hidden_far, "tp", 1)
    down_b, other_b, last_b = down_second(kept_b, after(came_b, hidden_far))
    down_a, _, last_a = down_second(*down_hop(hidden_far, after(hidden_far_near, other_b)))
    out_b = (wide(attended_b) + down_b + wide(last_b)).astype(jnp.bfloat16)
    out_a = (wide(attended_a) + down_a + wide(last_a)).astype(jnp.bfloat16)

    return attended, in_order(out_a, out_b)


def on_device(
    residual,
    latent,
    queries,
    lengths,
    value_weight,
    output_weight,
    norm_gain,
    gate_weight,
    up_weight,
    down_weight,
):
    row_count = residual.shape[0]
    ctx_place = lax.axis_index("ctx")
    n_ctx, n_tp = lax.axis_size("ctx"), lax.axis_size("tp")
    paired = (
        n_ctx == 4
        and n_tp == 4
        and row_count % 64 == 0
        and residual.shape[1] % 256 == 0
        and output_weight.shape[0] % 512 == 0
        and down_weight.shape[0] % 512 == 0
    )
    own_index = ctx_place * row_count + jnp.arange(row_count, dtype=jnp.int32)
    _, own_position = trace_info(own_index, lengths)
    key_order = jnp.arange(n_ctx * row_count, dtype=jnp.int32)
    if paired:
        key_index = key_order + (ctx_place - (n_ctx - 1)) * row_count
        _, key_position = trace_info(key_index, lengths)
        keys = rope_keys(gather_keys(latent, n_ctx), key_position, LAT)
    else:
        rotated_keys = rope_keys(latent, own_position, LAT)
        keys = lax.all_gather(rotated_keys, "ctx", axis=1, tiled=True)
        key_index = key_order
    heads_out = attention(queries, keys, key_index, own_index, own_position, value_weight)
    if paired:
        return paired_tail(
            heads_out,
            residual,
            output_weight,
            norm_gain,
            gate_weight,
            up_weight,
            down_weight,
            n_ctx,
            n_tp,
        )
    all_heads = lax.all_gather(heads_out, "tp", axis=1, tiled=True)
    head_block = lax.all_to_all(all_heads, "ctx", split_axis=1, concat_axis=0, tiled=True)
    head_sum = lax.psum_scatter(
        jnp.dot(head_block, output_weight, preferred_element_type=jnp.float32).astype(jnp.bfloat16),
        "ctx",
        scatter_dimension=0,
        tiled=True,
    ).astype(jnp.float32)
    attended = (residual.astype(jnp.float32) + head_sum).astype(jnp.bfloat16)
    attended_float = attended.astype(jnp.float32)
    squares = lax.psum(jnp.sum(attended_float * attended_float, axis=1), "tp")
    inverse_rms = lax.rsqrt(squares / D + norm_eps)
    scaled = (attended_float * inverse_rms[:, None] * norm_gain[None, :]).astype(jnp.bfloat16)
    scaled_all = lax.all_gather(scaled, "ctx", axis=0, tiled=True)
    unit_count = gate_weight.shape[1]
    gate_up = jnp.concatenate([gate_weight, up_weight], axis=1)
    summed = lax.psum_scatter(
        jnp.dot(scaled_all, gate_up, preferred_element_type=jnp.float32).astype(jnp.bfloat16),
        "tp",
        scatter_dimension=0,
        tiled=True,
    ).astype(jnp.float32)
    hidden_share = (jax.nn.silu(summed[:, :unit_count]) * summed[:, unit_count:]).astype(
        jnp.bfloat16
    )
    hidden_all = lax.all_gather(hidden_share, "tp", axis=0, tiled=True)
    down_sum = lax.psum_scatter(
        jnp.dot(hidden_all, down_weight, preferred_element_type=jnp.float32).astype(jnp.bfloat16),
        "ctx",
        scatter_dimension=0,
        tiled=True,
    ).astype(jnp.float32)
    layer_out = (attended_float + down_sum).astype(jnp.bfloat16)
    return (attended, layer_out)


def solution(mesh):
    in_specs = (
        P(("grp", "ctx"), "tp"),
        P(None, ("grp", "ctx")),
        P(("grp", "ctx"), "tp"),
        P("grp"),
        P(None, "tp"),
        P("ctx", "tp"),
        P("tp"),
        P("tp", "ctx"),
        P("tp", "ctx"),
        P("ctx", "tp"),
    )
    out_specs = (P(("grp", "ctx"), "tp"), P(("grp", "ctx"), "tp"))
    return jax.shard_map(
        on_device, mesh=mesh, in_specs=in_specs, out_specs=out_specs, check_vma=False
    )
```

```python
import functools

import jax
import jax.numpy as jnp
from jax import lax
from jax.experimental import pallas as pl
from jax.experimental.pallas import tpu as pltpu
from jax.sharding import PartitionSpec as P

D = 7168
LAT = 512
ROPE = 64
VHEAD = 128


score_scale = 192.0 ** (-0.5)
rope_base = 10000.0
norm_eps = 1e-06
masked_score = -1e30


def rope_freqs(half_width):
    return rope_base ** (-jnp.arange(half_width, dtype=jnp.float32) / half_width)


def trace_info(token_index, lengths):
    trace_ends = jnp.cumsum(lengths)
    starts = trace_ends - lengths
    trace_ids = jnp.sum((token_index[:, None] >= trace_ends[None, :]).astype(jnp.int32), axis=1)
    member = trace_ids[:, None] == jnp.arange(lengths.shape[0], dtype=jnp.int32)[None, :]
    pos_shift = jnp.sum(jnp.where(member, (0 - starts)[None, :], 0), axis=1)
    return (trace_ids, token_index + pos_shift)


def rope_keys(latent, positions, latent_width):
    values = latent.astype(jnp.float32)
    half_width = (values.shape[0] - latent_width) // 2
    angles = rope_freqs(half_width)[:, None] * positions.astype(jnp.float32)[None, :]
    first_half = values[latent_width : latent_width + half_width]
    second_half = values[latent_width + half_width :]
    cosine = jnp.cos(angles)
    sine_value = jnp.sin(angles)
    return jnp.concatenate(
        [
            values[:latent_width],
            first_half * cosine - second_half * sine_value,
            first_half * sine_value + second_half * cosine,
        ],
        axis=0,
    ).astype(jnp.bfloat16)


def rope_tables(positions, half_width, lanes):
    angles = positions.astype(jnp.float32)[:, None] * rope_freqs(half_width)[None, :]
    cosine, sine_value = jnp.cos(angles), jnp.sin(angles)
    cos_part = jnp.concatenate([cosine, cosine], axis=1)
    sin_part = jnp.concatenate([-sine_value, sine_value], axis=1)
    rest = lanes - 2 * half_width
    ones = jnp.ones((angles.shape[0], rest), jnp.float32)
    zeros = jnp.zeros((angles.shape[0], rest), jnp.float32)
    return jnp.stack(
        [
            jnp.concatenate([cos_part, ones], axis=1),
            jnp.concatenate([sin_part, zeros], axis=1),
            jnp.concatenate([ones, cos_part], axis=1),
            jnp.concatenate([zeros, sin_part], axis=1),
        ]
    )


def attention_kernel(
    group, tables, starts, own_index, key_index, keys, queries, value_weight, out, even, odd, values, bias
):
    row_count = queries.shape[0]
    width = queries.shape[1] // group
    half_width = (width - LAT) // 2
    lanes = 2 * (width - LAT)

    @pl.when(pl.program_id(0) == 0)
    def prepare():
        all_keys = keys[...]
        pad = jnp.zeros((width - LAT, all_keys.shape[1]), jnp.bfloat16)
        even[:width] = all_keys
        even[width:] = pad
        odd[: width - LAT] = pad
        odd[width - LAT :] = all_keys
        values[...] = keys[:LAT].astype(jnp.float32).T.astype(jnp.bfloat16)
        allowed = (key_index[...] >= starts[...]) & (key_index[...] <= own_index[...])
        bias[...] = jnp.where(allowed, 0.0, masked_score)

    lane = lax.broadcasted_iota(jnp.int32, (row_count, lanes), 1)
    low = (lane & (2 * half_width - 1)) < half_width

    def turned(start, which):
        entry = queries[:, start : start + lanes].astype(jnp.float32)
        partner = jnp.where(
            low, pltpu.roll(entry, lanes - half_width, 1), pltpu.roll(entry, half_width, 1)
        )
        return (entry * tables[2 * which] + partner * tables[2 * which + 1]).astype(jnp.bfloat16)

    for which, key_rows in ((0, even), (1, odd)):
        rows = []
        for head in range(which, group, 2):
            base = (head - which) * width
            if which == 0:
                rows.append(
                    jnp.concatenate([queries[:, base : base + LAT], turned(base + LAT, 0)], axis=1)
                )
            else:
                first = base + LAT
                rows.append(
                    jnp.concatenate(
                        [queries[:, first : first + LAT], turned(first + LAT, 1)], axis=1
                    )
                )
        stacked = jnp.concatenate(rows, axis=0)
        scores = jnp.dot(stacked, key_rows[...], preferred_element_type=jnp.float32)
        scores = scores.reshape(len(rows), row_count, -1) + bias[...][None]
        top = jnp.max(scores, axis=2, keepdims=True)
        exponent = jnp.exp((scores - top) * score_scale)
        total = jnp.sum(exponent, axis=2, keepdims=True).reshape(len(rows) * row_count, 1)
        weights = exponent.astype(jnp.bfloat16).reshape(len(rows) * row_count, -1)
        mixed = jnp.dot(weights, values[...], preferred_element_type=jnp.float32)
        mixed = (mixed / total).astype(jnp.bfloat16)
        for i in range(len(rows)):
            head = 2 * i + which
            out[:, head * VHEAD : (head + 1) * VHEAD] = jnp.dot(
                mixed[i * row_count : (i + 1) * row_count],
                value_weight[:, head * VHEAD : (head + 1) * VHEAD],
                preferred_element_type=jnp.float32,
            ).astype(jnp.bfloat16)


def attention(queries, keys, key_index, own_index, own_position, value_weight):
    row_count, query_width = queries.shape
    local_heads = value_weight.shape[1] // VHEAD
    width = query_width // local_heads
    group = 4 if local_heads % 4 == 0 else 2
    key_count = keys.shape[1]
    tables = rope_tables(own_position, (width - LAT) // 2, 2 * (width - LAT))
    whole = lambda shape: pl.BlockSpec(shape, lambda i: (0,) * len(shape))
    deep = 2 * width - LAT
    return pl.pallas_call(
        functools.partial(attention_kernel, group),
        grid=(local_heads // group,),
        in_specs=[
            whole(tables.shape),
            whole((row_count, 1)),
            whole((row_count, 1)),
            whole((1, key_count)),
            whole(keys.shape),
            pl.BlockSpec((row_count, group * width), lambda i: (0, i)),
            pl.BlockSpec((LAT, group * VHEAD), lambda i: (0, i)),
        ],
        out_specs=pl.BlockSpec((row_count, group * VHEAD), lambda i: (0, i)),
        out_shape=jax.ShapeDtypeStruct((row_count, local_heads * VHEAD), jnp.bfloat16),
        scratch_shapes=[
            pltpu.VMEM((deep, key_count), jnp.bfloat16),
            pltpu.VMEM((deep, key_count), jnp.bfloat16),
            pltpu.VMEM((key_count, LAT), jnp.bfloat16),
            pltpu.VMEM((row_count, key_count), jnp.float32),
        ],
        compiler_params=pltpu.CompilerParams(vmem_limit_bytes=(6 + key_count // 64) * 1024 * 1024),
        cost_estimate=pl.CostEstimate(
            flops=2 * row_count * local_heads * (key_count * (deep + LAT) + LAT * VHEAD),
            bytes_accessed=2 * (queries.size + keys.size + value_weight.size),
            transcendentals=row_count * local_heads * key_count,
        ),
    )(
        tables,
        (own_index - own_position)[:, None],
        own_index[:, None],
        key_index[None, :],
        keys,
        queries,
        value_weight,
    )


def swap(value, axis_name, bit):
    width = lax.axis_size(axis_name)
    return lax.ppermute(value, axis_name, [(i, i ^ bit) for i in range(width)])


def pick(value, index):
    return lax.dynamic_index_in_dim(value, index, 0, keepdims=False)


def wide(value):
    return value.astype(jnp.float32)


def matmul(a, b):
    return jnp.dot(a, b, preferred_element_type=jnp.float32).astype(jnp.bfloat16)


def streamed_kernel(depth, rows, weight, out, held, total, sems):
    steps = weight.shape[0] // depth
    copies = [
        pltpu.make_async_copy(
            weight.at[pl.ds(i * depth, depth)], held.at[pl.ds(i * depth, depth)], sems.at[i]
        )
        for i in range(steps)
    ]
    for copy in copies:
        copy.start()
    block = 256
    for i, copy in enumerate(copies):
        copy.wait()
        part = rows[:, i * depth : (i + 1) * depth]
        for start in range(0, weight.shape[1], block):
            columns = slice(start, start + block)
            term = jnp.dot(
                part,
                held[i * depth : (i + 1) * depth, columns],
                preferred_element_type=jnp.float32,
            )
            if i > 0:
                term = term + total[:, columns]
            if i < steps - 1:
                total[:, columns] = term
            else:
                out[:, columns] = term.astype(out.dtype)


def streamed_matmul(rows, weight):
    steps = weight.shape[0] // 512
    return pl.pallas_call(
        functools.partial(streamed_kernel, 512),
        in_specs=[
            pl.BlockSpec(memory_space=pltpu.VMEM),
            pl.BlockSpec(memory_space=pl.ANY),
        ],
        out_specs=pl.BlockSpec(memory_space=pltpu.VMEM),
        out_shape=jax.ShapeDtypeStruct((rows.shape[0], weight.shape[1]), jnp.bfloat16),
        scratch_shapes=[
            pltpu.VMEM(weight.shape, weight.dtype),
            pltpu.VMEM((rows.shape[0], weight.shape[1]), jnp.float32),
            pltpu.SemaphoreType.DMA((steps,)),
        ],
        compiler_params=pltpu.CompilerParams(vmem_limit_bytes=50 * 1024 * 1024),
        cost_estimate=pl.CostEstimate(flops=1024, bytes_accessed=1024, transcendentals=0),
    )(rows, weight)


def load_kernel(chunks, weight, out, sems):
    rows = weight.shape[0] // chunks
    copies = [
        pltpu.make_async_copy(
            weight.at[pl.ds(i * rows, rows)], out.at[pl.ds(i * rows, rows)], sems.at[i]
        )
        for i in range(chunks)
    ]
    for copy in copies:
        copy.start()
    for copy in copies:
        copy.wait()


def load(weight, grant):
    chunks = 8
    return pl.pallas_call(
        functools.partial(load_kernel, chunks),
        in_specs=[pl.BlockSpec(memory_space=pl.ANY)],
        out_specs=pl.BlockSpec(memory_space=pltpu.VMEM),
        out_shape=pltpu.VMEM(weight.shape, weight.dtype),
        scratch_shapes=[pltpu.SemaphoreType.DMA((chunks,))],
        compiler_params=pltpu.CompilerParams(vmem_limit_bytes=grant * 1024 * 1024),
        cost_estimate=pl.CostEstimate(flops=0, bytes_accessed=1024, transcendentals=0),
    )(weight)


def after(value, earlier):
    return lax.optimization_barrier((value, earlier))[0]


def gather_keys(latent, n_ctx):
    rows = latent.shape[0] // 2
    core = lax.axis_index("tp") & 1
    half = lax.dynamic_slice_in_dim(latent, core * rows, rows, 0)
    came = [
        lax.ppermute(half, "ctx", [(c, c + d) for c in range(n_ctx - d)])
        for d in range(n_ctx - 1, 0, -1)
    ]
    mine = jnp.concatenate(came, axis=1)
    other = swap(mine, "tp", 1)
    before = jnp.concatenate(
        [jnp.where(core == 0, mine, other), jnp.where(core == 0, other, mine)], axis=0
    )
    return jnp.concatenate([before, latent], axis=1)


def spread_heads(heads_out, n_ctx, n_tp):
    c, t = lax.axis_index("ctx"), lax.axis_index("tp")
    quarters = heads_out.reshape(n_tp, heads_out.shape[0] // n_tp, heads_out.shape[1])
    groups = jnp.stack(
        [pick(quarters, t)] + [swap(pick(quarters, t ^ m), "tp", m) for m in range(1, n_tp)]
    )
    return jnp.stack(
        [pick(groups, t ^ c)] + [swap(pick(groups, t ^ c ^ j), "ctx", j) for j in range(1, n_ctx)]
    )


def core_rows(mine, other):
    first = lax.axis_index("tp") & 1 == 0
    both = jnp.stack([jnp.where(first, mine, other), jnp.where(first, other, mine)], axis=1)
    return both.reshape(-1, mine.shape[-1])


def paired_tail(
    heads_out, residual, output_weight, norm_gain, gate_weight, up_weight, down_weight, n_ctx, n_tp
):
    row_count, width = residual.shape
    half = row_count // 2
    model_width = width * n_tp
    t = lax.axis_index("tp")
    core = t & 1
    first_half = t >> 1
    own = spread_heads(heads_out, n_ctx, n_tp)
    near = swap(own, "tp", 1)
    far = swap(own, "tp", 2)
    residual_halves = residual.reshape(2, half, width)

    def first_hop(rows):
        blocks = streamed_matmul(rows, output_weight).reshape(2, 2, half, width)
        sent = blocks[:, 1]
        return blocks[:, 0], sent, swap(sent, "ctx", 1)

    def second_hop(kept, came):
        other = (wide(kept[1]) + wide(came[1])).astype(jnp.bfloat16)
        return wide(kept[0]) + wide(came[0]), other, swap(other, "ctx", 2)

    def attend(mine, came, which):
        return (wide(pick(residual_halves, which)) + mine + wide(came)).astype(jnp.bfloat16)

    def scale(rows):
        values = wide(rows)
        scaled = (values * norm_gain[None, :]).astype(jnp.bfloat16)
        return jnp.sum(values * values, axis=1), scaled

    def gate_up(rows):
        squares, scaled = scale(rows)
        terms = [matmul(scaled, gate_weight), matmul(scaled, up_weight)]

        def side(which):
            return jnp.concatenate(
                [lax.dynamic_slice_in_dim(term, which * half, half, 0) for term in terms], axis=0
            )

        return side(core), side(1 - core), squares

    def chip_sum(kept, sent):
        return wide(kept) + wide(swap(sent, "tp", 1))

    kept_a, sent_a, came_a = first_hop(core_rows(own, near))
    far = after(far, sent_a)
    far_near = swap(far, "tp", 1)
    mine_a, other_a, last_a = second_hop(kept_a, came_a)
    kept_b, sent_b, came_b = first_hop(core_rows(far, after(far_near, other_a)))
    attended_a = attend(mine_a, after(last_a, sent_b), first_half)
    twin_a = swap(attended_a, "ctx", 2)
    gate_weight = load(after(gate_weight, attended_a), 44)
    twin_a, came_b, gate_weight = lax.optimization_barrier((twin_a, came_b, gate_weight))
    pair_a = jnp.concatenate([attended_a, twin_a], axis=0)
    rest_a = swap(pair_a, "ctx", 1)
    mine_b, other_b, last_b = second_hop(kept_b, after(came_b, pair_a))
    rest_a, last_b = lax.optimization_barrier((rest_a, last_b))
    attended_b = attend(mine_b, last_b, 1 - first_half)
    twin_b = swap(attended_b, "ctx", 2)
    all_a = jnp.concatenate([pair_a, rest_a], axis=0)
    squares_a, scaled = scale(all_a)

    def cross(rows, weight, earlier):
        term = matmul(rows, weight).reshape(2, 2, half, -1)

        def side(which):
            return lax.dynamic_index_in_dim(term, which, 1, keepdims=False).reshape(2 * half, -1)

        came = swap(side(1 - core), "tp", 1)
        if earlier is not None:
            came = after(came, earlier)
        total = (wide(side(core)) + wide(came)).astype(jnp.bfloat16)
        return total, swap(total, "tp", 2)

    sums_gate, across_gate = cross(scaled, gate_weight, None)
    sums_up, across_up = cross(after(scaled, sums_gate), up_weight, across_gate)
    across_squares = swap(squares_a + swap(squares_a, "tp", 1), "tp", 2)
    pair_b = jnp.concatenate([attended_b, after(twin_b, across_gate)], axis=0)
    rest_b = swap(pair_b, "ctx", 1)

    def hide(chip_terms, squares, across_gate, across_up, across_squares):
        squares = squares + swap(squares, "tp", 1) + across_squares
        squares = lax.dynamic_slice_in_dim(squares, core * half, half, 0)
        inverse_rms = lax.rsqrt(squares / model_width + norm_eps)[:, None]
        gate = (chip_terms[:half] + wide(across_gate)) * inverse_rms
        up = (chip_terms[half:] + wide(across_up)) * inverse_rms
        return (jax.nn.silu(gate) * up).astype(jnp.bfloat16)

    kept, sent, squares_p = gate_up(after(pair_b, sums_up))
    terms_p = chip_sum(kept, sent)
    down_loaded = load(after(down_weight, sent), 24)
    rest_b, across_up, down_loaded = lax.optimization_barrier((rest_b, across_up, down_loaded))
    kept, sent, squares_q = gate_up(rest_b)
    terms_q = chip_sum(kept, sent)
    parts = [
        hide(
            terms,
            squares,
            across_gate[i * half : (i + 1) * half],
            across_up[i * half : (i + 1) * half],
            across_squares[2 * i * half : 2 * (i + 1) * half],
        )
        for i, (terms, squares) in enumerate(((terms_p, squares_p), (terms_q, squares_q)))
    ]
    hidden = jnp.concatenate(parts, axis=0)
    hidden_near = swap(hidden, "tp", 1)
    hidden_far = swap(hidden, "tp", 2)

    def down_hop(mine, other, product, weight):
        blocks = product(jnp.concatenate([mine, other], axis=0), weight)
        blocks = blocks.reshape(2, 2, half, width)
        return blocks[:, 0], swap(blocks[:, 1], "ctx", 1)

    def down_second(kept, came):
        pair = wide(kept) + wide(came)
        other = pick(pair, 1 - core).astype(jnp.bfloat16)
        return pick(pair, core), other, swap(other, "ctx", 2)

    def in_order(a, b):
        first = first_half == 0
        return jnp.concatenate([jnp.where(first, a, b), jnp.where(first, b, a)], axis=0)

    attended = in_order(attended_a, attended_b)
    kept_b, came_b = down_hop(hidden, hidden_near, matmul, down_loaded)
    hidden_far = after(hidden_far, (kept_b, attended))
    hidden_far_near = swap(hidden_far, "tp", 1)
    down_b, other_b, last_b = down_second(kept_b, after(came_b, hidden_far))
    down_a, _, last_a = down_second(
        *down_hop(hidden_far, after(hidden_far_near, other_b), streamed_matmul, down_weight)
    )
    out_b = (wide(attended_b) + down_b + wide(last_b)).astype(jnp.bfloat16)
    out_a = (wide(attended_a) + down_a + wide(last_a)).astype(jnp.bfloat16)

    return attended, in_order(out_a, out_b)


def on_device(
    residual,
    latent,
    queries,
    lengths,
    value_weight,
    output_weight,
    norm_gain,
    gate_weight,
    up_weight,
    down_weight,
):
    row_count = residual.shape[0]
    ctx_place = lax.axis_index("ctx")
    n_ctx, n_tp = lax.axis_size("ctx"), lax.axis_size("tp")
    paired = (
        n_ctx == 4
        and n_tp == 4
        and row_count % 64 == 0
        and residual.shape[1] % 256 == 0
        and output_weight.shape[0] % 512 == 0
        and down_weight.shape[0] % 512 == 0
    )
    own_index = ctx_place * row_count + jnp.arange(row_count, dtype=jnp.int32)
    _, own_position = trace_info(own_index, lengths)
    key_order = jnp.arange(n_ctx * row_count, dtype=jnp.int32)
    if paired:
        key_index = key_order + (ctx_place - (n_ctx - 1)) * row_count
        _, key_position = trace_info(key_index, lengths)
        keys = rope_keys(gather_keys(latent, n_ctx), key_position, LAT)
    else:
        rotated_keys = rope_keys(latent, own_position, LAT)
        keys = lax.all_gather(rotated_keys, "ctx", axis=1, tiled=True)
        key_index = key_order
    heads_out = attention(queries, keys, key_index, own_index, own_position, value_weight)
    if paired:
        return paired_tail(
            heads_out,
            residual,
            output_weight,
            norm_gain,
            gate_weight,
            up_weight,
            down_weight,
            n_ctx,
            n_tp,
        )
    all_heads = lax.all_gather(heads_out, "tp", axis=1, tiled=True)
    head_block = lax.all_to_all(all_heads, "ctx", split_axis=1, concat_axis=0, tiled=True)
    head_sum = lax.psum_scatter(
        jnp.dot(head_block, output_weight, preferred_element_type=jnp.float32).astype(jnp.bfloat16),
        "ctx",
        scatter_dimension=0,
        tiled=True,
    ).astype(jnp.float32)
    attended = (residual.astype(jnp.float32) + head_sum).astype(jnp.bfloat16)
    attended_float = attended.astype(jnp.float32)
    squares = lax.psum(jnp.sum(attended_float * attended_float, axis=1), "tp")
    inverse_rms = lax.rsqrt(squares / D + norm_eps)
    scaled = (attended_float * inverse_rms[:, None] * norm_gain[None, :]).astype(jnp.bfloat16)
    scaled_all = lax.all_gather(scaled, "ctx", axis=0, tiled=True)
    unit_count = gate_weight.shape[1]
    gate_up = jnp.concatenate([gate_weight, up_weight], axis=1)
    summed = lax.psum_scatter(
        jnp.dot(scaled_all, gate_up, preferred_element_type=jnp.float32).astype(jnp.bfloat16),
        "tp",
        scatter_dimension=0,
        tiled=True,
    ).astype(jnp.float32)
    hidden_share = (jax.nn.silu(summed[:, :unit_count]) * summed[:, unit_count:]).astype(
        jnp.bfloat16
    )
    hidden_all = lax.all_gather(hidden_share, "tp", axis=0, tiled=True)
    down_sum = lax.psum_scatter(
        jnp.dot(hidden_all, down_weight, preferred_element_type=jnp.float32).astype(jnp.bfloat16),
        "ctx",
        scatter_dimension=0,
        tiled=True,
    ).astype(jnp.float32)
    layer_out = (attended_float + down_sum).astype(jnp.bfloat16)
    return (attended, layer_out)


def solution(mesh):
    in_specs = (
        P(("grp", "ctx"), "tp"),
        P(None, ("grp", "ctx")),
        P(("grp", "ctx"), "tp"),
        P("grp"),
        P(None, "tp"),
        P("ctx", "tp"),
        P("tp"),
        P("tp", "ctx"),
        P("tp", "ctx"),
        P("ctx", "tp"),
    )
    out_specs = (P(("grp", "ctx"), "tp"), P(("grp", "ctx"), "tp"))
    return jax.shard_map(
        on_device, mesh=mesh, in_specs=in_specs, out_specs=out_specs, check_vma=False
    )
```

```python
import functools

import jax
import jax.numpy as jnp
from jax import lax
from jax.experimental import pallas as pl
from jax.experimental.pallas import tpu as pltpu
from jax.sharding import PartitionSpec as P

D = 7168
LAT = 512
ROPE = 64
VHEAD = 128


score_scale = 192.0 ** (-0.5)
rope_base = 10000.0
norm_eps = 1e-06
masked_score = -1e30


def rope_freqs(half_width):
    return rope_base ** (-jnp.arange(half_width, dtype=jnp.float32) / half_width)


def trace_info(token_index, lengths):
    trace_ends = jnp.cumsum(lengths)
    starts = trace_ends - lengths
    trace_ids = jnp.sum((token_index[:, None] >= trace_ends[None, :]).astype(jnp.int32), axis=1)
    member = trace_ids[:, None] == jnp.arange(lengths.shape[0], dtype=jnp.int32)[None, :]
    pos_shift = jnp.sum(jnp.where(member, (0 - starts)[None, :], 0), axis=1)
    return (trace_ids, token_index + pos_shift)


def rope_keys(latent, positions, latent_width):
    values = latent.astype(jnp.float32)
    half_width = (values.shape[0] - latent_width) // 2
    angles = rope_freqs(half_width)[:, None] * positions.astype(jnp.float32)[None, :]
    first_half = values[latent_width : latent_width + half_width]
    second_half = values[latent_width + half_width :]
    cosine = jnp.cos(angles)
    sine_value = jnp.sin(angles)
    return jnp.concatenate(
        [
            values[:latent_width],
            first_half * cosine - second_half * sine_value,
            first_half * sine_value + second_half * cosine,
        ],
        axis=0,
    ).astype(jnp.bfloat16)


def rope_tables(positions, half_width, lanes):
    angles = positions.astype(jnp.float32)[:, None] * rope_freqs(half_width)[None, :]
    cosine, sine_value = jnp.cos(angles), jnp.sin(angles)
    cos_part = jnp.concatenate([cosine, cosine], axis=1)
    sin_part = jnp.concatenate([-sine_value, sine_value], axis=1)
    rest = lanes - 2 * half_width
    ones = jnp.ones((angles.shape[0], rest), jnp.float32)
    zeros = jnp.zeros((angles.shape[0], rest), jnp.float32)
    return jnp.stack(
        [
            jnp.concatenate([cos_part, ones], axis=1),
            jnp.concatenate([sin_part, zeros], axis=1),
            jnp.concatenate([ones, cos_part], axis=1),
            jnp.concatenate([zeros, sin_part], axis=1),
        ]
    )


def attention_kernel(
    group, tables, starts, own_index, key_index, keys, queries, value_weight, out, even, odd, values, bias
):
    row_count = queries.shape[0]
    width = queries.shape[1] // group
    half_width = (width - LAT) // 2
    lanes = 2 * (width - LAT)

    @pl.when(pl.program_id(0) == 0)
    def prepare():
        all_keys = keys[...]
        pad = jnp.zeros((width - LAT, all_keys.shape[1]), jnp.bfloat16)
        even[:width] = all_keys
        even[width:] = pad
        odd[: width - LAT] = pad
        odd[width - LAT :] = all_keys
        values[...] = keys[:LAT].astype(jnp.float32).T.astype(jnp.bfloat16)
        allowed = (key_index[...] >= starts[...]) & (key_index[...] <= own_index[...])
        bias[...] = jnp.where(allowed, 0.0, masked_score)

    lane = lax.broadcasted_iota(jnp.int32, (row_count, lanes), 1)
    low = (lane & (2 * half_width - 1)) < half_width

    def turned(start, which):
        entry = queries[:, start : start + lanes].astype(jnp.float32)
        partner = jnp.where(
            low, pltpu.roll(entry, lanes - half_width, 1), pltpu.roll(entry, half_width, 1)
        )
        return (entry * tables[2 * which] + partner * tables[2 * which + 1]).astype(jnp.bfloat16)

    for which, key_rows in ((0, even), (1, odd)):
        rows = []
        for head in range(which, group, 2):
            base = (head - which) * width
            if which == 0:
                rows.append(
                    jnp.concatenate([queries[:, base : base + LAT], turned(base + LAT, 0)], axis=1)
                )
            else:
                first = base + LAT
                rows.append(
                    jnp.concatenate(
                        [queries[:, first : first + LAT], turned(first + LAT, 1)], axis=1
                    )
                )
        stacked = jnp.concatenate(rows, axis=0)
        scores = jnp.dot(stacked, key_rows[...], preferred_element_type=jnp.float32)
        scores = scores.reshape(len(rows), row_count, -1) + bias[...][None]
        top = jnp.max(scores, axis=2, keepdims=True)
        exponent = jnp.exp((scores - top) * score_scale)
        total = jnp.sum(exponent, axis=2, keepdims=True).reshape(len(rows) * row_count, 1)
        weights = exponent.astype(jnp.bfloat16).reshape(len(rows) * row_count, -1)
        mixed = jnp.dot(weights, values[...], preferred_element_type=jnp.float32)
        mixed = (mixed / total).astype(jnp.bfloat16)
        for i in range(len(rows)):
            head = 2 * i + which
            out[:, head * VHEAD : (head + 1) * VHEAD] = jnp.dot(
                mixed[i * row_count : (i + 1) * row_count],
                value_weight[:, head * VHEAD : (head + 1) * VHEAD],
                preferred_element_type=jnp.float32,
            ).astype(jnp.bfloat16)


def attention(queries, keys, key_index, own_index, own_position, value_weight):
    row_count, query_width = queries.shape
    local_heads = value_weight.shape[1] // VHEAD
    width = query_width // local_heads
    group = 4 if local_heads % 4 == 0 else 2
    key_count = keys.shape[1]
    tables = rope_tables(own_position, (width - LAT) // 2, 2 * (width - LAT))
    whole = lambda shape: pl.BlockSpec(shape, lambda i: (0,) * len(shape))
    deep = 2 * width - LAT
    return pl.pallas_call(
        functools.partial(attention_kernel, group),
        grid=(local_heads // group,),
        in_specs=[
            whole(tables.shape),
            whole((row_count, 1)),
            whole((row_count, 1)),
            whole((1, key_count)),
            whole(keys.shape),
            pl.BlockSpec((row_count, group * width), lambda i: (0, i)),
            pl.BlockSpec((LAT, group * VHEAD), lambda i: (0, i)),
        ],
        out_specs=pl.BlockSpec((row_count, group * VHEAD), lambda i: (0, i)),
        out_shape=jax.ShapeDtypeStruct((row_count, local_heads * VHEAD), jnp.bfloat16),
        scratch_shapes=[
            pltpu.VMEM((deep, key_count), jnp.bfloat16),
            pltpu.VMEM((deep, key_count), jnp.bfloat16),
            pltpu.VMEM((key_count, LAT), jnp.bfloat16),
            pltpu.VMEM((row_count, key_count), jnp.float32),
        ],
        compiler_params=pltpu.CompilerParams(vmem_limit_bytes=min(40 + key_count // 64, 56) * 1024 * 1024),
        cost_estimate=pl.CostEstimate(
            flops=2 * row_count * local_heads * (key_count * (deep + LAT) + LAT * VHEAD),
            bytes_accessed=2 * (queries.size + keys.size + value_weight.size),
            transcendentals=row_count * local_heads * key_count,
        ),
    )(
        tables,
        (own_index - own_position)[:, None],
        own_index[:, None],
        key_index[None, :],
        keys,
        queries,
        value_weight,
    )


def swap(value, axis_name, bit):
    width = lax.axis_size(axis_name)
    return lax.ppermute(value, axis_name, [(i, i ^ bit) for i in range(width)])


def pick(value, index):
    return lax.dynamic_index_in_dim(value, index, 0, keepdims=False)


def wide(value):
    return value.astype(jnp.float32)


def matmul(a, b):
    return jnp.dot(a, b, preferred_element_type=jnp.float32).astype(jnp.bfloat16)


def streamed_kernel(depth, rows, weight, out, held, total, sems):
    steps = weight.shape[0] // depth
    copies = [
        pltpu.make_async_copy(
            weight.at[pl.ds(i * depth, depth)], held.at[pl.ds(i * depth, depth)], sems.at[i]
        )
        for i in range(steps)
    ]
    for copy in copies:
        copy.start()
    block = 256
    for i, copy in enumerate(copies):
        copy.wait()
        part = rows[:, i * depth : (i + 1) * depth]
        for start in range(0, weight.shape[1], block):
            columns = slice(start, start + block)
            term = jnp.dot(
                part,
                held[i * depth : (i + 1) * depth, columns],
                preferred_element_type=jnp.float32,
            )
            if i > 0:
                term = term + total[:, columns]
            if i < steps - 1:
                total[:, columns] = term
            else:
                out[:, columns] = term.astype(out.dtype)


def streamed_matmul(rows, weight):
    depth = 512 if weight.shape[0] % 512 == 0 else 256
    steps = weight.shape[0] // depth
    return pl.pallas_call(
        functools.partial(streamed_kernel, depth),
        in_specs=[
            pl.BlockSpec(memory_space=pltpu.VMEM),
            pl.BlockSpec(memory_space=pl.ANY),
        ],
        out_specs=pl.BlockSpec(memory_space=pltpu.VMEM),
        out_shape=jax.ShapeDtypeStruct((rows.shape[0], weight.shape[1]), jnp.bfloat16),
        scratch_shapes=[
            pltpu.VMEM(weight.shape, weight.dtype),
            pltpu.VMEM((rows.shape[0], weight.shape[1]), jnp.float32),
            pltpu.SemaphoreType.DMA((steps,)),
        ],
        compiler_params=pltpu.CompilerParams(vmem_limit_bytes=50 * 1024 * 1024),
        cost_estimate=pl.CostEstimate(flops=1024, bytes_accessed=1024, transcendentals=0),
    )(rows, weight)


def load_kernel(chunks, weight, out, sems):
    rows = weight.shape[0] // chunks
    copies = [
        pltpu.make_async_copy(
            weight.at[pl.ds(i * rows, rows)], out.at[pl.ds(i * rows, rows)], sems.at[i]
        )
        for i in range(chunks)
    ]
    for copy in copies:
        copy.start()
    for copy in copies:
        copy.wait()


def load(weight, grant):
    chunks = 8
    return pl.pallas_call(
        functools.partial(load_kernel, chunks),
        in_specs=[pl.BlockSpec(memory_space=pl.ANY)],
        out_specs=pl.BlockSpec(memory_space=pltpu.VMEM),
        out_shape=pltpu.VMEM(weight.shape, weight.dtype),
        scratch_shapes=[pltpu.SemaphoreType.DMA((chunks,))],
        compiler_params=pltpu.CompilerParams(vmem_limit_bytes=grant * 1024 * 1024),
        cost_estimate=pl.CostEstimate(flops=0, bytes_accessed=1024, transcendentals=0),
    )(weight)


def after(value, earlier):
    return lax.optimization_barrier((value, earlier))[0]


def gather_keys(latent, n_ctx):
    rows = latent.shape[0] // 2
    core = lax.axis_index("tp") & 1
    half = lax.dynamic_slice_in_dim(latent, core * rows, rows, 0)
    came = [
        lax.ppermute(half, "ctx", [(c, c + d) for c in range(n_ctx - d)])
        for d in range(n_ctx - 1, 0, -1)
    ]
    mine = jnp.concatenate(came, axis=1)
    other = swap(mine, "tp", 1)
    before = jnp.concatenate(
        [jnp.where(core == 0, mine, other), jnp.where(core == 0, other, mine)], axis=0
    )
    return jnp.concatenate([before, latent], axis=1)


def spread_heads(heads_out, n_ctx, n_tp):
    c, t = lax.axis_index("ctx"), lax.axis_index("tp")
    quarters = heads_out.reshape(n_tp, heads_out.shape[0] // n_tp, heads_out.shape[1])
    groups = jnp.stack(
        [pick(quarters, t)] + [swap(pick(quarters, t ^ m), "tp", m) for m in range(1, n_tp)]
    )
    return jnp.stack(
        [pick(groups, t ^ c)] + [swap(pick(groups, t ^ c ^ j), "ctx", j) for j in range(1, n_ctx)]
    )


def core_rows(mine, other):
    first = lax.axis_index("tp") & 1 == 0
    both = jnp.stack([jnp.where(first, mine, other), jnp.where(first, other, mine)], axis=1)
    return both.reshape(-1, mine.shape[-1])


def paired_tail(
    heads_out, residual, output_weight, norm_gain, gate_weight, up_weight, down_weight, n_ctx, n_tp
):
    row_count, width = residual.shape
    half = row_count // 2
    model_width = width * n_tp
    t = lax.axis_index("tp")
    core = t & 1
    first_half = t >> 1
    own = spread_heads(heads_out, n_ctx, n_tp)
    near = swap(own, "tp", 1)
    far = swap(own, "tp", 2)
    residual_halves = residual.reshape(2, half, width)

    def first_hop(rows):
        blocks = streamed_matmul(rows, output_weight).reshape(2, 2, half, width)
        sent = blocks[:, 1]
        return blocks[:, 0], sent, swap(sent, "ctx", 1)

    def second_hop(kept, came):
        other = (wide(kept[1]) + wide(came[1])).astype(jnp.bfloat16)
        return wide(kept[0]) + wide(came[0]), other, swap(other, "ctx", 2)

    def attend(mine, came, which):
        return (wide(pick(residual_halves, which)) + mine + wide(came)).astype(jnp.bfloat16)

    def scale(rows):
        values = wide(rows)
        scaled = (values * norm_gain[None, :]).astype(jnp.bfloat16)
        return jnp.sum(values * values, axis=1), scaled

    def gate_up(rows):
        squares, scaled = scale(rows)
        terms = [matmul(scaled, gate_weight), matmul(scaled, up_weight)]

        def side(which):
            return jnp.concatenate(
                [lax.dynamic_slice_in_dim(term, which * half, half, 0) for term in terms], axis=0
            )

        return side(core), side(1 - core), squares

    def chip_sum(kept, sent):
        return wide(kept) + wide(swap(sent, "tp", 1))

    kept_a, sent_a, came_a = first_hop(core_rows(own, near))
    far = after(far, sent_a)
    far_near = swap(far, "tp", 1)
    mine_a, other_a, last_a = second_hop(kept_a, came_a)
    kept_b, sent_b, came_b = first_hop(core_rows(far, after(far_near, other_a)))
    attended_a = attend(mine_a, after(last_a, sent_b), first_half)
    twin_a = swap(attended_a, "ctx", 2)
    pair_a = jnp.concatenate([attended_a, twin_a], axis=0)
    rest_a = swap(pair_a, "ctx", 1)
    mine_b, other_b, last_b = second_hop(kept_b, after(came_b, pair_a))
    rest_a, last_b = lax.optimization_barrier((rest_a, last_b))
    attended_b = attend(mine_b, last_b, 1 - first_half)
    twin_b = swap(attended_b, "ctx", 2)
    all_a = jnp.concatenate([pair_a, rest_a], axis=0)
    squares_a, scaled = scale(all_a)

    def cross(rows, weight):
        term = matmul(rows, weight).reshape(2, 2, half, -1)

        def side(which):
            return lax.dynamic_index_in_dim(term, which, 1, keepdims=False).reshape(2 * half, -1)

        sent = side(1 - core)
        total = chip_sum(side(core), sent).astype(jnp.bfloat16)
        return sent, total, swap(total, "tp", 2)

    sent_gate, _, across_gate = cross(scaled, gate_weight)
    _, sums_up, across_up = cross(after(scaled, sent_gate), up_weight)
    squares_a = after(squares_a, sums_up)
    across_squares = swap(squares_a + swap(squares_a, "tp", 1), "tp", 2)
    pair_b = jnp.concatenate([attended_b, after(twin_b, across_gate)], axis=0)
    rest_b = swap(pair_b, "ctx", 1)

    def hide(chip_terms, squares, across_gate, across_up, across_squares):
        squares = squares + swap(squares, "tp", 1) + across_squares
        squares = lax.dynamic_slice_in_dim(squares, core * half, half, 0)
        inverse_rms = lax.rsqrt(squares / model_width + norm_eps)[:, None]
        gate = (chip_terms[:half] + wide(across_gate)) * inverse_rms
        up = (chip_terms[half:] + wide(across_up)) * inverse_rms
        return (jax.nn.silu(gate) * up).astype(jnp.bfloat16)

    kept, sent, squares_p = gate_up(after(pair_b, sums_up))
    terms_p = chip_sum(kept, sent)
    down_loaded = load(after(down_weight, sent), 24)
    rest_b, across_up, down_loaded = lax.optimization_barrier((rest_b, across_up, down_loaded))
    kept, sent, squares_q = gate_up(rest_b)
    terms_q = chip_sum(kept, sent)
    parts = [
        hide(
            terms,
            squares,
            across_gate[i * half : (i + 1) * half],
            across_up[i * half : (i + 1) * half],
            across_squares[2 * i * half : 2 * (i + 1) * half],
        )
        for i, (terms, squares) in enumerate(((terms_p, squares_p), (terms_q, squares_q)))
    ]
    hidden = jnp.concatenate(parts, axis=0)
    hidden_near = swap(hidden, "tp", 1)
    hidden_far = swap(hidden, "tp", 2)

    def down_hop(mine, other, product, weight):
        blocks = product(jnp.concatenate([mine, other], axis=0), weight)
        blocks = blocks.reshape(2, 2, half, width)
        return blocks[:, 0], swap(blocks[:, 1], "ctx", 1)

    def down_second(kept, came):
        pair = wide(kept) + wide(came)
        other = pick(pair, 1 - core).astype(jnp.bfloat16)
        return pick(pair, core), other, swap(other, "ctx", 2)

    def in_order(a, b):
        first = first_half == 0
        return jnp.concatenate([jnp.where(first, a, b), jnp.where(first, b, a)], axis=0)

    attended = in_order(attended_a, attended_b)
    kept_b, came_b = down_hop(hidden, hidden_near, matmul, down_loaded)
    hidden_far = after(hidden_far, (kept_b, attended))
    hidden_far_near = swap(hidden_far, "tp", 1)
    down_b, other_b, last_b = down_second(kept_b, after(came_b, hidden_far))
    down_a, _, last_a = down_second(
        *down_hop(hidden_far, after(hidden_far_near, other_b), streamed_matmul, down_weight)
    )
    out_b = (wide(attended_b) + down_b + wide(last_b)).astype(jnp.bfloat16)
    out_a = (wide(attended_a) + down_a + wide(last_a)).astype(jnp.bfloat16)

    return attended, in_order(out_a, out_b)


def on_device(
    residual,
    latent,
    queries,
    lengths,
    value_weight,
    output_weight,
    norm_gain,
    gate_weight,
    up_weight,
    down_weight,
):
    row_count = residual.shape[0]
    ctx_place = lax.axis_index("ctx")
    n_ctx, n_tp = lax.axis_size("ctx"), lax.axis_size("tp")
    paired = (
        n_ctx == 4
        and n_tp == 4
        and row_count % 64 == 0
        and residual.shape[1] % 256 == 0
        and output_weight.shape[0] % 512 == 0
        and down_weight.shape[0] % 512 == 0
        and gate_weight.shape[0] % 256 == 0
        and gate_weight.shape[1] % 256 == 0
    )
    own_index = ctx_place * row_count + jnp.arange(row_count, dtype=jnp.int32)
    _, own_position = trace_info(own_index, lengths)
    key_order = jnp.arange(n_ctx * row_count, dtype=jnp.int32)
    if paired:
        key_index = key_order + (ctx_place - (n_ctx - 1)) * row_count
        _, key_position = trace_info(key_index, lengths)
        keys = rope_keys(gather_keys(latent, n_ctx), key_position, LAT)
    else:
        rotated_keys = rope_keys(latent, own_position, LAT)
        keys = lax.all_gather(rotated_keys, "ctx", axis=1, tiled=True)
        key_index = key_order
    heads_out = attention(queries, keys, key_index, own_index, own_position, value_weight)
    if paired:
        return paired_tail(
            heads_out,
            residual,
            output_weight,
            norm_gain,
            gate_weight,
            up_weight,
            down_weight,
            n_ctx,
            n_tp,
        )
    all_heads = lax.all_gather(heads_out, "tp", axis=1, tiled=True)
    head_block = lax.all_to_all(all_heads, "ctx", split_axis=1, concat_axis=0, tiled=True)
    head_sum = lax.psum_scatter(
        jnp.dot(head_block, output_weight, preferred_element_type=jnp.float32).astype(jnp.bfloat16),
        "ctx",
        scatter_dimension=0,
        tiled=True,
    ).astype(jnp.float32)
    attended = (residual.astype(jnp.float32) + head_sum).astype(jnp.bfloat16)
    attended_float = attended.astype(jnp.float32)
    squares = lax.psum(jnp.sum(attended_float * attended_float, axis=1), "tp")
    inverse_rms = lax.rsqrt(squares / D + norm_eps)
    scaled = (attended_float * inverse_rms[:, None] * norm_gain[None, :]).astype(jnp.bfloat16)
    scaled_all = lax.all_gather(scaled, "ctx", axis=0, tiled=True)
    unit_count = gate_weight.shape[1]
    gate_up = jnp.concatenate([gate_weight, up_weight], axis=1)
    summed = lax.psum_scatter(
        jnp.dot(scaled_all, gate_up, preferred_element_type=jnp.float32).astype(jnp.bfloat16),
        "tp",
        scatter_dimension=0,
        tiled=True,
    ).astype(jnp.float32)
    hidden_share = (jax.nn.silu(summed[:, :unit_count]) * summed[:, unit_count:]).astype(
        jnp.bfloat16
    )
    hidden_all = lax.all_gather(hidden_share, "tp", axis=0, tiled=True)
    down_sum = lax.psum_scatter(
        jnp.dot(hidden_all, down_weight, preferred_element_type=jnp.float32).astype(jnp.bfloat16),
        "ctx",
        scatter_dimension=0,
        tiled=True,
    ).astype(jnp.float32)
    layer_out = (attended_float + down_sum).astype(jnp.bfloat16)
    return (attended, layer_out)


def solution(mesh):
    in_specs = (
        P(("grp", "ctx"), "tp"),
        P(None, ("grp", "ctx")),
        P(("grp", "ctx"), "tp"),
        P("grp"),
        P(None, "tp"),
        P("ctx", "tp"),
        P("tp"),
        P("tp", "ctx"),
        P("tp", "ctx"),
        P("ctx", "tp"),
    )
    out_specs = (P(("grp", "ctx"), "tp"), P(("grp", "ctx"), "tp"))
    return jax.shard_map(
        on_device, mesh=mesh, in_specs=in_specs, out_specs=out_specs, check_vma=False
    )
```

```python
import functools

import jax
import jax.numpy as jnp
from jax import lax
from jax.experimental import pallas as pl
from jax.experimental.pallas import tpu as pltpu
from jax.sharding import PartitionSpec as P

D = 7168
LAT = 512
ROPE = 64
VHEAD = 128


score_scale = 192.0 ** (-0.5)
rope_base = 10000.0
norm_eps = 1e-06
masked_score = -1e30


def rope_freqs(half_width):
    return rope_base ** (-jnp.arange(half_width, dtype=jnp.float32) / half_width)


def trace_info(token_index, lengths):
    trace_ends = jnp.cumsum(lengths)
    starts = trace_ends - lengths
    trace_ids = jnp.sum((token_index[:, None] >= trace_ends[None, :]).astype(jnp.int32), axis=1)
    member = trace_ids[:, None] == jnp.arange(lengths.shape[0], dtype=jnp.int32)[None, :]
    pos_shift = jnp.sum(jnp.where(member, (0 - starts)[None, :], 0), axis=1)
    return (trace_ids, token_index + pos_shift)


def rope_keys(latent, positions, latent_width):
    values = latent.astype(jnp.float32)
    half_width = (values.shape[0] - latent_width) // 2
    angles = rope_freqs(half_width)[:, None] * positions.astype(jnp.float32)[None, :]
    first_half = values[latent_width : latent_width + half_width]
    second_half = values[latent_width + half_width :]
    cosine = jnp.cos(angles)
    sine_value = jnp.sin(angles)
    return jnp.concatenate(
        [
            values[:latent_width],
            first_half * cosine - second_half * sine_value,
            first_half * sine_value + second_half * cosine,
        ],
        axis=0,
    ).astype(jnp.bfloat16)


def rope_tables(positions, half_width, lanes):
    angles = positions.astype(jnp.float32)[:, None] * rope_freqs(half_width)[None, :]
    cosine, sine_value = jnp.cos(angles), jnp.sin(angles)
    cos_part = jnp.concatenate([cosine, cosine], axis=1)
    sin_part = jnp.concatenate([-sine_value, sine_value], axis=1)
    rest = lanes - 2 * half_width
    ones = jnp.ones((angles.shape[0], rest), jnp.float32)
    zeros = jnp.zeros((angles.shape[0], rest), jnp.float32)
    return jnp.stack(
        [
            jnp.concatenate([cos_part, ones], axis=1),
            jnp.concatenate([sin_part, zeros], axis=1),
            jnp.concatenate([ones, cos_part], axis=1),
            jnp.concatenate([zeros, sin_part], axis=1),
        ]
    )


def attention_kernel(
    group, tables, starts, own_index, key_index, keys, queries, value_weight, out, even, odd, values, bias
):
    row_count = queries.shape[0]
    width = queries.shape[1] // group
    half_width = (width - LAT) // 2
    lanes = 2 * (width - LAT)

    @pl.when(pl.program_id(0) == 0)
    def prepare():
        all_keys = keys[...]
        pad = jnp.zeros((width - LAT, all_keys.shape[1]), jnp.bfloat16)
        even[:width] = all_keys
        even[width:] = pad
        odd[: width - LAT] = pad
        odd[width - LAT :] = all_keys
        values[...] = keys[:LAT].astype(jnp.float32).T.astype(jnp.bfloat16)
        allowed = (key_index[...] >= starts[...]) & (key_index[...] <= own_index[...])
        bias[...] = jnp.where(allowed, 0.0, masked_score)

    lane = lax.broadcasted_iota(jnp.int32, (row_count, lanes), 1)
    low = (lane & (2 * half_width - 1)) < half_width

    def turned(start, which):
        entry = queries[:, start : start + lanes].astype(jnp.float32)
        partner = jnp.where(
            low, pltpu.roll(entry, lanes - half_width, 1), pltpu.roll(entry, half_width, 1)
        )
        return (entry * tables[2 * which] + partner * tables[2 * which + 1]).astype(jnp.bfloat16)

    for which, key_rows in ((0, even), (1, odd)):
        rows = []
        for head in range(which, group, 2):
            base = (head - which) * width
            if which == 0:
                rows.append(
                    jnp.concatenate([queries[:, base : base + LAT], turned(base + LAT, 0)], axis=1)
                )
            else:
                first = base + LAT
                rows.append(
                    jnp.concatenate(
                        [queries[:, first : first + LAT], turned(first + LAT, 1)], axis=1
                    )
                )
        stacked = jnp.concatenate(rows, axis=0)
        scores = jnp.dot(stacked, key_rows[...], preferred_element_type=jnp.float32)
        scores = scores.reshape(len(rows), row_count, -1) + bias[...][None]
        top = jnp.max(scores, axis=2, keepdims=True)
        exponent = jnp.exp((scores - top) * score_scale)
        total = jnp.sum(exponent, axis=2, keepdims=True).reshape(len(rows) * row_count, 1)
        weights = exponent.astype(jnp.bfloat16).reshape(len(rows) * row_count, -1)
        mixed = jnp.dot(weights, values[...], preferred_element_type=jnp.float32)
        mixed = (mixed / total).astype(jnp.bfloat16)
        for i in range(len(rows)):
            head = 2 * i + which
            out[:, head * VHEAD : (head + 1) * VHEAD] = jnp.dot(
                mixed[i * row_count : (i + 1) * row_count],
                value_weight[:, head * VHEAD : (head + 1) * VHEAD],
                preferred_element_type=jnp.float32,
            ).astype(jnp.bfloat16)


def attention(queries, keys, key_index, own_index, own_position, value_weight):
    row_count, query_width = queries.shape
    local_heads = value_weight.shape[1] // VHEAD
    width = query_width // local_heads
    group = 4 if local_heads % 4 == 0 else 2
    key_count = keys.shape[1]
    tables = rope_tables(own_position, (width - LAT) // 2, 2 * (width - LAT))
    whole = lambda shape: pl.BlockSpec(shape, lambda i: (0,) * len(shape))
    deep = 2 * width - LAT
    return pl.pallas_call(
        functools.partial(attention_kernel, group),
        grid=(local_heads // group,),
        in_specs=[
            whole(tables.shape),
            whole((row_count, 1)),
            whole((row_count, 1)),
            whole((1, key_count)),
            whole(keys.shape),
            pl.BlockSpec((row_count, group * width), lambda i: (0, i)),
            pl.BlockSpec((LAT, group * VHEAD), lambda i: (0, i)),
        ],
        out_specs=pl.BlockSpec((row_count, group * VHEAD), lambda i: (0, i)),
        out_shape=jax.ShapeDtypeStruct((row_count, local_heads * VHEAD), jnp.bfloat16),
        scratch_shapes=[
            pltpu.VMEM((deep, key_count), jnp.bfloat16),
            pltpu.VMEM((deep, key_count), jnp.bfloat16),
            pltpu.VMEM((key_count, LAT), jnp.bfloat16),
            pltpu.VMEM((row_count, key_count), jnp.float32),
        ],
        compiler_params=pltpu.CompilerParams(vmem_limit_bytes=(6 + key_count // 64) * 1024 * 1024),
        cost_estimate=pl.CostEstimate(
            flops=2 * row_count * local_heads * (key_count * (deep + LAT) + LAT * VHEAD),
            bytes_accessed=2 * (queries.size + keys.size + value_weight.size),
            transcendentals=row_count * local_heads * key_count,
        ),
    )(
        tables,
        (own_index - own_position)[:, None],
        own_index[:, None],
        key_index[None, :],
        keys,
        queries,
        value_weight,
    )


def swap(value, axis_name, bit):
    width = lax.axis_size(axis_name)
    return lax.ppermute(value, axis_name, [(i, i ^ bit) for i in range(width)])


def pick(value, index):
    return lax.dynamic_index_in_dim(value, index, 0, keepdims=False)


def wide(value):
    return value.astype(jnp.float32)


def matmul(a, b):
    return jnp.dot(a, b, preferred_element_type=jnp.float32).astype(jnp.bfloat16)


def streamed_kernel(depth, rows, weight, out, held, total, sems):
    steps = weight.shape[0] // depth
    each = depth // 2
    copies = [
        pltpu.make_async_copy(
            weight.at[pl.ds(i * each, each)], held.at[pl.ds(i * each, each)], sems.at[i]
        )
        for i in range(2 * steps)
    ]
    for copy in copies:
        copy.start()
    block = 256
    for i in range(steps):
        copies[2 * i].wait()
        copies[2 * i + 1].wait()
        part = rows[:, i * depth : (i + 1) * depth]
        for start in range(0, weight.shape[1], block):
            columns = slice(start, start + block)
            term = jnp.dot(
                part,
                held[i * depth : (i + 1) * depth, columns],
                preferred_element_type=jnp.float32,
            )
            if i > 0:
                term = term + total[:, columns]
            if i < steps - 1:
                total[:, columns] = term
            else:
                out[:, columns] = term.astype(out.dtype)


def streamed_matmul(rows, weight):
    steps = weight.shape[0] // 512
    return pl.pallas_call(
        functools.partial(streamed_kernel, 512),
        in_specs=[
            pl.BlockSpec(memory_space=pltpu.VMEM),
            pl.BlockSpec(memory_space=pl.ANY),
        ],
        out_specs=pl.BlockSpec(memory_space=pltpu.VMEM),
        out_shape=jax.ShapeDtypeStruct((rows.shape[0], weight.shape[1]), jnp.bfloat16),
        scratch_shapes=[
            pltpu.VMEM(weight.shape, weight.dtype),
            pltpu.VMEM((rows.shape[0], weight.shape[1]), jnp.float32),
            pltpu.SemaphoreType.DMA((2 * steps,)),
        ],
        compiler_params=pltpu.CompilerParams(vmem_limit_bytes=50 * 1024 * 1024),
        cost_estimate=pl.CostEstimate(flops=1024, bytes_accessed=1024, transcendentals=0),
    )(rows, weight)


def after(value, earlier):
    return lax.optimization_barrier((value, earlier))[0]


def gather_keys(latent, n_ctx):
    rows = latent.shape[0] // 2
    core = lax.axis_index("tp") & 1
    half = lax.dynamic_slice_in_dim(latent, core * rows, rows, 0)
    came = [
        lax.ppermute(half, "ctx", [(c, c + d) for c in range(n_ctx - d)])
        for d in range(n_ctx - 1, 0, -1)
    ]
    mine = jnp.concatenate(came, axis=1)
    other = swap(mine, "tp", 1)
    before = jnp.concatenate(
        [jnp.where(core == 0, mine, other), jnp.where(core == 0, other, mine)], axis=0
    )
    return jnp.concatenate([before, latent], axis=1)


def spread_heads(heads_out, n_ctx, n_tp):
    c, t = lax.axis_index("ctx"), lax.axis_index("tp")
    quarters = heads_out.reshape(n_tp, heads_out.shape[0] // n_tp, heads_out.shape[1])
    groups = jnp.stack(
        [pick(quarters, t)] + [swap(pick(quarters, t ^ m), "tp", m) for m in range(1, n_tp)]
    )
    return jnp.stack(
        [pick(groups, t ^ c)] + [swap(pick(groups, t ^ c ^ j), "ctx", j) for j in range(1, n_ctx)]
    )


def core_rows(mine, other):
    first = lax.axis_index("tp") & 1 == 0
    both = jnp.stack([jnp.where(first, mine, other), jnp.where(first, other, mine)], axis=1)
    return both.reshape(-1, mine.shape[-1])


def paired_tail(
    heads_out, residual, output_weight, norm_gain, gate_weight, up_weight, down_weight, n_ctx, n_tp
):
    row_count, width = residual.shape
    half = row_count // 2
    model_width = width * n_tp
    t = lax.axis_index("tp")
    core = t & 1
    first_half = t >> 1
    own = spread_heads(heads_out, n_ctx, n_tp)
    near = swap(own, "tp", 1)
    far = swap(own, "tp", 2)
    residual_halves = residual.reshape(2, half, width)

    def first_hop(rows):
        blocks = streamed_matmul(rows, output_weight).reshape(2, 2, half, width)
        sent = blocks[:, 1]
        return blocks[:, 0], sent, swap(sent, "ctx", 1)

    def second_hop(kept, came):
        other = (wide(kept[1]) + wide(came[1])).astype(jnp.bfloat16)
        return wide(kept[0]) + wide(came[0]), other, swap(other, "ctx", 2)

    def attend(mine, came, which):
        return (wide(pick(residual_halves, which)) + mine + wide(came)).astype(jnp.bfloat16)

    def scale(rows):
        values = wide(rows)
        scaled = (values * norm_gain[None, :]).astype(jnp.bfloat16)
        return jnp.sum(values * values, axis=1), scaled

    def gate_up(rows):
        squares, scaled = scale(rows)
        terms = [matmul(scaled, gate_weight), matmul(scaled, up_weight)]

        def side(which):
            return jnp.concatenate(
                [lax.dynamic_slice_in_dim(term, which * half, half, 0) for term in terms], axis=0
            )

        return side(core), side(1 - core), squares

    def chip_sum(kept, sent):
        return wide(kept) + wide(swap(sent, "tp", 1))

    kept_a, sent_a, came_a = first_hop(core_rows(own, near))
    far = after(far, sent_a)
    far_near = swap(far, "tp", 1)
    mine_a, other_a, last_a = second_hop(kept_a, came_a)
    kept_b, sent_b, came_b = first_hop(core_rows(far, after(far_near, other_a)))
    attended_a = attend(mine_a, after(last_a, sent_b), first_half)
    twin_a = swap(attended_a, "ctx", 2)
    pair_a = jnp.concatenate([attended_a, twin_a], axis=0)
    rest_a = swap(pair_a, "ctx", 1)
    mine_b, other_b, last_b = second_hop(kept_b, after(came_b, pair_a))
    rest_a, last_b = lax.optimization_barrier((rest_a, last_b))
    attended_b = attend(mine_b, last_b, 1 - first_half)
    twin_b = swap(attended_b, "ctx", 2)
    all_a = jnp.concatenate([pair_a, rest_a], axis=0)
    squares_a, scaled = scale(all_a)

    def cross(rows, weight):
        term = matmul(rows, weight).reshape(2, 2, half, -1)

        def side(which):
            return lax.dynamic_index_in_dim(term, which, 1, keepdims=False).reshape(2 * half, -1)

        sent = side(1 - core)
        total = chip_sum(side(core), sent).astype(jnp.bfloat16)
        return sent, total, swap(total, "tp", 2)

    sent_gate, _, across_gate = cross(scaled, gate_weight)
    _, sums_up, across_up = cross(after(scaled, sent_gate), up_weight)
    squares_a = after(squares_a, sums_up)
    across_squares = swap(squares_a + swap(squares_a, "tp", 1), "tp", 2)
    pair_b = jnp.concatenate([attended_b, after(twin_b, across_gate)], axis=0)
    rest_b = swap(pair_b, "ctx", 1)

    def hide(chip_terms, squares, across_gate, across_up, across_squares):
        squares = squares + swap(squares, "tp", 1) + across_squares
        squares = lax.dynamic_slice_in_dim(squares, core * half, half, 0)
        inverse_rms = lax.rsqrt(squares / model_width + norm_eps)[:, None]
        gate = (chip_terms[:half] + wide(across_gate)) * inverse_rms
        up = (chip_terms[half:] + wide(across_up)) * inverse_rms
        return (jax.nn.silu(gate) * up).astype(jnp.bfloat16)

    kept, sent, squares_p = gate_up(after(pair_b, sums_up))
    terms_p = chip_sum(kept, sent)
    rest_b, across_up, _ = lax.optimization_barrier((rest_b, across_up, sent))
    kept, sent, squares_q = gate_up(rest_b)
    terms_q = chip_sum(kept, sent)
    parts = [
        hide(
            terms,
            squares,
            across_gate[i * half : (i + 1) * half],
            across_up[i * half : (i + 1) * half],
            across_squares[2 * i * half : 2 * (i + 1) * half],
        )
        for i, (terms, squares) in enumerate(((terms_p, squares_p), (terms_q, squares_q)))
    ]
    hidden = jnp.concatenate(parts, axis=0)
    hidden_near = swap(hidden, "tp", 1)
    hidden_far = swap(hidden, "tp", 2)

    def down_hop(mine, other):
        blocks = streamed_matmul(jnp.concatenate([mine, other], axis=0), down_weight)
        blocks = blocks.reshape(2, 2, half, width)
        return blocks[:, 0], swap(blocks[:, 1], "ctx", 1)

    def down_second(kept, came):
        pair = wide(kept) + wide(came)
        other = pick(pair, 1 - core).astype(jnp.bfloat16)
        return pick(pair, core), other, swap(other, "ctx", 2)

    def in_order(a, b):
        first = first_half == 0
        return jnp.concatenate([jnp.where(first, a, b), jnp.where(first, b, a)], axis=0)

    attended = in_order(attended_a, attended_b)
    kept_b, came_b = down_hop(hidden, hidden_near)
    hidden_far = after(hidden_far, (kept_b, attended))
    hidden_far_near = swap(hidden_far, "tp", 1)
    down_b, other_b, last_b = down_second(kept_b, after(came_b, hidden_far))
    down_a, _, last_a = down_second(*down_hop(hidden_far, after(hidden_far_near, other_b)))
    out_b = (wide(attended_b) + down_b + wide(last_b)).astype(jnp.bfloat16)
    out_a = (wide(attended_a) + down_a + wide(last_a)).astype(jnp.bfloat16)

    return attended, in_order(out_a, out_b)


def on_device(
    residual,
    latent,
    queries,
    lengths,
    value_weight,
    output_weight,
    norm_gain,
    gate_weight,
    up_weight,
    down_weight,
):
    row_count = residual.shape[0]
    ctx_place = lax.axis_index("ctx")
    n_ctx, n_tp = lax.axis_size("ctx"), lax.axis_size("tp")
    paired = (
        n_ctx == 4
        and n_tp == 4
        and row_count % 64 == 0
        and residual.shape[1] % 256 == 0
        and output_weight.shape[0] % 512 == 0
        and down_weight.shape[0] % 512 == 0
    )
    own_index = ctx_place * row_count + jnp.arange(row_count, dtype=jnp.int32)
    _, own_position = trace_info(own_index, lengths)
    key_order = jnp.arange(n_ctx * row_count, dtype=jnp.int32)
    if paired:
        key_index = key_order + (ctx_place - (n_ctx - 1)) * row_count
        _, key_position = trace_info(key_index, lengths)
        keys = rope_keys(gather_keys(latent, n_ctx), key_position, LAT)
    else:
        rotated_keys = rope_keys(latent, own_position, LAT)
        keys = lax.all_gather(rotated_keys, "ctx", axis=1, tiled=True)
        key_index = key_order
    heads_out = attention(queries, keys, key_index, own_index, own_position, value_weight)
    if paired:
        return paired_tail(
            heads_out,
            residual,
            output_weight,
            norm_gain,
            gate_weight,
            up_weight,
            down_weight,
            n_ctx,
            n_tp,
        )
    all_heads = lax.all_gather(heads_out, "tp", axis=1, tiled=True)
    head_block = lax.all_to_all(all_heads, "ctx", split_axis=1, concat_axis=0, tiled=True)
    head_sum = lax.psum_scatter(
        jnp.dot(head_block, output_weight, preferred_element_type=jnp.float32).astype(jnp.bfloat16),
        "ctx",
        scatter_dimension=0,
        tiled=True,
    ).astype(jnp.float32)
    attended = (residual.astype(jnp.float32) + head_sum).astype(jnp.bfloat16)
    attended_float = attended.astype(jnp.float32)
    squares = lax.psum(jnp.sum(attended_float * attended_float, axis=1), "tp")
    inverse_rms = lax.rsqrt(squares / D + norm_eps)
    scaled = (attended_float * inverse_rms[:, None] * norm_gain[None, :]).astype(jnp.bfloat16)
    scaled_all = lax.all_gather(scaled, "ctx", axis=0, tiled=True)
    unit_count = gate_weight.shape[1]
    gate_up = jnp.concatenate([gate_weight, up_weight], axis=1)
    summed = lax.psum_scatter(
        jnp.dot(scaled_all, gate_up, preferred_element_type=jnp.float32).astype(jnp.bfloat16),
        "tp",
        scatter_dimension=0,
        tiled=True,
    ).astype(jnp.float32)
    hidden_share = (jax.nn.silu(summed[:, :unit_count]) * summed[:, unit_count:]).astype(
        jnp.bfloat16
    )
    hidden_all = lax.all_gather(hidden_share, "tp", axis=0, tiled=True)
    down_sum = lax.psum_scatter(
        jnp.dot(hidden_all, down_weight, preferred_element_type=jnp.float32).astype(jnp.bfloat16),
        "ctx",
        scatter_dimension=0,
        tiled=True,
    ).astype(jnp.float32)
    layer_out = (attended_float + down_sum).astype(jnp.bfloat16)
    return (attended, layer_out)


def solution(mesh):
    in_specs = (
        P(("grp", "ctx"), "tp"),
        P(None, ("grp", "ctx")),
        P(("grp", "ctx"), "tp"),
        P("grp"),
        P(None, "tp"),
        P("ctx", "tp"),
        P("tp"),
        P("tp", "ctx"),
        P("tp", "ctx"),
        P("ctx", "tp"),
    )
    out_specs = (P(("grp", "ctx"), "tp"), P(("grp", "ctx"), "tp"))
    return jax.shard_map(
        on_device, mesh=mesh, in_specs=in_specs, out_specs=out_specs, check_vma=False
    )
```

```python
import functools

import jax
import jax.numpy as jnp
from jax import lax
from jax.experimental import pallas as pl
from jax.experimental.pallas import tpu as pltpu
from jax.sharding import PartitionSpec as P

D = 7168
LAT = 512
ROPE = 64
VHEAD = 128


score_scale = 192.0 ** (-0.5)
rope_base = 10000.0
norm_eps = 1e-06
masked_score = -1e30


def rope_freqs(half_width):
    return rope_base ** (-jnp.arange(half_width, dtype=jnp.float32) / half_width)


def trace_info(token_index, lengths):
    trace_ends = jnp.cumsum(lengths)
    starts = trace_ends - lengths
    trace_ids = jnp.sum((token_index[:, None] >= trace_ends[None, :]).astype(jnp.int32), axis=1)
    member = trace_ids[:, None] == jnp.arange(lengths.shape[0], dtype=jnp.int32)[None, :]
    pos_shift = jnp.sum(jnp.where(member, (0 - starts)[None, :], 0), axis=1)
    return (trace_ids, token_index + pos_shift)


def rope_keys(latent, positions, latent_width):
    values = latent.astype(jnp.float32)
    half_width = (values.shape[0] - latent_width) // 2
    angles = rope_freqs(half_width)[:, None] * positions.astype(jnp.float32)[None, :]
    first_half = values[latent_width : latent_width + half_width]
    second_half = values[latent_width + half_width :]
    cosine = jnp.cos(angles)
    sine_value = jnp.sin(angles)
    return jnp.concatenate(
        [
            values[:latent_width],
            first_half * cosine - second_half * sine_value,
            first_half * sine_value + second_half * cosine,
        ],
        axis=0,
    ).astype(jnp.bfloat16)


def rope_tables(positions, half_width, lanes):
    angles = positions.astype(jnp.float32)[:, None] * rope_freqs(half_width)[None, :]
    cosine, sine_value = jnp.cos(angles), jnp.sin(angles)
    cos_part = jnp.concatenate([cosine, cosine], axis=1)
    sin_part = jnp.concatenate([-sine_value, sine_value], axis=1)
    rest = lanes - 2 * half_width
    ones = jnp.ones((angles.shape[0], rest), jnp.float32)
    zeros = jnp.zeros((angles.shape[0], rest), jnp.float32)
    return jnp.stack(
        [
            jnp.concatenate([cos_part, ones], axis=1),
            jnp.concatenate([sin_part, zeros], axis=1),
            jnp.concatenate([ones, cos_part], axis=1),
            jnp.concatenate([zeros, sin_part], axis=1),
        ]
    )


def attention_kernel(
    group, tables, starts, own_index, key_index, keys, queries, value_weight, out, even, odd, values, bias
):
    row_count = queries.shape[0]
    width = queries.shape[1] // group
    half_width = (width - LAT) // 2
    lanes = 2 * (width - LAT)

    @pl.when(pl.program_id(0) == 0)
    def prepare():
        all_keys = keys[...]
        pad = jnp.zeros((width - LAT, all_keys.shape[1]), jnp.bfloat16)
        even[:width] = all_keys
        even[width:] = pad
        odd[: width - LAT] = pad
        odd[width - LAT :] = all_keys
        values[...] = keys[:LAT].astype(jnp.float32).T.astype(jnp.bfloat16)
        allowed = (key_index[...] >= starts[...]) & (key_index[...] <= own_index[...])
        bias[...] = jnp.where(allowed, 0.0, masked_score)

    lane = lax.broadcasted_iota(jnp.int32, (row_count, lanes), 1)
    low = (lane & (2 * half_width - 1)) < half_width

    def turned(start, which):
        entry = queries[:, start : start + lanes].astype(jnp.float32)
        partner = jnp.where(
            low, pltpu.roll(entry, lanes - half_width, 1), pltpu.roll(entry, half_width, 1)
        )
        return (entry * tables[2 * which] + partner * tables[2 * which + 1]).astype(jnp.bfloat16)

    for which, key_rows in ((0, even), (1, odd)):
        rows = []
        for head in range(which, group, 2):
            base = (head - which) * width
            if which == 0:
                rows.append(
                    jnp.concatenate([queries[:, base : base + LAT], turned(base + LAT, 0)], axis=1)
                )
            else:
                first = base + LAT
                rows.append(
                    jnp.concatenate(
                        [queries[:, first : first + LAT], turned(first + LAT, 1)], axis=1
                    )
                )
        stacked = jnp.concatenate(rows, axis=0)
        scores = jnp.dot(stacked, key_rows[...], preferred_element_type=jnp.float32)
        scores = scores.reshape(len(rows), row_count, -1) + bias[...][None]
        top = jnp.max(scores, axis=2, keepdims=True)
        exponent = jnp.exp((scores - top) * score_scale)
        total = jnp.sum(exponent, axis=2, keepdims=True).reshape(len(rows) * row_count, 1)
        weights = exponent.astype(jnp.bfloat16).reshape(len(rows) * row_count, -1)
        mixed = jnp.dot(weights, values[...], preferred_element_type=jnp.float32)
        mixed = (mixed / total).astype(jnp.bfloat16)
        for i in range(len(rows)):
            head = 2 * i + which
            out[:, head * VHEAD : (head + 1) * VHEAD] = jnp.dot(
                mixed[i * row_count : (i + 1) * row_count],
                value_weight[:, head * VHEAD : (head + 1) * VHEAD],
                preferred_element_type=jnp.float32,
            ).astype(jnp.bfloat16)


def attention(queries, keys, key_index, own_index, own_position, value_weight):
    row_count, query_width = queries.shape
    local_heads = value_weight.shape[1] // VHEAD
    width = query_width // local_heads
    group = 4 if local_heads % 4 == 0 else 2
    key_count = keys.shape[1]
    tables = rope_tables(own_position, (width - LAT) // 2, 2 * (width - LAT))
    whole = lambda shape: pl.BlockSpec(shape, lambda i: (0,) * len(shape))
    deep = 2 * width - LAT
    return pl.pallas_call(
        functools.partial(attention_kernel, group),
        grid=(local_heads // group,),
        in_specs=[
            whole(tables.shape),
            whole((row_count, 1)),
            whole((row_count, 1)),
            whole((1, key_count)),
            whole(keys.shape),
            pl.BlockSpec((row_count, group * width), lambda i: (0, i)),
            pl.BlockSpec((LAT, group * VHEAD), lambda i: (0, i)),
        ],
        out_specs=pl.BlockSpec((row_count, group * VHEAD), lambda i: (0, i)),
        out_shape=jax.ShapeDtypeStruct((row_count, local_heads * VHEAD), jnp.bfloat16),
        scratch_shapes=[
            pltpu.VMEM((deep, key_count), jnp.bfloat16),
            pltpu.VMEM((deep, key_count), jnp.bfloat16),
            pltpu.VMEM((key_count, LAT), jnp.bfloat16),
            pltpu.VMEM((row_count, key_count), jnp.float32),
        ],
        compiler_params=pltpu.CompilerParams(vmem_limit_bytes=(6 + key_count // 64) * 1024 * 1024),
        cost_estimate=pl.CostEstimate(
            flops=2 * row_count * local_heads * (key_count * (deep + LAT) + LAT * VHEAD),
            bytes_accessed=2 * (queries.size + keys.size + value_weight.size),
            transcendentals=row_count * local_heads * key_count,
        ),
    )(
        tables,
        (own_index - own_position)[:, None],
        own_index[:, None],
        key_index[None, :],
        keys,
        queries,
        value_weight,
    )


def swap(value, axis_name, bit):
    width = lax.axis_size(axis_name)
    return lax.ppermute(value, axis_name, [(i, i ^ bit) for i in range(width)])


def pick(value, index):
    return lax.dynamic_index_in_dim(value, index, 0, keepdims=False)


def wide(value):
    return value.astype(jnp.float32)


def matmul(a, b):
    return jnp.dot(a, b, preferred_element_type=jnp.float32).astype(jnp.bfloat16)


def streamed_kernel(depth, rows, weight, out, held, total, sems):
    steps = weight.shape[0] // depth
    each = depth // 2
    copies = [
        pltpu.make_async_copy(
            weight.at[pl.ds(i * each, each)], held.at[pl.ds(i * each, each)], sems.at[i]
        )
        for i in range(2 * steps)
    ]
    for copy in copies:
        copy.start()
    block = 256
    for i in range(steps):
        copies[2 * i].wait()
        copies[2 * i + 1].wait()
        part = rows[:, i * depth : (i + 1) * depth]
        for start in range(0, weight.shape[1], block):
            columns = slice(start, start + block)
            term = jnp.dot(
                part,
                held[i * depth : (i + 1) * depth, columns],
                preferred_element_type=jnp.float32,
            )
            if i > 0:
                term = term + total[:, columns]
            if i < steps - 1:
                total[:, columns] = term
            else:
                out[:, columns] = term.astype(out.dtype)


def streamed_matmul(rows, weight):
    steps = weight.shape[0] // 512
    return pl.pallas_call(
        functools.partial(streamed_kernel, 512),
        in_specs=[
            pl.BlockSpec(memory_space=pltpu.VMEM),
            pl.BlockSpec(memory_space=pl.ANY),
        ],
        out_specs=pl.BlockSpec(memory_space=pltpu.VMEM),
        out_shape=jax.ShapeDtypeStruct((rows.shape[0], weight.shape[1]), jnp.bfloat16),
        scratch_shapes=[
            pltpu.VMEM(weight.shape, weight.dtype),
            pltpu.VMEM((rows.shape[0], weight.shape[1]), jnp.float32),
            pltpu.SemaphoreType.DMA((2 * steps,)),
        ],
        compiler_params=pltpu.CompilerParams(vmem_limit_bytes=50 * 1024 * 1024),
        cost_estimate=pl.CostEstimate(flops=1024, bytes_accessed=1024, transcendentals=0),
    )(rows, weight)


def add_kernel(mine, came, out):
    out[...] = (mine[...].astype(jnp.float32) + came[...].astype(jnp.float32)).astype(out.dtype)


def add_rows(mine, came):
    whole = pl.BlockSpec(memory_space=pltpu.VMEM)
    return pl.pallas_call(
        add_kernel,
        in_specs=[whole, whole],
        out_specs=whole,
        out_shape=jax.ShapeDtypeStruct(mine.shape, jnp.bfloat16),
        cost_estimate=pl.CostEstimate(
            flops=8 * 10**9, bytes_accessed=6 * mine.size, transcendentals=0
        ),
    )(mine, came)


def after(value, earlier):
    return lax.optimization_barrier((value, earlier))[0]


def gather_keys(latent, n_ctx):
    rows = latent.shape[0] // 2
    core = lax.axis_index("tp") & 1
    half = lax.dynamic_slice_in_dim(latent, core * rows, rows, 0)
    came = [
        lax.ppermute(half, "ctx", [(c, c + d) for c in range(n_ctx - d)])
        for d in range(n_ctx - 1, 0, -1)
    ]
    mine = jnp.concatenate(came, axis=1)
    other = swap(mine, "tp", 1)
    before = jnp.concatenate(
        [jnp.where(core == 0, mine, other), jnp.where(core == 0, other, mine)], axis=0
    )
    return jnp.concatenate([before, latent], axis=1)


def spread_heads(heads_out, n_ctx, n_tp):
    c, t = lax.axis_index("ctx"), lax.axis_index("tp")
    quarters = heads_out.reshape(n_tp, heads_out.shape[0] // n_tp, heads_out.shape[1])
    groups = jnp.stack(
        [pick(quarters, t)] + [swap(pick(quarters, t ^ m), "tp", m) for m in range(1, n_tp)]
    )
    return jnp.stack(
        [pick(groups, t ^ c)] + [swap(pick(groups, t ^ c ^ j), "ctx", j) for j in range(1, n_ctx)]
    )


def core_rows(mine, other):
    first = lax.axis_index("tp") & 1 == 0
    both = jnp.stack([jnp.where(first, mine, other), jnp.where(first, other, mine)], axis=1)
    return both.reshape(-1, mine.shape[-1])


def paired_tail(
    heads_out, residual, output_weight, norm_gain, gate_weight, up_weight, down_weight, n_ctx, n_tp
):
    row_count, width = residual.shape
    half = row_count // 2
    model_width = width * n_tp
    t = lax.axis_index("tp")
    core = t & 1
    first_half = t >> 1
    own = spread_heads(heads_out, n_ctx, n_tp)
    near = swap(own, "tp", 1)
    far = swap(own, "tp", 2)
    residual_halves = residual.reshape(2, half, width)

    def first_hop(rows):
        blocks = streamed_matmul(rows, output_weight).reshape(2, 2, half, width)
        sent = blocks[:, 1]
        return blocks[:, 0], sent, swap(sent, "ctx", 1)

    def second_hop(kept, came, add=lambda a, b: (wide(a) + wide(b)).astype(jnp.bfloat16)):
        other = add(kept[1], came[1])
        return wide(kept[0]) + wide(came[0]), other, swap(other, "ctx", 2)

    def attend(mine, came, which):
        return (wide(pick(residual_halves, which)) + mine + wide(came)).astype(jnp.bfloat16)

    def scale(rows):
        values = wide(rows)
        scaled = (values * norm_gain[None, :]).astype(jnp.bfloat16)
        return jnp.sum(values * values, axis=1), scaled

    def gate_up(rows):
        squares, scaled = scale(rows)
        terms = [matmul(scaled, gate_weight), matmul(scaled, up_weight)]

        def side(which):
            return jnp.concatenate(
                [lax.dynamic_slice_in_dim(term, which * half, half, 0) for term in terms], axis=0
            )

        return side(core), side(1 - core), squares

    def chip_sum(kept, sent):
        return wide(kept) + wide(swap(sent, "tp", 1))

    kept_a, sent_a, came_a = first_hop(core_rows(own, near))
    far = after(far, sent_a)
    far_near = swap(far, "tp", 1)
    mine_a, other_a, last_a = second_hop(kept_a, came_a)
    kept_b, sent_b, came_b = first_hop(core_rows(far, after(far_near, other_a)))
    attended_a = attend(mine_a, after(last_a, sent_b), first_half)
    twin_a = swap(attended_a, "ctx", 2)
    pair_a = jnp.concatenate([attended_a, twin_a], axis=0)
    rest_a = swap(pair_a, "ctx", 1)
    mine_b, other_b, last_b = second_hop(kept_b, after(came_b, pair_a), add_rows)
    rest_a, last_b = lax.optimization_barrier((rest_a, last_b))
    attended_b = attend(mine_b, last_b, 1 - first_half)
    twin_b = swap(attended_b, "ctx", 2)
    all_a = jnp.concatenate([pair_a, rest_a], axis=0)
    squares_a, scaled = scale(all_a)

    def cross(rows, weight):
        term = matmul(rows, weight).reshape(2, 2, half, -1)

        def side(which):
            return lax.dynamic_index_in_dim(term, which, 1, keepdims=False).reshape(2 * half, -1)

        sent = side(1 - core)
        total = chip_sum(side(core), sent).astype(jnp.bfloat16)
        return sent, total, swap(total, "tp", 2)

    sent_gate, _, across_gate = cross(scaled, gate_weight)
    _, sums_up, across_up = cross(after(scaled, sent_gate), up_weight)
    squares_a = after(squares_a, sums_up)
    across_squares = swap(squares_a + swap(squares_a, "tp", 1), "tp", 2)
    pair_b = jnp.concatenate([attended_b, after(twin_b, across_gate)], axis=0)
    rest_b = swap(pair_b, "ctx", 1)

    def hide(chip_terms, squares, across_gate, across_up, across_squares):
        squares = squares + swap(squares, "tp", 1) + across_squares
        squares = lax.dynamic_slice_in_dim(squares, core * half, half, 0)
        inverse_rms = lax.rsqrt(squares / model_width + norm_eps)[:, None]
        gate = (chip_terms[:half] + wide(across_gate)) * inverse_rms
        up = (chip_terms[half:] + wide(across_up)) * inverse_rms
        return (jax.nn.silu(gate) * up).astype(jnp.bfloat16)

    kept, sent, squares_p = gate_up(after(pair_b, sums_up))
    terms_p = chip_sum(kept, sent)
    rest_b, across_up, _ = lax.optimization_barrier((rest_b, across_up, sent))
    kept, sent, squares_q = gate_up(rest_b)
    terms_q = chip_sum(kept, sent)
    parts = [
        hide(
            terms,
            squares,
            across_gate[i * half : (i + 1) * half],
            across_up[i * half : (i + 1) * half],
            across_squares[2 * i * half : 2 * (i + 1) * half],
        )
        for i, (terms, squares) in enumerate(((terms_p, squares_p), (terms_q, squares_q)))
    ]
    hidden = jnp.concatenate(parts, axis=0)
    hidden_near = swap(hidden, "tp", 1)
    hidden_far = swap(hidden, "tp", 2)

    def down_hop(mine, other):
        blocks = streamed_matmul(jnp.concatenate([mine, other], axis=0), down_weight)
        blocks = blocks.reshape(2, 2, half, width)
        return blocks[:, 0], swap(blocks[:, 1], "ctx", 1)

    def down_second(kept, came):
        pair = wide(kept) + wide(came)
        other = pick(pair, 1 - core).astype(jnp.bfloat16)
        return pick(pair, core), other, swap(other, "ctx", 2)

    def in_order(a, b):
        first = first_half == 0
        return jnp.concatenate([jnp.where(first, a, b), jnp.where(first, b, a)], axis=0)

    attended = in_order(attended_a, attended_b)
    kept_b, came_b = down_hop(hidden, hidden_near)
    hidden_far = after(hidden_far, (kept_b, attended))
    hidden_far_near = swap(hidden_far, "tp", 1)
    down_b, other_b, last_b = down_second(kept_b, after(came_b, hidden_far))
    down_a, _, last_a = down_second(*down_hop(hidden_far, after(hidden_far_near, other_b)))
    out_b = (wide(attended_b) + down_b + wide(last_b)).astype(jnp.bfloat16)
    out_a = (wide(attended_a) + down_a + wide(last_a)).astype(jnp.bfloat16)

    return attended, in_order(out_a, out_b)


def on_device(
    residual,
    latent,
    queries,
    lengths,
    value_weight,
    output_weight,
    norm_gain,
    gate_weight,
    up_weight,
    down_weight,
):
    row_count = residual.shape[0]
    ctx_place = lax.axis_index("ctx")
    n_ctx, n_tp = lax.axis_size("ctx"), lax.axis_size("tp")
    paired = (
        n_ctx == 4
        and n_tp == 4
        and row_count % 64 == 0
        and residual.shape[1] % 256 == 0
        and output_weight.shape[0] % 512 == 0
        and down_weight.shape[0] % 512 == 0
    )
    own_index = ctx_place * row_count + jnp.arange(row_count, dtype=jnp.int32)
    _, own_position = trace_info(own_index, lengths)
    key_order = jnp.arange(n_ctx * row_count, dtype=jnp.int32)
    if paired:
        key_index = key_order + (ctx_place - (n_ctx - 1)) * row_count
        _, key_position = trace_info(key_index, lengths)
        keys = rope_keys(gather_keys(latent, n_ctx), key_position, LAT)
    else:
        rotated_keys = rope_keys(latent, own_position, LAT)
        keys = lax.all_gather(rotated_keys, "ctx", axis=1, tiled=True)
        key_index = key_order
    heads_out = attention(queries, keys, key_index, own_index, own_position, value_weight)
    if paired:
        return paired_tail(
            heads_out,
            residual,
            output_weight,
            norm_gain,
            gate_weight,
            up_weight,
            down_weight,
            n_ctx,
            n_tp,
        )
    all_heads = lax.all_gather(heads_out, "tp", axis=1, tiled=True)
    head_block = lax.all_to_all(all_heads, "ctx", split_axis=1, concat_axis=0, tiled=True)
    head_sum = lax.psum_scatter(
        jnp.dot(head_block, output_weight, preferred_element_type=jnp.float32).astype(jnp.bfloat16),
        "ctx",
        scatter_dimension=0,
        tiled=True,
    ).astype(jnp.float32)
    attended = (residual.astype(jnp.float32) + head_sum).astype(jnp.bfloat16)
    attended_float = attended.astype(jnp.float32)
    squares = lax.psum(jnp.sum(attended_float * attended_float, axis=1), "tp")
    inverse_rms = lax.rsqrt(squares / D + norm_eps)
    scaled = (attended_float * inverse_rms[:, None] * norm_gain[None, :]).astype(jnp.bfloat16)
    scaled_all = lax.all_gather(scaled, "ctx", axis=0, tiled=True)
    unit_count = gate_weight.shape[1]
    gate_up = jnp.concatenate([gate_weight, up_weight], axis=1)
    summed = lax.psum_scatter(
        jnp.dot(scaled_all, gate_up, preferred_element_type=jnp.float32).astype(jnp.bfloat16),
        "tp",
        scatter_dimension=0,
        tiled=True,
    ).astype(jnp.float32)
    hidden_share = (jax.nn.silu(summed[:, :unit_count]) * summed[:, unit_count:]).astype(
        jnp.bfloat16
    )
    hidden_all = lax.all_gather(hidden_share, "tp", axis=0, tiled=True)
    down_sum = lax.psum_scatter(
        jnp.dot(hidden_all, down_weight, preferred_element_type=jnp.float32).astype(jnp.bfloat16),
        "ctx",
        scatter_dimension=0,
        tiled=True,
    ).astype(jnp.float32)
    layer_out = (attended_float + down_sum).astype(jnp.bfloat16)
    return (attended, layer_out)


def solution(mesh):
    in_specs = (
        P(("grp", "ctx"), "tp"),
        P(None, ("grp", "ctx")),
        P(("grp", "ctx"), "tp"),
        P("grp"),
        P(None, "tp"),
        P("ctx", "tp"),
        P("tp"),
        P("tp", "ctx"),
        P("tp", "ctx"),
        P("ctx", "tp"),
    )
    out_specs = (P(("grp", "ctx"), "tp"), P(("grp", "ctx"), "tp"))
    return jax.shard_map(
        on_device, mesh=mesh, in_specs=in_specs, out_specs=out_specs, check_vma=False
    )
```

```python
import functools

import jax
import jax.numpy as jnp
from jax import lax
from jax.experimental import pallas as pl
from jax.experimental.pallas import tpu as pltpu
from jax.sharding import PartitionSpec as P

D = 7168
LAT = 512
ROPE = 64
VHEAD = 128


score_scale = 192.0 ** (-0.5)
rope_base = 10000.0
norm_eps = 1e-06
masked_score = -1e30


def rope_freqs(half_width):
    return rope_base ** (-jnp.arange(half_width, dtype=jnp.float32) / half_width)


def trace_info(token_index, lengths):
    trace_ends = jnp.cumsum(lengths)
    starts = trace_ends - lengths
    trace_ids = jnp.sum((token_index[:, None] >= trace_ends[None, :]).astype(jnp.int32), axis=1)
    member = trace_ids[:, None] == jnp.arange(lengths.shape[0], dtype=jnp.int32)[None, :]
    pos_shift = jnp.sum(jnp.where(member, (0 - starts)[None, :], 0), axis=1)
    return (trace_ids, token_index + pos_shift)


def rope_keys(latent, positions, latent_width):
    values = latent.astype(jnp.float32)
    half_width = (values.shape[0] - latent_width) // 2
    angles = rope_freqs(half_width)[:, None] * positions.astype(jnp.float32)[None, :]
    first_half = values[latent_width : latent_width + half_width]
    second_half = values[latent_width + half_width :]
    cosine = jnp.cos(angles)
    sine_value = jnp.sin(angles)
    return jnp.concatenate(
        [
            values[:latent_width],
            first_half * cosine - second_half * sine_value,
            first_half * sine_value + second_half * cosine,
        ],
        axis=0,
    ).astype(jnp.bfloat16)


def rope_tables(positions, half_width, lanes):
    angles = positions.astype(jnp.float32)[:, None] * rope_freqs(half_width)[None, :]
    cosine, sine_value = jnp.cos(angles), jnp.sin(angles)
    cos_part = jnp.concatenate([cosine, cosine], axis=1)
    sin_part = jnp.concatenate([-sine_value, sine_value], axis=1)
    rest = lanes - 2 * half_width
    ones = jnp.ones((angles.shape[0], rest), jnp.float32)
    zeros = jnp.zeros((angles.shape[0], rest), jnp.float32)
    return jnp.stack(
        [
            jnp.concatenate([cos_part, ones], axis=1),
            jnp.concatenate([sin_part, zeros], axis=1),
            jnp.concatenate([ones, cos_part], axis=1),
            jnp.concatenate([zeros, sin_part], axis=1),
        ]
    )


def attention_kernel(
    group, tables, starts, own_index, key_index, keys, queries, value_weight, out, even, odd, values, bias
):
    row_count = queries.shape[0]
    width = queries.shape[1] // group
    half_width = (width - LAT) // 2
    lanes = 2 * (width - LAT)

    @pl.when(pl.program_id(0) == 0)
    def prepare():
        all_keys = keys[...]
        pad = jnp.zeros((width - LAT, all_keys.shape[1]), jnp.bfloat16)
        even[:width] = all_keys
        even[width:] = pad
        odd[: width - LAT] = pad
        odd[width - LAT :] = all_keys
        values[...] = keys[:LAT].astype(jnp.float32).T.astype(jnp.bfloat16)
        allowed = (key_index[...] >= starts[...]) & (key_index[...] <= own_index[...])
        bias[...] = jnp.where(allowed, 0.0, masked_score)

    lane = lax.broadcasted_iota(jnp.int32, (row_count, lanes), 1)
    low = (lane & (2 * half_width - 1)) < half_width

    def turned(start, which):
        entry = queries[:, start : start + lanes].astype(jnp.float32)
        partner = jnp.where(
            low, pltpu.roll(entry, lanes - half_width, 1), pltpu.roll(entry, half_width, 1)
        )
        return (entry * tables[2 * which] + partner * tables[2 * which + 1]).astype(jnp.bfloat16)

    for which, key_rows in ((0, even), (1, odd)):
        rows = []
        for head in range(which, group, 2):
            base = (head - which) * width
            if which == 0:
                rows.append(
                    jnp.concatenate([queries[:, base : base + LAT], turned(base + LAT, 0)], axis=1)
                )
            else:
                first = base + LAT
                rows.append(
                    jnp.concatenate(
                        [queries[:, first : first + LAT], turned(first + LAT, 1)], axis=1
                    )
                )
        stacked = jnp.concatenate(rows, axis=0)
        scores = jnp.dot(stacked, key_rows[...], preferred_element_type=jnp.float32)
        scores = scores.reshape(len(rows), row_count, -1) + bias[...][None]
        top = jnp.max(scores, axis=2, keepdims=True)
        exponent = jnp.exp((scores - top) * score_scale)
        total = jnp.sum(exponent, axis=2, keepdims=True).reshape(len(rows) * row_count, 1)
        weights = exponent.astype(jnp.bfloat16).reshape(len(rows) * row_count, -1)
        mixed = jnp.dot(weights, values[...], preferred_element_type=jnp.float32)
        mixed = (mixed / total).astype(jnp.bfloat16)
        for i in range(len(rows)):
            head = 2 * i + which
            out[:, head * VHEAD : (head + 1) * VHEAD] = jnp.dot(
                mixed[i * row_count : (i + 1) * row_count],
                value_weight[:, head * VHEAD : (head + 1) * VHEAD],
                preferred_element_type=jnp.float32,
            ).astype(jnp.bfloat16)


def attention(queries, keys, key_index, own_index, own_position, value_weight):
    row_count, query_width = queries.shape
    local_heads = value_weight.shape[1] // VHEAD
    width = query_width // local_heads
    group = 4 if local_heads % 4 == 0 else 2
    key_count = keys.shape[1]
    tables = rope_tables(own_position, (width - LAT) // 2, 2 * (width - LAT))
    whole = lambda shape: pl.BlockSpec(shape, lambda i: (0,) * len(shape))
    deep = 2 * width - LAT
    return pl.pallas_call(
        functools.partial(attention_kernel, group),
        grid=(local_heads // group,),
        in_specs=[
            whole(tables.shape),
            whole((row_count, 1)),
            whole((row_count, 1)),
            whole((1, key_count)),
            whole(keys.shape),
            pl.BlockSpec((row_count, group * width), lambda i: (0, i)),
            pl.BlockSpec((LAT, group * VHEAD), lambda i: (0, i)),
        ],
        out_specs=pl.BlockSpec((row_count, group * VHEAD), lambda i: (0, i)),
        out_shape=jax.ShapeDtypeStruct((row_count, local_heads * VHEAD), jnp.bfloat16),
        scratch_shapes=[
            pltpu.VMEM((deep, key_count), jnp.bfloat16),
            pltpu.VMEM((deep, key_count), jnp.bfloat16),
            pltpu.VMEM((key_count, LAT), jnp.bfloat16),
            pltpu.VMEM((row_count, key_count), jnp.float32),
        ],
        compiler_params=pltpu.CompilerParams(vmem_limit_bytes=(6 + key_count // 64) * 1024 * 1024),
        cost_estimate=pl.CostEstimate(
            flops=2 * row_count * local_heads * (key_count * (deep + LAT) + LAT * VHEAD),
            bytes_accessed=2 * (queries.size + keys.size + value_weight.size),
            transcendentals=row_count * local_heads * key_count,
        ),
    )(
        tables,
        (own_index - own_position)[:, None],
        own_index[:, None],
        key_index[None, :],
        keys,
        queries,
        value_weight,
    )


def swap(value, axis_name, bit):
    width = lax.axis_size(axis_name)
    return lax.ppermute(value, axis_name, [(i, i ^ bit) for i in range(width)])


def pick(value, index):
    return lax.dynamic_index_in_dim(value, index, 0, keepdims=False)


def wide(value):
    return value.astype(jnp.float32)


def matmul(a, b):
    return jnp.dot(a, b, preferred_element_type=jnp.float32).astype(jnp.bfloat16)


def streamed_kernel(depth, rows, weight, out, held, total, sems):
    steps = weight.shape[0] // depth
    each = depth // 2
    copies = [
        pltpu.make_async_copy(
            weight.at[pl.ds(i * each, each)], held.at[pl.ds(i * each, each)], sems.at[i]
        )
        for i in range(2 * steps)
    ]
    for copy in copies:
        copy.start()
    block = 256
    for i in range(steps):
        copies[2 * i].wait()
        copies[2 * i + 1].wait()
        part = rows[:, i * depth : (i + 1) * depth]
        for start in range(0, weight.shape[1], block):
            columns = slice(start, start + block)
            term = jnp.dot(
                part,
                held[i * depth : (i + 1) * depth, columns],
                preferred_element_type=jnp.float32,
            )
            if i > 0:
                term = term + total[:, columns]
            if i < steps - 1:
                total[:, columns] = term
            else:
                out[:, columns] = term.astype(out.dtype)


def streamed_matmul(rows, weight):
    steps = weight.shape[0] // 512
    return pl.pallas_call(
        functools.partial(streamed_kernel, 512),
        in_specs=[
            pl.BlockSpec(memory_space=pltpu.VMEM),
            pl.BlockSpec(memory_space=pl.ANY),
        ],
        out_specs=pl.BlockSpec(memory_space=pltpu.VMEM),
        out_shape=jax.ShapeDtypeStruct((rows.shape[0], weight.shape[1]), jnp.bfloat16),
        scratch_shapes=[
            pltpu.VMEM(weight.shape, weight.dtype),
            pltpu.VMEM((rows.shape[0], weight.shape[1]), jnp.float32),
            pltpu.SemaphoreType.DMA((2 * steps,)),
        ],
        compiler_params=pltpu.CompilerParams(vmem_limit_bytes=50 * 1024 * 1024),
        cost_estimate=pl.CostEstimate(flops=1024, bytes_accessed=1024, transcendentals=0),
    )(rows, weight)


def add_kernel(mine, came, out):
    out[...] = (mine[...].astype(jnp.float32) + came[...].astype(jnp.float32)).astype(out.dtype)


def add_rows(mine, came):
    whole = pl.BlockSpec(memory_space=pltpu.VMEM)
    return pl.pallas_call(
        add_kernel,
        in_specs=[whole, whole],
        out_specs=whole,
        out_shape=jax.ShapeDtypeStruct(mine.shape, jnp.bfloat16),
        compiler_params=pltpu.CompilerParams(vmem_limit_bytes=4 * 1024 * 1024),
        cost_estimate=pl.CostEstimate(
            flops=8 * 10**9, bytes_accessed=6 * mine.size, transcendentals=0
        ),
    )(mine, came)


def after(value, earlier):
    return lax.optimization_barrier((value, earlier))[0]


def gather_keys(latent, n_ctx):
    rows = latent.shape[0] // 2
    core = lax.axis_index("tp") & 1
    half = lax.dynamic_slice_in_dim(latent, core * rows, rows, 0)
    came = [
        lax.ppermute(half, "ctx", [(c, c + d) for c in range(n_ctx - d)])
        for d in range(n_ctx - 1, 0, -1)
    ]
    mine = jnp.concatenate(came, axis=1)
    other = swap(mine, "tp", 1)
    before = jnp.concatenate(
        [jnp.where(core == 0, mine, other), jnp.where(core == 0, other, mine)], axis=0
    )
    return jnp.concatenate([before, latent], axis=1)


def spread_heads(heads_out, n_ctx, n_tp):
    c, t = lax.axis_index("ctx"), lax.axis_index("tp")
    quarters = heads_out.reshape(n_tp, heads_out.shape[0] // n_tp, heads_out.shape[1])
    groups = jnp.stack(
        [pick(quarters, t)] + [swap(pick(quarters, t ^ m), "tp", m) for m in range(1, n_tp)]
    )
    return jnp.stack(
        [pick(groups, t ^ c)] + [swap(pick(groups, t ^ c ^ j), "ctx", j) for j in range(1, n_ctx)]
    )


def core_rows(mine, other):
    first = lax.axis_index("tp") & 1 == 0
    both = jnp.stack([jnp.where(first, mine, other), jnp.where(first, other, mine)], axis=1)
    return both.reshape(-1, mine.shape[-1])


def paired_tail(
    heads_out, residual, output_weight, norm_gain, gate_weight, up_weight, down_weight, n_ctx, n_tp
):
    row_count, width = residual.shape
    half = row_count // 2
    model_width = width * n_tp
    t = lax.axis_index("tp")
    core = t & 1
    first_half = t >> 1
    own = spread_heads(heads_out, n_ctx, n_tp)
    near = swap(own, "tp", 1)
    far = swap(own, "tp", 2)
    residual_halves = residual.reshape(2, half, width)

    def first_hop(rows):
        blocks = streamed_matmul(rows, output_weight).reshape(2, 2, half, width)
        sent = blocks[:, 1]
        return blocks[:, 0], sent, swap(sent, "ctx", 1)

    def second_hop(kept, came, add=lambda a, b: (wide(a) + wide(b)).astype(jnp.bfloat16)):
        other = add(kept[1], came[1])
        return wide(kept[0]) + wide(came[0]), other, swap(other, "ctx", 2)

    def attend(mine, came, which):
        return (wide(pick(residual_halves, which)) + mine + wide(came)).astype(jnp.bfloat16)

    def scale(rows):
        values = wide(rows)
        scaled = (values * norm_gain[None, :]).astype(jnp.bfloat16)
        return jnp.sum(values * values, axis=1), scaled

    def gate_up(rows):
        squares, scaled = scale(rows)
        terms = [matmul(scaled, gate_weight), matmul(scaled, up_weight)]

        def side(which):
            return jnp.concatenate(
                [lax.dynamic_slice_in_dim(term, which * half, half, 0) for term in terms], axis=0
            )

        return side(core), side(1 - core), squares

    def chip_sum(kept, sent):
        return wide(kept) + wide(swap(sent, "tp", 1))

    kept_a, sent_a, came_a = first_hop(core_rows(own, near))
    far = after(far, sent_a)
    far_near = swap(far, "tp", 1)
    mine_a, other_a, last_a = second_hop(kept_a, came_a)
    kept_b, sent_b, came_b = first_hop(core_rows(far, after(far_near, other_a)))
    attended_a = attend(mine_a, after(last_a, sent_b), first_half)
    twin_a = swap(attended_a, "ctx", 2)
    pair_a = jnp.concatenate([attended_a, twin_a], axis=0)
    rest_a = swap(pair_a, "ctx", 1)
    mine_b, other_b, last_b = second_hop(kept_b, after(came_b, pair_a), add_rows)
    rest_a, last_b = lax.optimization_barrier((rest_a, last_b))
    attended_b = attend(mine_b, last_b, 1 - first_half)
    twin_b = swap(attended_b, "ctx", 2)
    all_a = jnp.concatenate([pair_a, rest_a], axis=0)
    squares_a, scaled = scale(all_a)

    def cross(rows, weight):
        term = matmul(rows, weight).reshape(2, 2, half, -1)

        def side(which):
            return lax.dynamic_index_in_dim(term, which, 1, keepdims=False).reshape(2 * half, -1)

        sent = side(1 - core)
        total = chip_sum(side(core), sent).astype(jnp.bfloat16)
        return sent, total, swap(total, "tp", 2)

    sent_gate, _, across_gate = cross(scaled, gate_weight)
    _, sums_up, across_up = cross(after(scaled, sent_gate), up_weight)
    squares_a = after(squares_a, sums_up)
    across_squares = swap(squares_a + swap(squares_a, "tp", 1), "tp", 2)
    pair_b = jnp.concatenate([attended_b, after(twin_b, across_gate)], axis=0)
    rest_b = swap(pair_b, "ctx", 1)

    def hide(chip_terms, squares, across_gate, across_up, across_squares):
        squares = squares + swap(squares, "tp", 1) + across_squares
        squares = lax.dynamic_slice_in_dim(squares, core * half, half, 0)
        inverse_rms = lax.rsqrt(squares / model_width + norm_eps)[:, None]
        gate = (chip_terms[:half] + wide(across_gate)) * inverse_rms
        up = (chip_terms[half:] + wide(across_up)) * inverse_rms
        return (jax.nn.silu(gate) * up).astype(jnp.bfloat16)

    kept, sent, squares_p = gate_up(after(pair_b, sums_up))
    terms_p = chip_sum(kept, sent)
    rest_b, across_up, _ = lax.optimization_barrier((rest_b, across_up, sent))
    kept, sent, squares_q = gate_up(rest_b)
    terms_q = chip_sum(kept, sent)
    parts = [
        hide(
            terms,
            squares,
            across_gate[i * half : (i + 1) * half],
            across_up[i * half : (i + 1) * half],
            across_squares[2 * i * half : 2 * (i + 1) * half],
        )
        for i, (terms, squares) in enumerate(((terms_p, squares_p), (terms_q, squares_q)))
    ]
    hidden = jnp.concatenate(parts, axis=0)
    hidden_near = swap(hidden, "tp", 1)
    hidden_far = swap(hidden, "tp", 2)

    def down_hop(mine, other):
        blocks = streamed_matmul(jnp.concatenate([mine, other], axis=0), down_weight)
        blocks = blocks.reshape(2, 2, half, width)
        return blocks[:, 0], swap(blocks[:, 1], "ctx", 1)

    def down_second(kept, came):
        pair = wide(kept) + wide(came)
        other = pick(pair, 1 - core).astype(jnp.bfloat16)
        return pick(pair, core), other, swap(other, "ctx", 2)

    def in_order(a, b):
        first = first_half == 0
        return jnp.concatenate([jnp.where(first, a, b), jnp.where(first, b, a)], axis=0)

    attended = in_order(attended_a, attended_b)
    kept_b, came_b = down_hop(hidden, hidden_near)
    hidden_far = after(hidden_far, (kept_b, attended))
    hidden_far_near = swap(hidden_far, "tp", 1)
    down_b, other_b, last_b = down_second(kept_b, after(came_b, hidden_far))
    down_a, _, last_a = down_second(*down_hop(hidden_far, after(hidden_far_near, other_b)))
    out_b = (wide(attended_b) + down_b + wide(last_b)).astype(jnp.bfloat16)
    out_a = (wide(attended_a) + down_a + wide(last_a)).astype(jnp.bfloat16)

    return attended, in_order(out_a, out_b)


def on_device(
    residual,
    latent,
    queries,
    lengths,
    value_weight,
    output_weight,
    norm_gain,
    gate_weight,
    up_weight,
    down_weight,
):
    row_count = residual.shape[0]
    ctx_place = lax.axis_index("ctx")
    n_ctx, n_tp = lax.axis_size("ctx"), lax.axis_size("tp")
    paired = (
        n_ctx == 4
        and n_tp == 4
        and row_count % 64 == 0
        and residual.shape[1] % 256 == 0
        and output_weight.shape[0] % 512 == 0
        and down_weight.shape[0] % 512 == 0
    )
    own_index = ctx_place * row_count + jnp.arange(row_count, dtype=jnp.int32)
    _, own_position = trace_info(own_index, lengths)
    key_order = jnp.arange(n_ctx * row_count, dtype=jnp.int32)
    if paired:
        key_index = key_order + (ctx_place - (n_ctx - 1)) * row_count
        _, key_position = trace_info(key_index, lengths)
        keys = rope_keys(gather_keys(latent, n_ctx), key_position, LAT)
    else:
        rotated_keys = rope_keys(latent, own_position, LAT)
        keys = lax.all_gather(rotated_keys, "ctx", axis=1, tiled=True)
        key_index = key_order
    heads_out = attention(queries, keys, key_index, own_index, own_position, value_weight)
    if paired:
        return paired_tail(
            heads_out,
            residual,
            output_weight,
            norm_gain,
            gate_weight,
            up_weight,
            down_weight,
            n_ctx,
            n_tp,
        )
    all_heads = lax.all_gather(heads_out, "tp", axis=1, tiled=True)
    head_block = lax.all_to_all(all_heads, "ctx", split_axis=1, concat_axis=0, tiled=True)
    head_sum = lax.psum_scatter(
        jnp.dot(head_block, output_weight, preferred_element_type=jnp.float32).astype(jnp.bfloat16),
        "ctx",
        scatter_dimension=0,
        tiled=True,
    ).astype(jnp.float32)
    attended = (residual.astype(jnp.float32) + head_sum).astype(jnp.bfloat16)
    attended_float = attended.astype(jnp.float32)
    squares = lax.psum(jnp.sum(attended_float * attended_float, axis=1), "tp")
    inverse_rms = lax.rsqrt(squares / D + norm_eps)
    scaled = (attended_float * inverse_rms[:, None] * norm_gain[None, :]).astype(jnp.bfloat16)
    scaled_all = lax.all_gather(scaled, "ctx", axis=0, tiled=True)
    unit_count = gate_weight.shape[1]
    gate_up = jnp.concatenate([gate_weight, up_weight], axis=1)
    summed = lax.psum_scatter(
        jnp.dot(scaled_all, gate_up, preferred_element_type=jnp.float32).astype(jnp.bfloat16),
        "tp",
        scatter_dimension=0,
        tiled=True,
    ).astype(jnp.float32)
    hidden_share = (jax.nn.silu(summed[:, :unit_count]) * summed[:, unit_count:]).astype(
        jnp.bfloat16
    )
    hidden_all = lax.all_gather(hidden_share, "tp", axis=0, tiled=True)
    down_sum = lax.psum_scatter(
        jnp.dot(hidden_all, down_weight, preferred_element_type=jnp.float32).astype(jnp.bfloat16),
        "ctx",
        scatter_dimension=0,
        tiled=True,
    ).astype(jnp.float32)
    layer_out = (attended_float + down_sum).astype(jnp.bfloat16)
    return (attended, layer_out)


def solution(mesh):
    in_specs = (
        P(("grp", "ctx"), "tp"),
        P(None, ("grp", "ctx")),
        P(("grp", "ctx"), "tp"),
        P("grp"),
        P(None, "tp"),
        P("ctx", "tp"),
        P("tp"),
        P("tp", "ctx"),
        P("tp", "ctx"),
        P("ctx", "tp"),
    )
    out_specs = (P(("grp", "ctx"), "tp"), P(("grp", "ctx"), "tp"))
    return jax.shard_map(
        on_device, mesh=mesh, in_specs=in_specs, out_specs=out_specs, check_vma=False
    )
```

```python
import functools

import jax
import jax.numpy as jnp
from jax import lax
from jax.experimental import pallas as pl
from jax.experimental.pallas import tpu as pltpu
from jax.sharding import PartitionSpec as P

D = 7168
LAT = 512
ROPE = 64
VHEAD = 128


score_scale = 192.0 ** (-0.5)
rope_base = 10000.0
norm_eps = 1e-06
masked_score = -1e30


def rope_freqs(half_width):
    return rope_base ** (-jnp.arange(half_width, dtype=jnp.float32) / half_width)


def trace_info(token_index, lengths):
    trace_ends = jnp.cumsum(lengths)
    starts = trace_ends - lengths
    trace_ids = jnp.sum((token_index[:, None] >= trace_ends[None, :]).astype(jnp.int32), axis=1)
    member = trace_ids[:, None] == jnp.arange(lengths.shape[0], dtype=jnp.int32)[None, :]
    pos_shift = jnp.sum(jnp.where(member, (0 - starts)[None, :], 0), axis=1)
    return (trace_ids, token_index + pos_shift)


def rope_keys(latent, positions, latent_width):
    values = latent.astype(jnp.float32)
    half_width = (values.shape[0] - latent_width) // 2
    angles = rope_freqs(half_width)[:, None] * positions.astype(jnp.float32)[None, :]
    first_half = values[latent_width : latent_width + half_width]
    second_half = values[latent_width + half_width :]
    cosine = jnp.cos(angles)
    sine_value = jnp.sin(angles)
    return jnp.concatenate(
        [
            values[:latent_width],
            first_half * cosine - second_half * sine_value,
            first_half * sine_value + second_half * cosine,
        ],
        axis=0,
    ).astype(jnp.bfloat16)


def rope_tables(positions, half_width, lanes):
    angles = positions.astype(jnp.float32)[:, None] * rope_freqs(half_width)[None, :]
    cosine, sine_value = jnp.cos(angles), jnp.sin(angles)
    cos_part = jnp.concatenate([cosine, cosine], axis=1)
    sin_part = jnp.concatenate([-sine_value, sine_value], axis=1)
    rest = lanes - 2 * half_width
    ones = jnp.ones((angles.shape[0], rest), jnp.float32)
    zeros = jnp.zeros((angles.shape[0], rest), jnp.float32)
    return jnp.stack(
        [
            jnp.concatenate([cos_part, ones], axis=1),
            jnp.concatenate([sin_part, zeros], axis=1),
            jnp.concatenate([ones, cos_part], axis=1),
            jnp.concatenate([zeros, sin_part], axis=1),
        ]
    )


def attention_kernel(
    group, tables, starts, own_index, key_index, keys, queries, value_weight, out, even, odd, values, bias
):
    row_count = queries.shape[0]
    width = queries.shape[1] // group
    half_width = (width - LAT) // 2
    lanes = 2 * (width - LAT)

    @pl.when(pl.program_id(0) == 0)
    def prepare():
        all_keys = keys[...]
        pad = jnp.zeros((width - LAT, all_keys.shape[1]), jnp.bfloat16)
        even[:width] = all_keys
        even[width:] = pad
        odd[: width - LAT] = pad
        odd[width - LAT :] = all_keys
        values[...] = keys[:LAT].astype(jnp.float32).T.astype(jnp.bfloat16)
        allowed = (key_index[...] >= starts[...]) & (key_index[...] <= own_index[...])
        bias[...] = jnp.where(allowed, 0.0, masked_score)

    lane = lax.broadcasted_iota(jnp.int32, (row_count, lanes), 1)
    low = (lane & (2 * half_width - 1)) < half_width

    def turned(start, which):
        entry = queries[:, start : start + lanes].astype(jnp.float32)
        partner = jnp.where(
            low, pltpu.roll(entry, lanes - half_width, 1), pltpu.roll(entry, half_width, 1)
        )
        return (entry * tables[2 * which] + partner * tables[2 * which + 1]).astype(jnp.bfloat16)

    for which, key_rows in ((0, even), (1, odd)):
        rows = []
        for head in range(which, group, 2):
            base = (head - which) * width
            if which == 0:
                rows.append(
                    jnp.concatenate([queries[:, base : base + LAT], turned(base + LAT, 0)], axis=1)
                )
            else:
                first = base + LAT
                rows.append(
                    jnp.concatenate(
                        [queries[:, first : first + LAT], turned(first + LAT, 1)], axis=1
                    )
                )
        stacked = jnp.concatenate(rows, axis=0)
        scores = jnp.dot(stacked, key_rows[...], preferred_element_type=jnp.float32)
        scores = scores.reshape(len(rows), row_count, -1) + bias[...][None]
        top = jnp.max(scores, axis=2, keepdims=True)
        exponent = jnp.exp((scores - top) * score_scale)
        total = jnp.sum(exponent, axis=2, keepdims=True).reshape(len(rows) * row_count, 1)
        weights = exponent.astype(jnp.bfloat16).reshape(len(rows) * row_count, -1)
        mixed = jnp.dot(weights, values[...], preferred_element_type=jnp.float32)
        mixed = (mixed / total).astype(jnp.bfloat16)
        for i in range(len(rows)):
            head = 2 * i + which
            out[:, head * VHEAD : (head + 1) * VHEAD] = jnp.dot(
                mixed[i * row_count : (i + 1) * row_count],
                value_weight[:, head * VHEAD : (head + 1) * VHEAD],
                preferred_element_type=jnp.float32,
            ).astype(jnp.bfloat16)


def attention(queries, keys, key_index, own_index, own_position, value_weight):
    row_count, query_width = queries.shape
    local_heads = value_weight.shape[1] // VHEAD
    width = query_width // local_heads
    group = 4 if local_heads % 4 == 0 else 2
    key_count = keys.shape[1]
    tables = rope_tables(own_position, (width - LAT) // 2, 2 * (width - LAT))
    whole = lambda shape: pl.BlockSpec(shape, lambda i: (0,) * len(shape))
    deep = 2 * width - LAT
    return pl.pallas_call(
        functools.partial(attention_kernel, group),
        grid=(local_heads // group,),
        in_specs=[
            whole(tables.shape),
            whole((row_count, 1)),
            whole((row_count, 1)),
            whole((1, key_count)),
            whole(keys.shape),
            pl.BlockSpec((row_count, group * width), lambda i: (0, i)),
            pl.BlockSpec((LAT, group * VHEAD), lambda i: (0, i)),
        ],
        out_specs=pl.BlockSpec((row_count, group * VHEAD), lambda i: (0, i)),
        out_shape=jax.ShapeDtypeStruct((row_count, local_heads * VHEAD), jnp.bfloat16),
        scratch_shapes=[
            pltpu.VMEM((deep, key_count), jnp.bfloat16),
            pltpu.VMEM((deep, key_count), jnp.bfloat16),
            pltpu.VMEM((key_count, LAT), jnp.bfloat16),
            pltpu.VMEM((row_count, key_count), jnp.float32),
        ],
        compiler_params=pltpu.CompilerParams(vmem_limit_bytes=(6 + key_count // 64) * 1024 * 1024),
        cost_estimate=pl.CostEstimate(
            flops=2 * row_count * local_heads * (key_count * (deep + LAT) + LAT * VHEAD),
            bytes_accessed=2 * (queries.size + keys.size + value_weight.size),
            transcendentals=row_count * local_heads * key_count,
        ),
    )(
        tables,
        (own_index - own_position)[:, None],
        own_index[:, None],
        key_index[None, :],
        keys,
        queries,
        value_weight,
    )


def swap(value, axis_name, bit):
    width = lax.axis_size(axis_name)
    return lax.ppermute(value, axis_name, [(i, i ^ bit) for i in range(width)])


def pick(value, index):
    return lax.dynamic_index_in_dim(value, index, 0, keepdims=False)


def wide(value):
    return value.astype(jnp.float32)


def matmul(a, b):
    return jnp.dot(a, b, preferred_element_type=jnp.float32).astype(jnp.bfloat16)


def streamed_kernel(depth, rows, weight, out, held, total, sems):
    steps = weight.shape[0] // depth
    each = depth // 2
    copies = [
        pltpu.make_async_copy(
            weight.at[pl.ds(i * each, each)], held.at[pl.ds(i * each, each)], sems.at[i]
        )
        for i in range(2 * steps)
    ]
    for copy in copies:
        copy.start()
    block = 256
    for i in range(steps):
        copies[2 * i].wait()
        copies[2 * i + 1].wait()
        part = rows[:, i * depth : (i + 1) * depth]
        for start in range(0, weight.shape[1], block):
            columns = slice(start, start + block)
            term = jnp.dot(
                part,
                held[i * depth : (i + 1) * depth, columns],
                preferred_element_type=jnp.float32,
            )
            if i > 0:
                term = term + total[:, columns]
            if i < steps - 1:
                total[:, columns] = term
            else:
                out[:, columns] = term.astype(out.dtype)


def streamed_matmul(rows, weight, grant=50, flops=1024):
    depth = 512 if weight.shape[0] % 512 == 0 else 256
    steps = weight.shape[0] // depth
    return pl.pallas_call(
        functools.partial(streamed_kernel, depth),
        in_specs=[
            pl.BlockSpec(memory_space=pltpu.VMEM),
            pl.BlockSpec(memory_space=pl.ANY),
        ],
        out_specs=pl.BlockSpec(memory_space=pltpu.VMEM),
        out_shape=jax.ShapeDtypeStruct((rows.shape[0], weight.shape[1]), jnp.bfloat16),
        scratch_shapes=[
            pltpu.VMEM(weight.shape, weight.dtype),
            pltpu.VMEM((rows.shape[0], weight.shape[1]), jnp.float32),
            pltpu.SemaphoreType.DMA((2 * steps,)),
        ],
        compiler_params=pltpu.CompilerParams(vmem_limit_bytes=grant * 1024 * 1024),
        cost_estimate=pl.CostEstimate(flops=flops, bytes_accessed=1024, transcendentals=0),
    )(rows, weight)


def add_kernel(mine, came, out):
    out[...] = (mine[...].astype(jnp.float32) + came[...].astype(jnp.float32)).astype(out.dtype)


def add_rows(mine, came):
    whole = pl.BlockSpec(memory_space=pltpu.VMEM)
    return pl.pallas_call(
        add_kernel,
        in_specs=[whole, whole],
        out_specs=whole,
        out_shape=jax.ShapeDtypeStruct(mine.shape, jnp.bfloat16),
        compiler_params=pltpu.CompilerParams(vmem_limit_bytes=4 * 1024 * 1024),
        cost_estimate=pl.CostEstimate(
            flops=8 * 10**9, bytes_accessed=6 * mine.size, transcendentals=0
        ),
    )(mine, came)


def after(value, earlier):
    return lax.optimization_barrier((value, earlier))[0]


def gather_keys(latent, n_ctx):
    rows = latent.shape[0] // 2
    core = lax.axis_index("tp") & 1
    half = lax.dynamic_slice_in_dim(latent, core * rows, rows, 0)
    came = [
        lax.ppermute(half, "ctx", [(c, c + d) for c in range(n_ctx - d)])
        for d in range(n_ctx - 1, 0, -1)
    ]
    mine = jnp.concatenate(came, axis=1)
    other = swap(mine, "tp", 1)
    before = jnp.concatenate(
        [jnp.where(core == 0, mine, other), jnp.where(core == 0, other, mine)], axis=0
    )
    return jnp.concatenate([before, latent], axis=1)


def spread_heads(heads_out, n_ctx, n_tp):
    c, t = lax.axis_index("ctx"), lax.axis_index("tp")
    quarters = heads_out.reshape(n_tp, heads_out.shape[0] // n_tp, heads_out.shape[1])
    groups = jnp.stack(
        [pick(quarters, t)] + [swap(pick(quarters, t ^ m), "tp", m) for m in range(1, n_tp)]
    )
    return jnp.stack(
        [pick(groups, t ^ c)] + [swap(pick(groups, t ^ c ^ j), "ctx", j) for j in range(1, n_ctx)]
    )


def core_rows(mine, other):
    first = lax.axis_index("tp") & 1 == 0
    both = jnp.stack([jnp.where(first, mine, other), jnp.where(first, other, mine)], axis=1)
    return both.reshape(-1, mine.shape[-1])


def paired_tail(
    heads_out, residual, output_weight, norm_gain, gate_weight, up_weight, down_weight, n_ctx, n_tp
):
    row_count, width = residual.shape
    half = row_count // 2
    model_width = width * n_tp
    t = lax.axis_index("tp")
    core = t & 1
    first_half = t >> 1
    own = spread_heads(heads_out, n_ctx, n_tp)
    near = swap(own, "tp", 1)
    far = swap(own, "tp", 2)
    residual_halves = residual.reshape(2, half, width)

    def first_hop(rows):
        blocks = streamed_matmul(rows, output_weight).reshape(2, 2, half, width)
        sent = blocks[:, 1]
        return blocks[:, 0], sent, swap(sent, "ctx", 1)

    def second_hop(kept, came, add=lambda a, b: (wide(a) + wide(b)).astype(jnp.bfloat16)):
        other = add(kept[1], came[1])
        return wide(kept[0]) + wide(came[0]), other, swap(other, "ctx", 2)

    def attend(mine, came, which):
        return (wide(pick(residual_halves, which)) + mine + wide(came)).astype(jnp.bfloat16)

    def scale(rows):
        values = wide(rows)
        scaled = (values * norm_gain[None, :]).astype(jnp.bfloat16)
        return jnp.sum(values * values, axis=1), scaled

    def gate_up(rows):
        squares, scaled = scale(rows)
        terms = [matmul(scaled, gate_weight), matmul(scaled, up_weight)]

        def side(which):
            return jnp.concatenate(
                [lax.dynamic_slice_in_dim(term, which * half, half, 0) for term in terms], axis=0
            )

        return side(core), side(1 - core), squares

    def chip_sum(kept, sent):
        return wide(kept) + wide(swap(sent, "tp", 1))

    kept_a, sent_a, came_a = first_hop(core_rows(own, near))
    far = after(far, sent_a)
    far_near = swap(far, "tp", 1)
    mine_a, other_a, last_a = second_hop(kept_a, came_a)
    kept_b, sent_b, came_b = first_hop(core_rows(far, after(far_near, other_a)))
    attended_a = attend(mine_a, after(last_a, sent_b), first_half)
    twin_a = swap(attended_a, "ctx", 2)
    pair_a = jnp.concatenate([attended_a, twin_a], axis=0)
    rest_a = swap(pair_a, "ctx", 1)
    mine_b, other_b, last_b = second_hop(kept_b, after(came_b, pair_a), add_rows)
    rest_a, last_b = lax.optimization_barrier((rest_a, last_b))
    attended_b = attend(mine_b, last_b, 1 - first_half)
    twin_b = swap(attended_b, "ctx", 2)
    all_a = jnp.concatenate([pair_a, rest_a], axis=0)
    squares_a, scaled = scale(all_a)

    def cross(rows, weight, product):
        term = product(rows, weight).reshape(2, 2, half, -1)

        def side(which):
            return lax.dynamic_index_in_dim(term, which, 1, keepdims=False).reshape(2 * half, -1)

        sent = side(1 - core)
        total = chip_sum(side(core), sent).astype(jnp.bfloat16)
        return sent, total, swap(total, "tp", 2)

    streamed = functools.partial(streamed_matmul, grant=24, flops=6 * 10**9)
    sent_gate, _, across_gate = cross(scaled, gate_weight, streamed)
    _, sums_up, across_up = cross(after(scaled, sent_gate), up_weight, matmul)
    squares_a = after(squares_a, sums_up)
    across_squares = swap(squares_a + swap(squares_a, "tp", 1), "tp", 2)
    pair_b = jnp.concatenate([attended_b, after(twin_b, across_gate)], axis=0)
    rest_b = swap(pair_b, "ctx", 1)

    def hide(chip_terms, squares, across_gate, across_up, across_squares):
        squares = squares + swap(squares, "tp", 1) + across_squares
        squares = lax.dynamic_slice_in_dim(squares, core * half, half, 0)
        inverse_rms = lax.rsqrt(squares / model_width + norm_eps)[:, None]
        gate = (chip_terms[:half] + wide(across_gate)) * inverse_rms
        up = (chip_terms[half:] + wide(across_up)) * inverse_rms
        return (jax.nn.silu(gate) * up).astype(jnp.bfloat16)

    kept, sent, squares_p = gate_up(after(pair_b, sums_up))
    terms_p = chip_sum(kept, sent)
    rest_b, across_up, _ = lax.optimization_barrier((rest_b, across_up, sent))
    kept, sent, squares_q = gate_up(rest_b)
    terms_q = chip_sum(kept, sent)
    parts = [
        hide(
            terms,
            squares,
            across_gate[i * half : (i + 1) * half],
            across_up[i * half : (i + 1) * half],
            across_squares[2 * i * half : 2 * (i + 1) * half],
        )
        for i, (terms, squares) in enumerate(((terms_p, squares_p), (terms_q, squares_q)))
    ]
    hidden = jnp.concatenate(parts, axis=0)
    hidden_near = swap(hidden, "tp", 1)
    hidden_far = swap(hidden, "tp", 2)

    def down_hop(mine, other):
        blocks = streamed_matmul(jnp.concatenate([mine, other], axis=0), down_weight)
        blocks = blocks.reshape(2, 2, half, width)
        return blocks[:, 0], swap(blocks[:, 1], "ctx", 1)

    def down_second(kept, came):
        pair = wide(kept) + wide(came)
        other = pick(pair, 1 - core).astype(jnp.bfloat16)
        return pick(pair, core), other, swap(other, "ctx", 2)

    def in_order(a, b):
        first = first_half == 0
        return jnp.concatenate([jnp.where(first, a, b), jnp.where(first, b, a)], axis=0)

    attended = in_order(attended_a, attended_b)
    kept_b, came_b = down_hop(hidden, hidden_near)
    hidden_far = after(hidden_far, (kept_b, attended))
    hidden_far_near = swap(hidden_far, "tp", 1)
    down_b, other_b, last_b = down_second(kept_b, after(came_b, hidden_far))
    down_a, _, last_a = down_second(*down_hop(hidden_far, after(hidden_far_near, other_b)))
    out_b = (wide(attended_b) + down_b + wide(last_b)).astype(jnp.bfloat16)
    out_a = (wide(attended_a) + down_a + wide(last_a)).astype(jnp.bfloat16)

    return attended, in_order(out_a, out_b)


def on_device(
    residual,
    latent,
    queries,
    lengths,
    value_weight,
    output_weight,
    norm_gain,
    gate_weight,
    up_weight,
    down_weight,
):
    row_count = residual.shape[0]
    ctx_place = lax.axis_index("ctx")
    n_ctx, n_tp = lax.axis_size("ctx"), lax.axis_size("tp")
    paired = (
        n_ctx == 4
        and n_tp == 4
        and row_count % 64 == 0
        and residual.shape[1] % 256 == 0
        and output_weight.shape[0] % 512 == 0
        and down_weight.shape[0] % 512 == 0
        and gate_weight.shape[0] % 256 == 0
        and gate_weight.shape[1] % 256 == 0
    )
    own_index = ctx_place * row_count + jnp.arange(row_count, dtype=jnp.int32)
    _, own_position = trace_info(own_index, lengths)
    key_order = jnp.arange(n_ctx * row_count, dtype=jnp.int32)
    if paired:
        key_index = key_order + (ctx_place - (n_ctx - 1)) * row_count
        _, key_position = trace_info(key_index, lengths)
        keys = rope_keys(gather_keys(latent, n_ctx), key_position, LAT)
    else:
        rotated_keys = rope_keys(latent, own_position, LAT)
        keys = lax.all_gather(rotated_keys, "ctx", axis=1, tiled=True)
        key_index = key_order
    heads_out = attention(queries, keys, key_index, own_index, own_position, value_weight)
    if paired:
        return paired_tail(
            heads_out,
            residual,
            output_weight,
            norm_gain,
            gate_weight,
            up_weight,
            down_weight,
            n_ctx,
            n_tp,
        )
    all_heads = lax.all_gather(heads_out, "tp", axis=1, tiled=True)
    head_block = lax.all_to_all(all_heads, "ctx", split_axis=1, concat_axis=0, tiled=True)
    head_sum = lax.psum_scatter(
        jnp.dot(head_block, output_weight, preferred_element_type=jnp.float32).astype(jnp.bfloat16),
        "ctx",
        scatter_dimension=0,
        tiled=True,
    ).astype(jnp.float32)
    attended = (residual.astype(jnp.float32) + head_sum).astype(jnp.bfloat16)
    attended_float = attended.astype(jnp.float32)
    squares = lax.psum(jnp.sum(attended_float * attended_float, axis=1), "tp")
    inverse_rms = lax.rsqrt(squares / D + norm_eps)
    scaled = (attended_float * inverse_rms[:, None] * norm_gain[None, :]).astype(jnp.bfloat16)
    scaled_all = lax.all_gather(scaled, "ctx", axis=0, tiled=True)
    unit_count = gate_weight.shape[1]
    gate_up = jnp.concatenate([gate_weight, up_weight], axis=1)
    summed = lax.psum_scatter(
        jnp.dot(scaled_all, gate_up, preferred_element_type=jnp.float32).astype(jnp.bfloat16),
        "tp",
        scatter_dimension=0,
        tiled=True,
    ).astype(jnp.float32)
    hidden_share = (jax.nn.silu(summed[:, :unit_count]) * summed[:, unit_count:]).astype(
        jnp.bfloat16
    )
    hidden_all = lax.all_gather(hidden_share, "tp", axis=0, tiled=True)
    down_sum = lax.psum_scatter(
        jnp.dot(hidden_all, down_weight, preferred_element_type=jnp.float32).astype(jnp.bfloat16),
        "ctx",
        scatter_dimension=0,
        tiled=True,
    ).astype(jnp.float32)
    layer_out = (attended_float + down_sum).astype(jnp.bfloat16)
    return (attended, layer_out)


def solution(mesh):
    in_specs = (
        P(("grp", "ctx"), "tp"),
        P(None, ("grp", "ctx")),
        P(("grp", "ctx"), "tp"),
        P("grp"),
        P(None, "tp"),
        P("ctx", "tp"),
        P("tp"),
        P("tp", "ctx"),
        P("tp", "ctx"),
        P("ctx", "tp"),
    )
    out_specs = (P(("grp", "ctx"), "tp"), P(("grp", "ctx"), "tp"))
    return jax.shard_map(
        on_device, mesh=mesh, in_specs=in_specs, out_specs=out_specs, check_vma=False
    )
```
